32 devices in a mesh: groups: 2 (over y), space: 4 (over z), chan: 4 (over x, core).
Axes of the slice: x: 2, y: 2, z: 4, core: 2. Of those that a mesh axis runs over, the one named last changes fastest.
Arguments:
- inputs: bfloat16 [2, 128, 8, 1024], P('groups', 'chan', 'space'), parts along dimension 0, may hold values from -6 to 6
- pre_act: bfloat16 [2, 128, 8, 1024], P('groups', 'chan', 'space'), parts along dimension 0, may hold values from -6 to 6
- out_grad: bfloat16 [2, 256, 4, 256], P('groups', 'chan', 'space'), parts along dimension 0, may hold values from -12 to 12
- weight_one: bfloat16 [3, 3, 3, 128, 128], P(None, None, None, 'chan'), may hold values from -0.109375 to 0.109375
- weight_two: bfloat16 [3, 3, 3, 128, 256], P(None, None, None, 'chan'), may hold values from -0.109375 to 0.109375
Outputs:
- in_grad: bfloat16 [2, 128, 8, 1024], P('groups', 'chan', 'space'), parts along dimension 0
- filter_one_grad: float32 [6, 3, 3, 128, 128], P('groups', None, None, 'chan'), parts along dimension 0
- filter_two_grad: float32 [6, 3, 3, 128, 256], P('groups', None, None, 'chan'), parts along dimension 0
The draws below stay inside these ranges and needn't reach their ends.
There are 2 independent parts, one for each index of `groups`. The reference program is written for one: setup_inputs(seed, part) draws one part's arguments, and reference() takes and returns one part's arrays. A program takes and returns all parts, laid end to end along the dimension named above; an argument that names none is the same for every part. Nothing has to cross between parts.
All inputs are finite; a program needn't handle non-finite values.
Results may differ from the reference program's by a relative error of at most 0.0049.
Values may be sent and summed in bfloat16 or wider, within the bound.
No kernel may reach another device: no remote copies, remote signals or barrier semaphores. Data moves between devices by JAX's collectives and lax.ppermute only.
A program may use at most 64 MiB of HBM per device.

```python
import math
import jax
import jax.numpy as jnp
from jax import lax

SAMPLES = 1
GRID = 32
CH = 128
CH2 = 256
DEPTH = 8
ODEPTH = 4
OGRID = 16


def shard_levels(own_key, shape, cuts, smallest, top_value):
    def one(dim, shards_of):
        steps = jax.random.uniform(jax.random.fold_in(jax.random.fold_in(own_key, 6), dim), (shards_of,), jnp.float32, smallest / len(cuts), top_value / len(cuts))
        return jnp.repeat(jnp.exp(steps), shape[dim] // shards_of).reshape((-1,) + (1,) * (len(shape) - dim - 1))

    factor_of = one(*cuts[0])
    for cut in cuts[1:]:
        factor_of = factor_of * one(*cut)
    return factor_of


def normal_values(stream_key, extent, width, most, shards=(), held_as=jnp.bfloat16):
    gain = shard_levels(stream_key, extent, shards, -0.22, 0.18) if shards else 1.0
    entries = jax.random.normal(stream_key, extent, jnp.float32) * width * gain
    return jnp.minimum(jnp.maximum(entries, -most), most).astype(held_as)


def setup_inputs(seed: int = 0, part: int = 0) -> dict:
    seeds = jax.random.split(jax.random.key(seed), 6)
    part_splits = jax.random.split(jax.random.fold_in(seeds[5], part), 6)
    inputs = normal_values(part_splits[0], (SAMPLES, CH, DEPTH, GRID * GRID), 1.0, 6.0, ((1, 4), (2, 4)))
    pre_act = normal_values(part_splits[1], (SAMPLES, CH, DEPTH, GRID * GRID), 1.0, 6.0, ((1, 4), (2, 4)))
    out_grad = normal_values(part_splits[2], (SAMPLES, CH2, ODEPTH, OGRID * OGRID), 2.0, 12.0, ((1, 4), (2, 4)))
    weight_one = normal_values(seeds[3], (3, 3, 3, CH, CH), (27 * CH) ** -0.5, 0.109375, ((3, 4),))
    weight_two = normal_values(seeds[4], (3, 3, 3, CH, CH2), (27 * CH) ** -0.5, 0.109375, ((3, 4),))
    return {"inputs": inputs, "pre_act": pre_act, "out_grad": out_grad, "weight_one": weight_one, "weight_two": weight_two}


leak_slope = 0.3
layout = ('NCDHW', 'DHWIO', 'NCDHW')

def conv_wide(field, kernel, padding, dilation):
    return lax.conv_general_dilated(field.astype(jnp.float32), kernel.astype(jnp.float32), (1, 1, 1), padding, lhs_dilation=dilation, dimension_numbers=layout, precision=lax.Precision.HIGHEST)

def filter_terms(source, grads, stride):
    counts = grads.shape[2:]
    leading = source.shape[:2]
    result = []
    for depth_tap in range(3):
        for row_tap in range(3):
            for col_tap in range(3):
                begin = (0, 0, depth_tap, row_tap, col_tap)
                finish = (leading[0], leading[1], depth_tap + stride * (counts[0] - 1) + 1, row_tap + stride * (counts[1] - 1) + 1, col_tap + stride * (counts[2] - 1) + 1)
                window = lax.slice(source, begin, finish, (1, 1, stride, stride, stride))
                result.append(jnp.einsum('bcdhw,bodhw->co', window.astype(jnp.float32), grads.astype(jnp.float32), precision=lax.Precision.HIGHEST))
    return jnp.stack(result).reshape(3, 3, 3, source.shape[1], grads.shape[1])

def reference(inputs, pre_act, out_grad, weight_one, weight_two):
    source = inputs.reshape(SAMPLES, CH, DEPTH, GRID, GRID)
    pre_value = pre_act.reshape(SAMPLES, CH, DEPTH, GRID, GRID).astype(jnp.float32)
    grads = out_grad.reshape(SAMPLES, CH2, ODEPTH, OGRID, OGRID)
    activation = jnp.where(pre_value > 0, pre_value, leak_slope * pre_value).astype(jnp.bfloat16)
    kernel_two = jnp.swapaxes(jnp.flip(weight_two, (0, 1, 2)), 3, 4)
    act_grad = conv_wide(grads, kernel_two, [(1, 2), (1, 2), (1, 2)], (2, 2, 2))
    pre_grad = jnp.where(pre_value > 0, act_grad, leak_slope * act_grad).astype(jnp.bfloat16)
    kernel_one = jnp.swapaxes(jnp.flip(weight_one, (0, 1, 2)), 3, 4)
    in_grad = conv_wide(pre_grad, kernel_one, [(1, 1), (1, 1), (1, 1)], (1, 1, 1)).astype(jnp.bfloat16)
    margins = ((0, 0), (0, 0), (1, 1), (1, 1), (1, 1))
    scale_one = 1.0 / math.sqrt(SAMPLES * DEPTH * GRID * GRID)
    scale_two = 1.0 / math.sqrt(SAMPLES * ODEPTH * OGRID * OGRID)
    filter_one_grad = filter_terms(jnp.pad(source, margins), pre_grad, 1) * scale_one
    filter_two_grad = filter_terms(jnp.pad(activation, margins), grads, 2) * scale_two
    return (in_grad.reshape(SAMPLES, CH, DEPTH, GRID * GRID), filter_one_grad, filter_two_grad)
```

```python
import math

import jax
import jax.numpy as jnp
import numpy as np
from jax import lax
from jax.experimental import pallas as pl
from jax.experimental.pallas import tpu as pltpu
from jax.sharding import PartitionSpec as P

leak_slope = 0.3
F32 = jnp.float32
BF16 = jnp.bfloat16
CONTRACT_LAST = (((1,), (1,)), ((), ()))


def moved(value, rows, cols, og):
    if rows == 0 and cols == 0:
        return value
    width = og * og
    value = value.astype(F32)
    lane = lax.broadcasted_iota(jnp.int32, value.shape, 1)
    rolled = pltpu.roll(value, (-(rows * og + cols)) % width, 1)
    keep = None
    for step, place in ((rows, lane // og), (cols, lane % og)):
        if step:
            good = place < og - 1 if step > 0 else place > 0
            keep = good if keep is None else keep & good
    return jnp.where(keep, rolled, 0.0)


def neighbour(parity, step):
    place = parity + step
    return place % 2, place // 2


def leaky(value, gate):
    return jnp.where(gate > 0, value, leak_slope * value)


def split_matrix(og):
    width = og * og
    grid = 2 * og
    cell = np.arange(width)
    row, col = cell // grid, cell % grid
    place = ((row % 2) * 2 + col % 2) * (width // 4) + (row // 2) * og + col // 2
    return (place[:, None] == np.arange(width)[None, :]).astype(np.float32)


def split_kernel(og, planes, chans, x_ref, h_ref, e_ref, xp_ref, hp_ref):
    width = og * og
    part = width // 4
    matrix = e_ref[...]
    for source, target in ((x_ref, xp_ref), (h_ref, hp_ref)):
        value = source[...]
        stacked = jnp.concatenate([value[:, i * width : (i + 1) * width] for i in range(4 * planes)], axis=0)
        sorted_cells = jnp.dot(stacked, matrix, preferred_element_type=F32)
        for plane in range(planes):
            for parity in range(4):
                pieces = [
                    sorted_cells[(plane * 4 + i) * chans : (plane * 4 + i + 1) * chans, parity * part : (parity + 1) * part]
                    for i in range(4)
                ]
                at = (plane * 4 + parity) * chans
                target[at : at + chans, :] = jnp.concatenate(pieces, axis=1).astype(BF16)


def transposed_taps(taps, chans, og):
    def tap(row, col):
        at = (row * 3 + col) * chans
        return taps[at : at + chans]

    return [
        tap(1, 1),
        tap(1, 2) + moved(tap(1, 0), 0, 1, og),
        tap(2, 1) + moved(tap(0, 1), 1, 0, og),
        tap(2, 2) + moved(tap(0, 2), 1, 0, og) + moved(tap(2, 0), 0, 1, og) + moved(tap(0, 0), 1, 1, og),
    ]


def plane_grad(w_ref, near, after, gates, chans, og, out_ref, at, live):
    block = 9 * chans
    if after is None:
        taps = jnp.dot(w_ref[block : 2 * block, :], near, preferred_element_type=F32)
    else:
        taps = jnp.dot(w_ref[2 * block : 3 * block, :], near, preferred_element_type=F32)
        taps = taps + jnp.dot(w_ref[0:block, :], after, preferred_element_type=F32)
    for parity, value in enumerate(transposed_taps(taps, chans, og)):
        gate = gates[parity * chans : (parity + 1) * chans].astype(F32)
        value = leaky(value, gate)
        if live is not None:
            value = jnp.where(live, value, 0.0)
        out_ref[at + parity * chans : at + (parity + 1) * chans, :] = value.astype(BF16)


def own_grad_kernel(og, chans, count, w_ref, g_ref, gn_ref, hp_ref, p_ref):
    s = lax.axis_index("space")
    half = 4 * chans
    here = g_ref[...]
    after = jnp.where(s < count - 1, gn_ref[...].astype(F32), 0.0).astype(BF16)
    plane_grad(w_ref, here, None, hp_ref[0:half, :], chans, og, p_ref, 0, None)
    plane_grad(w_ref, here, after, hp_ref[half : 2 * half, :], chans, og, p_ref, half, None)


def rim_grad_kernel(og, chans, count, w_ref, gp_ref, g_ref, gn_ref, hp_prev_ref, hp_next_ref, p_ref):
    s = lax.axis_index("space")
    half = 4 * chans
    plane_grad(w_ref, gp_ref[...], g_ref[...], hp_prev_ref[half : 2 * half, :], chans, og, p_ref, 0, s > 0)
    plane_grad(w_ref, gn_ref[...], None, hp_next_ref[0:half, :], chans, og, p_ref, half, s < count - 1)


def window_rows(blocks, parity, og):
    rows = []
    for row_tap in range(3):
        row_parity, row_move = neighbour(parity // 2, row_tap - 1)
        for col_tap in range(3):
            col_parity, col_move = neighbour(parity % 2, col_tap - 1)
            rows.append(blocks[(row_parity * 2 + col_parity, row_move, col_move)])
    return jnp.concatenate(rows, axis=0)


def moved_blocks(plane, chans, og):
    result = {}
    for parity in range(4):
        value = plane[parity * chans : (parity + 1) * chans]
        for row_move in (0, -1 if parity // 2 else 1):
            for col_move in (0, -1 if parity % 2 else 1):
                result[parity, row_move, col_move] = moved(value, row_move, col_move, og).astype(BF16)
    return result


def filter_one_kernel(og, chans, count, rows, a_ref, xprev_ref, xp_ref, xnext_ref, own_ref, *rest):
    outs, (p_scr, x_scr, f_scr) = rest[: count - 1], rest[count - 1 :]
    s = lax.axis_index("space")
    width = og * og
    shards = a_ref.shape[0]
    all_chans = shards * chans
    half = 4 * chans
    block = 9 * chans
    for plane in range(2):
        for parity in range(4):
            for j in range(shards):
                at = plane * all_chans + j * chans
                p_scr[at : at + chans, parity * width : (parity + 1) * width] = a_ref[
                    j, (plane * 4 + parity) * chans : (plane * 4 + parity + 1) * chans, :
                ]
    planes = (xprev_ref[...], xp_ref[0:half, :], xp_ref[half : 2 * half, :], xnext_ref[...])
    ends = ((0, all_chans), (0, 2 * all_chans), (0, 2 * all_chans), (all_chans, 2 * all_chans))
    products = []
    for index, plane in enumerate(planes):
        blocks = moved_blocks(plane, chans, og)
        for parity in range(4):
            x_scr[index, :, parity * width : (parity + 1) * width] = window_rows(blocks, parity, og)
        first, last = ends[index]
        products.append(
            lax.dot_general(x_scr[index], p_scr[first:last, :], CONTRACT_LAST, preferred_element_type=F32)
        )
    before, even, odd, after = products
    f_scr[0:block, :] = before + even[:, all_chans:]
    f_scr[block : 2 * block, :] = even[:, :all_chans] + odd[:, all_chans:]
    f_scr[2 * block : 3 * block, :] = odd[:, :all_chans] + after
    if count * rows > 3 * block:
        f_scr[3 * block :, :] = jnp.zeros((count * rows - 3 * block, all_chans), F32)

    def piece(step):
        at = pl.multiple_of(lax.rem(s + step, count) * rows, 16)
        return f_scr[pl.ds(at, rows), :]

    own_ref[...] = piece(0)
    for step, out in enumerate(outs):
        out[...] = piece(step + 1).astype(BF16)


def in_grad_kernel(og, chans, w_ref, a_ref, r_ref, e_ref, out_ref, p_scr):
    width = og * og
    part = width // 4
    shards = a_ref.shape[0]
    all_chans = shards * chans
    block = 9 * chans
    for index in range(4):
        source, first = (r_ref, index // 3) if index in (0, 3) else (a_ref, index - 1)
        for parity in range(4):
            for j in range(shards):
                at = index * all_chans + j * chans
                p_scr[at : at + chans, parity * width : (parity + 1) * width] = source[
                    j, (first * 4 + parity) * chans : (first * 4 + parity + 1) * chans, :
                ]
    weights = jnp.concatenate([w_ref[depth * block : (depth + 1) * block, :] for depth in (2, 1, 0)], axis=1)
    stacked = []
    for plane in range(2):
        taps = jnp.dot(
            weights, p_scr[plane * all_chans : (plane + 3) * all_chans, :], preferred_element_type=F32
        )
        sums = []
        for parity in range(4):
            terms = {}
            for row_tap in range(3):
                row_parity, row_move = neighbour(parity // 2, 1 - row_tap)
                for col_tap in range(3):
                    col_parity, col_move = neighbour(parity % 2, 1 - col_tap)
                    at = (row_tap * 3 + col_tap) * chans
                    lane = (row_parity * 2 + col_parity) * width
                    term = taps[at : at + chans, lane : lane + width]
                    key = (row_move, col_move)
                    terms[key] = term if key not in terms else terms[key] + term
            total = None
            for (row_move, col_move), term in terms.items():
                term = moved(term, row_move, col_move, og)
                total = term if total is None else total + term
            sums.append(total)
        for i in range(4):
            stacked.append(
                jnp.concatenate([value[:, i * part : (i + 1) * part] for value in sums], axis=1).astype(BF16)
            )
    joined = lax.dot_general(jnp.concatenate(stacked, axis=0), e_ref[...], CONTRACT_LAST, preferred_element_type=F32)
    for i in range(8):
        out_ref[:, i * width : (i + 1) * width] = joined[i * chans : (i + 1) * chans].astype(BF16)


def filter_two_kernel(og, chans, count, scale, *refs):
    grads, gates, out_ref = refs[:count], refs[count : 2 * count], refs[2 * count]
    g_scr, even_scr, odd_scr = refs[2 * count + 1 :]
    s = lax.axis_index("space")
    half = 4 * chans
    block = 9 * chans
    for step in range(count):
        at = lax.rem(s + count - step, count)
        g_scr[at] = grads[step][...]
        value = gates[step][...].astype(F32)
        act = leaky(value, value).astype(BF16)
        for plane, target in enumerate((even_scr, odd_scr)):
            blocks = moved_blocks(act[plane * half : (plane + 1) * half], chans, og)
            target[at] = window_rows(blocks, 0, og)
    totals = [jnp.zeros((block, g_scr.shape[1]), F32) for _ in range(3)]
    for at in range(count):
        sources = (odd_scr.at[at - 1] if at else None, even_scr.at[at], odd_scr.at[at])
        for depth, source in enumerate(sources):
            if source is not None:
                totals[depth] = totals[depth] + lax.dot_general(
                    source[...], g_scr[at], CONTRACT_LAST, preferred_element_type=F32
                )
    for depth in range(3):
        out_ref[depth * block : (depth + 1) * block, :] = totals[depth] * scale


def place_kernel(count, rows, *refs):
    pieces, out_ref, scr = refs[:count], refs[count], refs[count + 1]
    s = lax.axis_index("space")
    for step, piece in enumerate(pieces):
        at = pl.multiple_of(lax.rem(s + count - step, count) * rows, 16)
        scr[pl.ds(at, rows), :] = piece[...].astype(F32)
    out_ref[...] = scr[0 : out_ref.shape[0], :]


def local_call(kernel, out_shape, scratch, flops, *operands):
    total = sum(value.size * value.dtype.itemsize for value in operands)
    total += sum(math.prod(o.shape) * o.dtype.itemsize for o in jax.tree.leaves(out_shape))
    return pl.pallas_call(
        kernel,
        out_shape=out_shape,
        in_specs=[pl.BlockSpec(memory_space=pltpu.VMEM)] * len(operands),
        out_specs=jax.tree.map(lambda _: pl.BlockSpec(memory_space=pltpu.VMEM), out_shape),
        scratch_shapes=scratch,
        cost_estimate=pl.CostEstimate(flops=flops, bytes_accessed=total, transcendentals=0),
        compiler_params=pltpu.CompilerParams(vmem_limit_bytes=50 * 1024 * 1024),
    )(*operands)


def ring(value, step):
    count = lax.axis_size("space")
    return lax.ppermute(value, "space", [(i, (i + step) % count) for i in range(count)])


def shards(inputs, pre_act, out_grad, weight_one, weight_two):
    samples, chans, planes, cells = inputs.shape
    count = lax.axis_size("space")
    og = math.isqrt(out_grad.shape[3])
    width = og * og
    half = 4 * chans
    block = 9 * chans
    all_chans = weight_one.shape[4]
    all_out = weight_two.shape[4]
    w1 = weight_one.reshape(3 * block, all_chans)
    w2 = weight_two.reshape(3 * block, all_out)
    matrix = jnp.asarray(split_matrix(og), BF16)
    shape = jax.ShapeDtypeStruct

    grads = lax.all_gather(out_grad.reshape(-1, width), "chan", axis=0, tiled=True)
    xp, hp = local_call(
        lambda *r: split_kernel(og, planes, chans, *r),
        [shape((planes * half, width), BF16)] * 2,
        [],
        2 * 2 * planes * half * width * width,
        inputs.reshape(chans, planes * cells),
        pre_act.reshape(chans, planes * cells),
        matrix,
    )
    grads_next = ring(grads, count - 1)
    up = [(i, i + 1) for i in range(count - 1)]
    down = [(i + 1, i) for i in range(count - 1)]
    x_prev = lax.ppermute(xp[half:], "space", up)
    x_next = lax.ppermute(xp[:half], "space", down)

    p_own = local_call(
        lambda *r: own_grad_kernel(og, chans, count, *r),
        shape((2 * half, width), BF16),
        [],
        2 * 3 * block * all_out * width,
        w2,
        grads,
        grads_next,
        hp,
    )
    a_own = lax.all_gather(p_own, "chan", axis=0)

    all_grads = [grads] + [ring(grads, step) for step in range(1, count - 1)] + [grads_next]
    all_hp = [hp] + [ring(hp, step) for step in range(1, count)]

    rows = -(-3 * block // (16 * count)) * 16
    pieces = local_call(
        lambda *r: filter_one_kernel(og, chans, count, rows, *r),
        [shape((rows, all_chans), F32)] + [shape((rows, all_chans), BF16)] * (count - 1),
        [
            pltpu.VMEM((2 * all_chans, 4 * width), BF16),
            pltpu.VMEM((4, block, 4 * width), BF16),
            pltpu.VMEM((count * rows, all_chans), F32),
        ],
        2 * 6 * block * all_chans * cells,
        a_own,
        x_prev,
        xp,
        x_next,
    )
    total = pieces[0]
    for step in range(1, count):
        total = total + ring(pieces[step], step).astype(F32)
    scale_one = 1.0 / math.sqrt(samples * planes * count * cells)
    scale_two = 1.0 / math.sqrt(samples * out_grad.shape[2] * count * width)
    total = (total * scale_one).astype(BF16)

    p_rim = local_call(
        lambda *r: rim_grad_kernel(og, chans, count, *r),
        shape((2 * half, width), BF16),
        [],
        2 * 3 * block * all_out * width,
        w2,
        all_grads[1],
        grads,
        grads_next,
        all_hp[1],
        all_hp[count - 1],
    )
    a_rim = lax.all_gather(p_rim, "chan", axis=0)
    in_grad = local_call(
        lambda *r: in_grad_kernel(og, chans, *r),
        shape((chans, planes * cells), BF16),
        [pltpu.VMEM((4 * all_chans, 4 * width), BF16)],
        2 * 6 * block * all_chans * cells,
        w1,
        a_own,
        a_rim,
        matrix,
    )
    filter_two = local_call(
        lambda *r: filter_two_kernel(og, chans, count, scale_two, *r),
        shape((3 * block, all_out), F32),
        [
            pltpu.VMEM((count, all_out, width), BF16),
            pltpu.VMEM((count, block, width), BF16),
            pltpu.VMEM((count, block, width), BF16),
        ],
        2 * 3 * count * block * all_out * width,
        *all_grads,
        *all_hp,
    )
    filter_one = local_call(
        lambda *r: place_kernel(count, rows, *r),
        shape((3 * block, all_chans), F32),
        [pltpu.VMEM((count * rows, all_chans), F32)],
        0,
        total,
        *[ring(total, step) for step in range(1, count)],
    )
    return (
        in_grad.reshape(samples, chans, planes, cells),
        filter_one.reshape(3, 3, 3, chans, all_chans),
        filter_two.reshape(3, 3, 3, chans, all_out),
    )


def solution(mesh):
    in_specs = (
        P("groups", "chan", "space", None),
        P("groups", "chan", "space", None),
        P("groups", "chan", "space", None),
        P(None, None, None, "chan", None),
        P(None, None, None, "chan", None),
    )
    out_specs = (
        P("groups", "chan", "space", None),
        P("groups", None, None, "chan", None),
        P("groups", None, None, "chan", None),
    )
    return jax.shard_map(shards, mesh=mesh, in_specs=in_specs, out_specs=out_specs, check_vma=False)
```

```python
import math

import jax
import jax.numpy as jnp
import numpy as np
from jax import lax
from jax.experimental import pallas as pl
from jax.experimental.pallas import tpu as pltpu
from jax.sharding import PartitionSpec as P

leak_slope = 0.3
F32 = jnp.float32
BF16 = jnp.bfloat16
CONTRACT_LAST = (((1,), (1,)), ((), ()))


def moved(value, rows, cols, og):
    if rows == 0 and cols == 0:
        return value
    width = og * og
    value = value.astype(F32)
    lane = lax.broadcasted_iota(jnp.int32, value.shape, 1)
    rolled = pltpu.roll(value, (-(rows * og + cols)) % width, 1)
    keep = None
    for step, place in ((rows, lane // og), (cols, lane % og)):
        if step:
            good = place < og - 1 if step > 0 else place > 0
            keep = good if keep is None else keep & good
    return jnp.where(keep, rolled, 0.0)


def neighbour(parity, step):
    place = parity + step
    return place % 2, place // 2


def leaky(value, gate):
    return jnp.where(gate > 0, value, leak_slope * value)


def split_matrix(og):
    width = og * og
    grid = 2 * og
    cell = np.arange(width)
    row, col = cell // grid, cell % grid
    place = ((row % 2) * 2 + col % 2) * (width // 4) + (row // 2) * og + col // 2
    return (place[:, None] == np.arange(width)[None, :]).astype(np.float32)


def split_kernel(og, planes, chans, x_ref, h_ref, e_ref, xp_ref, hp_ref):
    width = og * og
    part = width // 4
    matrix = e_ref[...]
    for source, target in ((x_ref, xp_ref), (h_ref, hp_ref)):
        value = source[...]
        stacked = jnp.concatenate([value[:, i * width : (i + 1) * width] for i in range(4 * planes)], axis=0)
        sorted_cells = jnp.dot(stacked, matrix, preferred_element_type=F32)
        for plane in range(planes):
            for parity in range(4):
                pieces = [
                    sorted_cells[(plane * 4 + i) * chans : (plane * 4 + i + 1) * chans, parity * part : (parity + 1) * part]
                    for i in range(4)
                ]
                at = (plane * 4 + parity) * chans
                target[at : at + chans, :] = jnp.concatenate(pieces, axis=1).astype(BF16)


def transposed_taps(taps, chans, og):
    def tap(row, col):
        at = (row * 3 + col) * chans
        return taps[at : at + chans]

    return [
        tap(1, 1),
        tap(1, 2) + moved(tap(1, 0), 0, 1, og),
        tap(2, 1) + moved(tap(0, 1), 1, 0, og),
        tap(2, 2) + moved(tap(0, 2), 1, 0, og) + moved(tap(2, 0), 0, 1, og) + moved(tap(0, 0), 1, 1, og),
    ]


def plane_grad(w_ref, near, after, gates, chans, og, out_ref, at, live):
    block = 9 * chans
    if after is None:
        taps = jnp.dot(w_ref[block : 2 * block, :], near, preferred_element_type=F32)
    else:
        taps = jnp.dot(w_ref[2 * block : 3 * block, :], near, preferred_element_type=F32)
        taps = taps + jnp.dot(w_ref[0:block, :], after, preferred_element_type=F32)
    for parity, value in enumerate(transposed_taps(taps, chans, og)):
        gate = gates[parity * chans : (parity + 1) * chans].astype(F32)
        value = leaky(value, gate)
        if live is not None:
            value = jnp.where(live, value, 0.0)
        out_ref[at + parity * chans : at + (parity + 1) * chans, :] = value.astype(BF16)


def own_grad_kernel(og, chans, count, w_ref, g_ref, gn_ref, hp_ref, p_ref):
    s = lax.axis_index("space")
    half = 4 * chans
    here = g_ref[...]
    after = jnp.where(s < count - 1, gn_ref[...].astype(F32), 0.0).astype(BF16)
    plane_grad(w_ref, here, None, hp_ref[0:half, :], chans, og, p_ref, 0, None)
    plane_grad(w_ref, here, after, hp_ref[half : 2 * half, :], chans, og, p_ref, half, None)


def rim_grad_kernel(og, chans, count, w_ref, gp_ref, g_ref, gn_ref, hp_prev_ref, hp_next_ref, p_ref):
    s = lax.axis_index("space")
    half = 4 * chans
    plane_grad(w_ref, gp_ref[...], g_ref[...], hp_prev_ref[half : 2 * half, :], chans, og, p_ref, 0, s > 0)
    plane_grad(w_ref, gn_ref[...], None, hp_next_ref[0:half, :], chans, og, p_ref, half, s < count - 1)


def window_rows(blocks, parity, og):
    rows = []
    for row_tap in range(3):
        row_parity, row_move = neighbour(parity // 2, row_tap - 1)
        for col_tap in range(3):
            col_parity, col_move = neighbour(parity % 2, col_tap - 1)
            rows.append(blocks[(row_parity * 2 + col_parity, row_move, col_move)])
    return jnp.concatenate(rows, axis=0)


def moved_blocks(plane, chans, og):
    result = {}
    for parity in range(4):
        value = plane[parity * chans : (parity + 1) * chans]
        for row_move in (0, -1 if parity // 2 else 1):
            for col_move in (0, -1 if parity % 2 else 1):
                result[parity, row_move, col_move] = moved(value, row_move, col_move, og).astype(BF16)
    return result


def filter_one_kernel(og, chans, count, rows, a_ref, xprev_ref, xp_ref, xnext_ref, own_ref, *rest):
    outs, (p_scr, x_scr, f_scr) = rest[: count - 1], rest[count - 1 :]
    s = lax.axis_index("space")
    width = og * og
    shards = a_ref.shape[0]
    all_chans = shards * chans
    half = 4 * chans
    block = 9 * chans
    for plane in range(2):
        for parity in range(4):
            for j in range(shards):
                at = plane * all_chans + j * chans
                p_scr[at : at + chans, parity * width : (parity + 1) * width] = a_ref[
                    j, (plane * 4 + parity) * chans : (plane * 4 + parity + 1) * chans, :
                ]
    planes = (xprev_ref[...], xp_ref[0:half, :], xp_ref[half : 2 * half, :], xnext_ref[...])
    ends = ((0, all_chans), (0, 2 * all_chans), (0, 2 * all_chans), (all_chans, 2 * all_chans))
    products = []
    for index, plane in enumerate(planes):
        blocks = moved_blocks(plane, chans, og)
        for parity in range(4):
            x_scr[index, :, parity * width : (parity + 1) * width] = window_rows(blocks, parity, og)
        first, last = ends[index]
        products.append(
            lax.dot_general(x_scr[index], p_scr[first:last, :], CONTRACT_LAST, preferred_element_type=F32)
        )
    before, even, odd, after = products
    f_scr[0:block, :] = before + even[:, all_chans:]
    f_scr[block : 2 * block, :] = even[:, :all_chans] + odd[:, all_chans:]
    f_scr[2 * block : 3 * block, :] = odd[:, :all_chans] + after
    if count * rows > 3 * block:
        f_scr[3 * block :, :] = jnp.zeros((count * rows - 3 * block, all_chans), F32)

    def piece(step):
        at = pl.multiple_of(lax.rem(s + step, count) * rows, 16)
        return f_scr[pl.ds(at, rows), :]

    own_ref[...] = piece(0)
    for step, out in enumerate(outs):
        out[...] = piece(step + 1).astype(BF16)


def in_grad_kernel(og, chans, w_ref, a_ref, r_ref, e_ref, out_ref, p_scr):
    width = og * og
    shards = a_ref.shape[0]
    all_chans = shards * chans
    for index in range(4):
        source, first = (r_ref, index // 3) if index in (0, 3) else (a_ref, index - 1)
        for parity in range(4):
            for j in range(shards):
                at = index * all_chans + j * chans
                p_scr[at : at + chans, parity * width : (parity + 1) * width] = source[
                    j, (first * 4 + parity) * chans : (first * 4 + parity + 1) * chans, :
                ]
    in_grad_planes(og, chans, all_chans, w_ref, e_ref, out_ref, p_scr)


def in_grad_planes(og, chans, all_chans, w_ref, e_ref, out_ref, p_scr):
    width = og * og
    part = width // 4
    block = 9 * chans
    weights = jnp.concatenate([w_ref[depth * block : (depth + 1) * block, :] for depth in (2, 1, 0)], axis=1)
    stacked = []
    for plane in range(2):
        taps = jnp.dot(
            weights, p_scr[plane * all_chans : (plane + 3) * all_chans, :], preferred_element_type=F32
        )
        sums = []
        for parity in range(4):
            terms = {}
            for row_tap in range(3):
                row_parity, row_move = neighbour(parity // 2, 1 - row_tap)
                for col_tap in range(3):
                    col_parity, col_move = neighbour(parity % 2, 1 - col_tap)
                    at = (row_tap * 3 + col_tap) * chans
                    lane = (row_parity * 2 + col_parity) * width
                    term = taps[at : at + chans, lane : lane + width]
                    key = (row_move, col_move)
                    terms[key] = term if key not in terms else terms[key] + term
            total = None
            for (row_move, col_move), term in terms.items():
                term = moved(term, row_move, col_move, og)
                total = term if total is None else total + term
            sums.append(total)
        for i in range(4):
            stacked.append(
                jnp.concatenate([value[:, i * part : (i + 1) * part] for value in sums], axis=1).astype(BF16)
            )
    joined = lax.dot_general(jnp.concatenate(stacked, axis=0), e_ref[...], CONTRACT_LAST, preferred_element_type=F32)
    for i in range(8):
        out_ref[:, i * width : (i + 1) * width] = joined[i * chans : (i + 1) * chans].astype(BF16)


def filter_two_kernel(og, chans, count, scale, gathered, *refs):
    number = 1 if gathered else count
    grads, gates, out_ref = refs[:number], refs[number : number + count], refs[number + count]
    g_scr, even_scr, odd_scr = refs[number + count + 1 :]
    s = lax.axis_index("space")
    half = 4 * chans
    block = 9 * chans
    for step in range(count):
        at = lax.rem(s + count - step, count)
        if gathered:
            part = grads[0].shape[1] // count
            for j in range(grads[0].shape[0]):
                g_scr[at, j * part : (j + 1) * part, :] = grads[0][j, step * part : (step + 1) * part, :]
        else:
            g_scr[at] = grads[step][...]
        value = gates[step][...].astype(F32)
        act = leaky(value, value).astype(BF16)
        for plane, target in enumerate((even_scr, odd_scr)):
            blocks = moved_blocks(act[plane * half : (plane + 1) * half], chans, og)
            target[at] = window_rows(blocks, 0, og)
    totals = [jnp.zeros((block, g_scr.shape[1]), F32) for _ in range(3)]
    for at in range(count):
        sources = (odd_scr.at[at - 1] if at else None, even_scr.at[at], odd_scr.at[at])
        for depth, source in enumerate(sources):
            if source is not None:
                totals[depth] = totals[depth] + lax.dot_general(
                    source[...], g_scr[at], CONTRACT_LAST, preferred_element_type=F32
                )
    for depth in range(3):
        out_ref[depth * block : (depth + 1) * block, :] = totals[depth] * scale


def place_kernel(count, rows, *refs):
    pieces, out_ref, scr = refs[:count], refs[count], refs[count + 1]
    s = lax.axis_index("space")
    for step, piece in enumerate(pieces):
        at = pl.multiple_of(lax.rem(s + count - step, count) * rows, 16)
        scr[pl.ds(at, rows), :] = piece[...].astype(F32)
    out_ref[...] = scr[0 : out_ref.shape[0], :]


def all_grad_kernel(og, chans, count, w_ref, g_ref, *refs):
    gates, (all_ref, local_ref, g_scr, h_scr, p_scr) = refs[:count], refs[count:]
    s = lax.axis_index("space")
    half = 4 * chans
    part = g_ref.shape[1] // count
    for step in range(count):
        at = lax.rem(s + count - step, count)
        for j in range(g_ref.shape[0]):
            g_scr[at, j * part : (j + 1) * part, :] = g_ref[j, step * part : (step + 1) * part, :]
        h_scr[at] = gates[step][...]
    empty = jnp.zeros((half, og * og), BF16)
    p_scr[0] = empty
    p_scr[2 * count + 1] = empty
    for q in range(count):
        here = g_scr[q]
        plane_grad(w_ref, here, None, h_scr[q, 0:half, :], chans, og, p_scr.at[2 * q + 1], 0, None)
        after = g_scr[q + 1] if q < count - 1 else jnp.zeros_like(here)
        plane_grad(w_ref, here, after, h_scr[q, half : 2 * half, :], chans, og, p_scr.at[2 * q + 2], 0, None)
    all_ref[...] = p_scr[1 : 2 * count + 1]
    local_ref[...] = p_scr[pl.ds(2 * s, 4)]


def block_rows(chans):
    return -(-27 * chans // 64) * 16


def filter_block_kernel(og, chans, count, scale, p_ref, x_ref, out_ref, p_scr, x_scr):
    width = og * og
    half = 4 * chans
    block = 9 * chans
    lanes = 4 * chans
    planes = 2 * count
    empty = jnp.zeros((chans, 4 * width), BF16)
    for index in (0, planes + 1, planes + 2):
        p_scr[index * chans : (index + 1) * chans, :] = empty
    for plane in range(planes):
        at = (plane + 1) * chans
        for parity in range(4):
            p_scr[at : at + chans, parity * width : (parity + 1) * width] = p_ref[
                plane, parity * chans : (parity + 1) * chans, :
            ]
    total = jnp.zeros((block, lanes), F32)
    for plane in range(planes):
        first = (plane % 2) * half
        blocks = moved_blocks(x_ref[plane // 2, first : first + half, :], chans, og)
        for parity in range(4):
            x_scr[plane % 2, :, parity * width : (parity + 1) * width] = window_rows(blocks, parity, og)
        total = total + lax.dot_general(
            x_scr[plane % 2], p_scr[plane * chans : plane * chans + lanes, :], CONTRACT_LAST, preferred_element_type=F32
        )
    total = total * scale
    rows = block_rows(chans)
    tail = total[rows:]
    moved_tail = [pltpu.roll(tail, lanes - (i + 1) * chans, 1) for i in range(3)]
    spare = rows - 3 * (block - rows)
    if spare:
        moved_tail.append(jnp.zeros((spare, lanes), F32))
    lane = lax.broadcasted_iota(jnp.int32, (rows, lanes), 1)
    out_ref[...] = jnp.where(lane < 3 * chans, total[:rows], jnp.concatenate(moved_tail, axis=0)).astype(BF16)


def join_kernel(chans, count, *refs):
    pieces, out_ref, scr = refs[:count], refs[count], refs[count + 1]
    s = lax.axis_index("space")
    lanes = 4 * chans
    block = 9 * chans
    rows = block_rows(chans)
    rest = block - rows
    for step, piece in enumerate(pieces):
        scr[step] = piece[...].astype(F32)
    group = lax.broadcasted_iota(jnp.int32, (block, lanes), 1) // chans
    sums = [jnp.zeros((block, lanes), F32) for _ in range(3)]
    for j in range(count):
        value = scr[lax.rem(s + count - j, count)]
        tail = [pltpu.roll(value[i * rest : (i + 1) * rest], (i + 1) * chans, 1) for i in range(3)]
        tail = jnp.where(group[:rest] == 0, tail[0], jnp.where(group[:rest] == 1, tail[1], tail[2]))
        whole = jnp.concatenate([value, tail], axis=0)
        for depth in range(3):
            shift = (j - (2 - depth)) * chans % lanes
            placed = pltpu.roll(whole, shift, 1) if shift else whole
            sums[depth] = jnp.where(group == j, placed, sums[depth])
    for depth in range(3):
        out_ref[depth * block : (depth + 1) * block, :] = sums[depth]


def in_grad_square_kernel(og, chans, count, w_ref, e_ref, *refs):
    sources, out_ref, p_scr = refs[:count], refs[count], refs[count + 1]
    i = lax.axis_index("chan")
    width = og * og
    all_chans = count * chans
    for mask, source in enumerate(sources):
        j = lax.bitwise_xor(i, mask)
        for index in range(4):
            at = pl.multiple_of(index * all_chans + j * chans, chans)
            for parity in range(4):
                p_scr[pl.ds(at, chans), parity * width : (parity + 1) * width] = source[
                    index, parity * chans : (parity + 1) * chans, :
                ]
    in_grad_planes(og, chans, all_chans, w_ref, e_ref, out_ref, p_scr)


def local_call(kernel, out_shape, scratch, flops, *operands):
    total = sum(value.size * value.dtype.itemsize for value in operands)
    total += sum(math.prod(o.shape) * o.dtype.itemsize for o in jax.tree.leaves(out_shape))
    return pl.pallas_call(
        kernel,
        out_shape=out_shape,
        in_specs=[pl.BlockSpec(memory_space=pltpu.VMEM)] * len(operands),
        out_specs=jax.tree.map(lambda _: pl.BlockSpec(memory_space=pltpu.VMEM), out_shape),
        scratch_shapes=scratch,
        cost_estimate=pl.CostEstimate(flops=flops, bytes_accessed=total, transcendentals=0),
        compiler_params=pltpu.CompilerParams(vmem_limit_bytes=50 * 1024 * 1024),
    )(*operands)


def ring(value, step):
    count = lax.axis_size("space")
    return lax.ppermute(value, "space", [(i, (i + step) % count) for i in range(count)])


def ring_shards(inputs, pre_act, out_grad, weight_one, weight_two):
    samples, chans, planes, cells = inputs.shape
    count = lax.axis_size("space")
    og = math.isqrt(out_grad.shape[3])
    width = og * og
    half = 4 * chans
    block = 9 * chans
    all_chans = weight_one.shape[4]
    all_out = weight_two.shape[4]
    w1 = weight_one.reshape(3 * block, all_chans)
    w2 = weight_two.reshape(3 * block, all_out)
    matrix = jnp.asarray(split_matrix(og), BF16)
    shape = jax.ShapeDtypeStruct

    grads = lax.all_gather(out_grad.reshape(-1, width), "chan", axis=0, tiled=True)
    xp, hp = local_call(
        lambda *r: split_kernel(og, planes, chans, *r),
        [shape((planes * half, width), BF16)] * 2,
        [],
        2 * 2 * planes * half * width * width,
        inputs.reshape(chans, planes * cells),
        pre_act.reshape(chans, planes * cells),
        matrix,
    )
    grads_next = ring(grads, count - 1)
    up = [(i, i + 1) for i in range(count - 1)]
    down = [(i + 1, i) for i in range(count - 1)]
    x_prev = lax.ppermute(xp[half:], "space", up)
    x_next = lax.ppermute(xp[:half], "space", down)

    p_own = local_call(
        lambda *r: own_grad_kernel(og, chans, count, *r),
        shape((2 * half, width), BF16),
        [],
        2 * 3 * block * all_out * width,
        w2,
        grads,
        grads_next,
        hp,
    )
    a_own = lax.all_gather(p_own, "chan", axis=0)

    all_grads = [grads] + [ring(grads, step) for step in range(1, count - 1)] + [grads_next]
    all_hp = [hp] + [ring(hp, step) for step in range(1, count)]

    rows = -(-3 * block // (16 * count)) * 16
    pieces = local_call(
        lambda *r: filter_one_kernel(og, chans, count, rows, *r),
        [shape((rows, all_chans), F32)] + [shape((rows, all_chans), BF16)] * (count - 1),
        [
            pltpu.VMEM((2 * all_chans, 4 * width), BF16),
            pltpu.VMEM((4, block, 4 * width), BF16),
            pltpu.VMEM((count * rows, all_chans), F32),
        ],
        2 * 6 * block * all_chans * cells,
        a_own,
        x_prev,
        xp,
        x_next,
    )
    total = pieces[0]
    for step in range(1, count):
        total = total + ring(pieces[step], step).astype(F32)
    scale_one = 1.0 / math.sqrt(samples * planes * count * cells)
    scale_two = 1.0 / math.sqrt(samples * out_grad.shape[2] * count * width)
    total = (total * scale_one).astype(BF16)

    p_rim = local_call(
        lambda *r: rim_grad_kernel(og, chans, count, *r),
        shape((2 * half, width), BF16),
        [],
        2 * 3 * block * all_out * width,
        w2,
        all_grads[1],
        grads,
        grads_next,
        all_hp[1],
        all_hp[count - 1],
    )
    a_rim = lax.all_gather(p_rim, "chan", axis=0)
    in_grad = local_call(
        lambda *r: in_grad_kernel(og, chans, *r),
        shape((chans, planes * cells), BF16),
        [pltpu.VMEM((4 * all_chans, 4 * width), BF16)],
        2 * 6 * block * all_chans * cells,
        w1,
        a_own,
        a_rim,
        matrix,
    )
    filter_two = local_call(
        lambda *r: filter_two_kernel(og, chans, count, scale_two, False, *r),
        shape((3 * block, all_out), F32),
        [
            pltpu.VMEM((count, all_out, width), BF16),
            pltpu.VMEM((count, block, width), BF16),
            pltpu.VMEM((count, block, width), BF16),
        ],
        2 * 3 * count * block * all_out * width,
        *all_grads,
        *all_hp,
    )
    filter_one = local_call(
        lambda *r: place_kernel(count, rows, *r),
        shape((3 * block, all_chans), F32),
        [pltpu.VMEM((count * rows, all_chans), F32)],
        0,
        total,
        *[ring(total, step) for step in range(1, count)],
    )
    return (
        in_grad.reshape(samples, chans, planes, cells),
        filter_one.reshape(3, 3, 3, chans, all_chans),
        filter_two.reshape(3, 3, 3, chans, all_out),
    )


def square_shards(inputs, pre_act, out_grad, weight_one, weight_two):
    samples, chans, planes, cells = inputs.shape
    count = lax.axis_size("space")
    og = math.isqrt(out_grad.shape[3])
    width = og * og
    half = 4 * chans
    block = 9 * chans
    all_chans = weight_one.shape[4]
    all_out = weight_two.shape[4]
    w1 = weight_one.reshape(3 * block, all_chans)
    w2 = weight_two.reshape(3 * block, all_out)
    matrix = jnp.asarray(split_matrix(og), BF16)
    shape = jax.ShapeDtypeStruct
    both = ("space", "chan")
    scale_one = 1.0 / math.sqrt(samples * planes * count * cells)
    scale_two = 1.0 / math.sqrt(samples * out_grad.shape[2] * count * width)

    near = out_grad.reshape(-1, width)
    near = jnp.concatenate([near] + [ring(near, step) for step in range(1, count)], axis=0)
    xp, hp = local_call(
        lambda *r: split_kernel(og, planes, chans, *r),
        [shape((planes * half, width), BF16)] * 2,
        [],
        2 * 2 * planes * half * width * width,
        inputs.reshape(chans, planes * cells),
        pre_act.reshape(chans, planes * cells),
        matrix,
    )
    turn = [(a * count + b, b * count + a) for a in range(count) for b in range(count)]
    x_turned = lax.ppermute(xp, both, turn)
    all_hp = [hp] + [ring(hp, step) for step in range(1, count)]
    grads = lax.all_gather(near, "chan", axis=0)
    p_all, p_local = local_call(
        lambda *r: all_grad_kernel(og, chans, count, *r),
        [shape((planes * count, half, width), BF16), shape((4, half, width), BF16)],
        [
            pltpu.VMEM((count, all_out, width), BF16),
            pltpu.VMEM((count, planes * half, width), BF16),
            pltpu.VMEM((planes * count + 2, half, width), BF16),
        ],
        2 * 3 * count * block * all_out * width,
        w2,
        grads,
        *all_hp,
    )
    near_p = [p_local]
    bit = count // 2
    found = {0: p_local}
    while bit:
        pairs = [(i, i ^ bit) for i in range(count)]
        found.update({mask ^ bit: lax.ppermute(value, "chan", pairs) for mask, value in found.items()})
        bit //= 2
    near_p = [found[mask] for mask in range(count)]

    x_all = lax.all_gather(x_turned, "chan", axis=0)
    rows = block_rows(chans)
    piece = local_call(
        lambda *r: filter_block_kernel(og, chans, count, scale_one, *r),
        shape((rows, all_chans), BF16),
        [
            pltpu.VMEM(((planes * count + 3) * chans, 4 * width), BF16),
            pltpu.VMEM((2, block, 4 * width), BF16),
        ],
        2 * 3 * count * block * all_chans * cells,
        p_all,
        x_all,
    )
    pieces = []
    for step in range(count):
        pairs = [(a * count + b, (b + step) % count * count + a) for a in range(count) for b in range(count)]
        pieces.append(lax.ppermute(piece, both, pairs))
    filter_two = local_call(
        lambda *r: filter_two_kernel(og, chans, count, scale_two, True, *r),
        shape((3 * block, all_out), F32),
        [
            pltpu.VMEM((count, all_out, width), BF16),
            pltpu.VMEM((count, block, width), BF16),
            pltpu.VMEM((count, block, width), BF16),
        ],
        2 * 3 * count * block * all_out * width,
        grads,
        *all_hp,
    )
    in_grad = local_call(
        lambda *r: in_grad_square_kernel(og, chans, count, *r),
        shape((chans, planes * cells), BF16),
        [pltpu.VMEM((4 * all_chans, 4 * width), BF16)],
        2 * 6 * block * all_chans * cells,
        w1,
        matrix,
        *near_p,
    )
    filter_one = local_call(
        lambda *r: join_kernel(chans, count, *r),
        shape((3 * block, all_chans), F32),
        [pltpu.VMEM((count, rows, all_chans), F32)],
        0,
        *pieces,
    )
    return (
        in_grad.reshape(samples, chans, planes, cells),
        filter_one.reshape(3, 3, 3, chans, all_chans),
        filter_two.reshape(3, 3, 3, chans, all_out),
    )


def shards(*arguments):
    count = lax.axis_size("space")
    square = count == lax.axis_size("chan") and 4 * arguments[0].shape[1] == arguments[3].shape[4]
    return (square_shards if square else ring_shards)(*arguments)


def solution(mesh):
    in_specs = (
        P("groups", "chan", "space", None),
        P("groups", "chan", "space", None),
        P("groups", "chan", "space", None),
        P(None, None, None, "chan", None),
        P(None, None, None, "chan", None),
    )
    out_specs = (
        P("groups", "chan", "space", None),
        P("groups", None, None, "chan", None),
        P("groups", None, None, "chan", None),
    )
    return jax.shard_map(shards, mesh=mesh, in_specs=in_specs, out_specs=out_specs, check_vma=False)
```

```python
import math

import jax
import jax.numpy as jnp
import numpy as np
from jax import lax
from jax.experimental import pallas as pl
from jax.experimental.pallas import tpu as pltpu
from jax.sharding import PartitionSpec as P

leak_slope = 0.3
F32 = jnp.float32
BF16 = jnp.bfloat16
CONTRACT_LAST = (((1,), (1,)), ((), ()))


def moved(value, rows, cols, og):
    if rows == 0 and cols == 0:
        return value
    width = og * og
    value = value.astype(F32)
    lane = lax.broadcasted_iota(jnp.int32, value.shape, 1)
    rolled = pltpu.roll(value, (-(rows * og + cols)) % width, 1)
    keep = None
    for step, place in ((rows, lane // og), (cols, lane % og)):
        if step:
            good = place < og - 1 if step > 0 else place > 0
            keep = good if keep is None else keep & good
    return jnp.where(keep, rolled, 0.0)


def neighbour(parity, step):
    place = parity + step
    return place % 2, place // 2


def leaky(value, gate):
    return jnp.where(gate > 0, value, leak_slope * value)


def split_matrix(og):
    width = og * og
    grid = 2 * og
    cell = np.arange(width)
    row, col = cell // grid, cell % grid
    place = ((row % 2) * 2 + col % 2) * (width // 4) + (row // 2) * og + col // 2
    return (place[:, None] == np.arange(width)[None, :]).astype(np.float32)


def split_kernel(og, planes, chans, x_ref, h_ref, e_ref, xp_ref, hp_ref):
    width = og * og
    part = width // 4
    matrix = e_ref[...]
    for source, target in ((x_ref, xp_ref), (h_ref, hp_ref)):
        value = source[...]
        stacked = jnp.concatenate([value[:, i * width : (i + 1) * width] for i in range(4 * planes)], axis=0)
        sorted_cells = jnp.dot(stacked, matrix, preferred_element_type=F32)
        for plane in range(planes):
            for parity in range(4):
                pieces = [
                    sorted_cells[(plane * 4 + i) * chans : (plane * 4 + i + 1) * chans, parity * part : (parity + 1) * part]
                    for i in range(4)
                ]
                at = (plane * 4 + parity) * chans
                target[at : at + chans, :] = jnp.concatenate(pieces, axis=1).astype(BF16)


def transposed_taps(taps, chans, og):
    def tap(row, col):
        at = (row * 3 + col) * chans
        return taps[at : at + chans]

    return [
        tap(1, 1),
        tap(1, 2) + moved(tap(1, 0), 0, 1, og),
        tap(2, 1) + moved(tap(0, 1), 1, 0, og),
        tap(2, 2) + moved(tap(0, 2), 1, 0, og) + moved(tap(2, 0), 0, 1, og) + moved(tap(0, 0), 1, 1, og),
    ]


def plane_grad(w_ref, near, after, gates, chans, og, out_ref, at, live):
    block = 9 * chans
    if after is None:
        taps = jnp.dot(w_ref[block : 2 * block, :], near, preferred_element_type=F32)
    else:
        taps = jnp.dot(w_ref[2 * block : 3 * block, :], near, preferred_element_type=F32)
        taps = taps + jnp.dot(w_ref[0:block, :], after, preferred_element_type=F32)
    for parity, value in enumerate(transposed_taps(taps, chans, og)):
        gate = gates[parity * chans : (parity + 1) * chans].astype(F32)
        value = leaky(value, gate)
        if live is not None:
            value = jnp.where(live, value, 0.0)
        out_ref[at + parity * chans : at + (parity + 1) * chans, :] = value.astype(BF16)


def own_grad_kernel(og, chans, count, w_ref, g_ref, gn_ref, hp_ref, p_ref):
    s = lax.axis_index("space")
    half = 4 * chans
    here = g_ref[...]
    after = jnp.where(s < count - 1, gn_ref[...].astype(F32), 0.0).astype(BF16)
    plane_grad(w_ref, here, None, hp_ref[0:half, :], chans, og, p_ref, 0, None)
    plane_grad(w_ref, here, after, hp_ref[half : 2 * half, :], chans, og, p_ref, half, None)


def rim_grad_kernel(og, chans, count, w_ref, gp_ref, g_ref, gn_ref, hp_prev_ref, hp_next_ref, p_ref):
    s = lax.axis_index("space")
    half = 4 * chans
    plane_grad(w_ref, gp_ref[...], g_ref[...], hp_prev_ref[half : 2 * half, :], chans, og, p_ref, 0, s > 0)
    plane_grad(w_ref, gn_ref[...], None, hp_next_ref[0:half, :], chans, og, p_ref, half, s < count - 1)


def window_rows(blocks, parity, og):
    rows = []
    for row_tap in range(3):
        row_parity, row_move = neighbour(parity // 2, row_tap - 1)
        for col_tap in range(3):
            col_parity, col_move = neighbour(parity % 2, col_tap - 1)
            rows.append(blocks[(row_parity * 2 + col_parity, row_move, col_move)])
    return jnp.concatenate(rows, axis=0)


def moved_blocks(plane, chans, og):
    result = {}
    for parity in range(4):
        value = plane[parity * chans : (parity + 1) * chans]
        for row_move in (0, -1 if parity // 2 else 1):
            for col_move in (0, -1 if parity % 2 else 1):
                result[parity, row_move, col_move] = moved(value, row_move, col_move, og).astype(BF16)
    return result


def filter_one_kernel(og, chans, count, rows, a_ref, xprev_ref, xp_ref, xnext_ref, own_ref, *rest):
    outs, (p_scr, x_scr, f_scr) = rest[: count - 1], rest[count - 1 :]
    s = lax.axis_index("space")
    width = og * og
    shards = a_ref.shape[0]
    all_chans = shards * chans
    half = 4 * chans
    block = 9 * chans
    for plane in range(2):
        for parity in range(4):
            for j in range(shards):
                at = plane * all_chans + j * chans
                p_scr[at : at + chans, parity * width : (parity + 1) * width] = a_ref[
                    j, (plane * 4 + parity) * chans : (plane * 4 + parity + 1) * chans, :
                ]
    planes = (xprev_ref[...], xp_ref[0:half, :], xp_ref[half : 2 * half, :], xnext_ref[...])
    ends = ((0, all_chans), (0, 2 * all_chans), (0, 2 * all_chans), (all_chans, 2 * all_chans))
    products = []
    for index, plane in enumerate(planes):
        blocks = moved_blocks(plane, chans, og)
        for parity in range(4):
            x_scr[index, :, parity * width : (parity + 1) * width] = window_rows(blocks, parity, og)
        first, last = ends[index]
        products.append(
            lax.dot_general(x_scr[index], p_scr[first:last, :], CONTRACT_LAST, preferred_element_type=F32)
        )
    before, even, odd, after = products
    f_scr[0:block, :] = before + even[:, all_chans:]
    f_scr[block : 2 * block, :] = even[:, :all_chans] + odd[:, all_chans:]
    f_scr[2 * block : 3 * block, :] = odd[:, :all_chans] + after
    if count * rows > 3 * block:
        f_scr[3 * block :, :] = jnp.zeros((count * rows - 3 * block, all_chans), F32)

    def piece(step):
        at = pl.multiple_of(lax.rem(s + step, count) * rows, 16)
        return f_scr[pl.ds(at, rows), :]

    own_ref[...] = piece(0)
    for step, out in enumerate(outs):
        out[...] = piece(step + 1).astype(BF16)


def in_grad_kernel(og, chans, w_ref, a_ref, r_ref, e_ref, out_ref, p_scr):
    width = og * og
    shards = a_ref.shape[0]
    all_chans = shards * chans
    for index in range(4):
        source, first = (r_ref, index // 3) if index in (0, 3) else (a_ref, index - 1)
        for parity in range(4):
            for j in range(shards):
                at = index * all_chans + j * chans
                p_scr[at : at + chans, parity * width : (parity + 1) * width] = source[
                    j, (first * 4 + parity) * chans : (first * 4 + parity + 1) * chans, :
                ]
    joined = in_grad_planes(og, chans, all_chans, w_ref, e_ref, p_scr)
    for i in range(8):
        out_ref[:, i * width : (i + 1) * width] = joined[i * chans : (i + 1) * chans].astype(BF16)


def in_grad_planes(og, chans, all_chans, w_ref, e_ref, p_scr):
    width = og * og
    part = width // 4
    block = 9 * chans
    weights = jnp.concatenate([w_ref[depth * block : (depth + 1) * block, :] for depth in (2, 1, 0)], axis=1)
    stacked = []
    for plane in range(2):
        taps = jnp.dot(
            weights, p_scr[plane * all_chans : (plane + 3) * all_chans, :], preferred_element_type=F32
        )
        sums = []
        for parity in range(4):
            terms = {}
            for row_tap in range(3):
                row_parity, row_move = neighbour(parity // 2, 1 - row_tap)
                for col_tap in range(3):
                    col_parity, col_move = neighbour(parity % 2, 1 - col_tap)
                    at = (row_tap * 3 + col_tap) * chans
                    lane = (row_parity * 2 + col_parity) * width
                    term = taps[at : at + chans, lane : lane + width]
                    key = (row_move, col_move)
                    terms[key] = term if key not in terms else terms[key] + term
            total = None
            for (row_move, col_move), term in terms.items():
                term = moved(term, row_move, col_move, og)
                total = term if total is None else total + term
            sums.append(total)
        for i in range(4):
            stacked.append(
                jnp.concatenate([value[:, i * part : (i + 1) * part] for value in sums], axis=1).astype(BF16)
            )
    return lax.dot_general(jnp.concatenate(stacked, axis=0), e_ref[...], CONTRACT_LAST, preferred_element_type=F32)


def filter_two_kernel(og, chans, count, scale, *refs):
    grads, gates, out_ref = refs[:count], refs[count : 2 * count], refs[2 * count]
    g_scr, even_scr, odd_scr = refs[2 * count + 1 :]
    s = lax.axis_index("space")
    half = 4 * chans
    block = 9 * chans
    for step in range(count):
        at = lax.rem(s + count - step, count)
        g_scr[at] = grads[step][...]
        value = gates[step][...].astype(F32)
        act = leaky(value, value).astype(BF16)
        for plane, target in enumerate((even_scr, odd_scr)):
            blocks = moved_blocks(act[plane * half : (plane + 1) * half], chans, og)
            target[at] = window_rows(blocks, 0, og)
    filter_two_sums(count, block, scale, g_scr, even_scr, odd_scr, out_ref)


def filter_two_square_kernel(og, chans, count, scale, g_ref, act_ref, out_ref, even_scr, odd_scr):
    half = 4 * chans
    for at in range(count):
        for plane, target in enumerate((even_scr, odd_scr)):
            blocks = moved_blocks(act_ref[at, plane * half : (plane + 1) * half, :], chans, og)
            target[at] = window_rows(blocks, 0, og)
    filter_two_sums(count, 9 * chans, scale, g_ref, even_scr, odd_scr, out_ref)


def filter_two_sums(count, block, scale, g_scr, even_scr, odd_scr, out_ref):
    totals = [jnp.zeros((block, g_scr.shape[1]), F32) for _ in range(3)]
    for at in range(count):
        sources = (odd_scr.at[at - 1] if at else None, even_scr.at[at], odd_scr.at[at])
        for depth, source in enumerate(sources):
            if source is not None:
                totals[depth] = totals[depth] + lax.dot_general(
                    source[...], g_scr[at], CONTRACT_LAST, preferred_element_type=F32
                )
    for depth in range(3):
        out_ref[depth * block : (depth + 1) * block, :] = totals[depth] * scale


def place_kernel(count, rows, *refs):
    pieces, out_ref, scr = refs[:count], refs[count], refs[count + 1]
    s = lax.axis_index("space")
    for step, piece in enumerate(pieces):
        at = pl.multiple_of(lax.rem(s + count - step, count) * rows, 16)
        scr[pl.ds(at, rows), :] = piece[...].astype(F32)
    out_ref[...] = scr[0 : out_ref.shape[0], :]


def plane_matrix(chans, planes):
    row = np.arange(chans * planes)
    place = (row % planes) * chans + row // planes
    return (place[None, :] == np.arange(chans * planes)[:, None]).astype(np.float32)


def split_planes(value, order, matrix, chans, planes, og):
    width = og * og
    part = width // 4
    value = value.reshape(chans * planes, 4 * width)
    value = jnp.dot(order, value, preferred_element_type=F32).astype(BF16)
    stacked = jnp.concatenate([value[:, i * width : (i + 1) * width] for i in range(4)], axis=0)
    cells = jnp.dot(stacked, matrix, preferred_element_type=F32)
    rows = chans * planes
    result = []
    for plane in range(planes):
        for parity in range(4):
            pieces = [
                cells[i * rows + plane * chans : i * rows + (plane + 1) * chans, parity * part : (parity + 1) * part]
                for i in range(4)
            ]
            result.append(jnp.concatenate(pieces, axis=1))
    return jnp.concatenate(result, axis=0)


def pack_kernel(*refs):
    sources, out_ref = refs[:-1], refs[-1]
    rows = sources[0].shape[0]
    for step, source in enumerate(sources):
        out_ref[step * rows : (step + 1) * rows, :] = source[...]


def all_grad_kernel(og, chans, count, scale, w_ref, e_ref, order_ref, *refs):
    grads, gates, x_all, refs = refs[0], refs[1 : count + 1], refs[count + 1], refs[count + 2 :]
    local_ref, g_ref, act_ref, piece_ref, h_scr, p_scr, *block_refs = refs
    s = lax.axis_index("space")
    half = 4 * chans
    part = grads.shape[1] // count
    for step in range(count):
        at = lax.rem(s + count - step, count)
        for j in range(count):
            g_ref[at, j * part : (j + 1) * part, :] = grads[j, step * part : (step + 1) * part, :]
        value = split_planes(gates[step][...], order_ref[...], e_ref[...], chans, 2, og)
        h_scr[at] = value.astype(BF16)
        act_ref[at] = leaky(value, value).astype(BF16)
    empty = jnp.zeros((half, og * og), BF16)
    p_scr[0] = empty
    p_scr[2 * count + 1] = empty
    for q in range(count):
        here = g_ref[q]
        plane_grad(w_ref, here, None, h_scr[q, 0:half, :], chans, og, p_scr.at[2 * q + 1], 0, None)
        after = g_ref[q + 1] if q < count - 1 else jnp.zeros_like(here)
        plane_grad(w_ref, here, after, h_scr[q, half : 2 * half, :], chans, og, p_scr.at[2 * q + 2], 0, None)
    local_ref[...] = p_scr[pl.ds(2 * s, 4)]
    filter_block(og, chans, count, scale, p_scr, e_ref, order_ref, x_all, piece_ref, *block_refs)


def mixed(index, count):
    return index % 2 * (count // 2) + index // 2


def block_rows(chans):
    return -(-27 * chans // 64) * 16


def filter_block(og, chans, count, scale, p_ref, e_ref, order_ref, source, out_ref, x_ref, p_scr, x_scr):
    width = og * og
    half = 4 * chans
    block = 9 * chans
    lanes = 4 * chans
    planes = 2 * count
    for j in range(count):
        value = split_planes(source[j], order_ref[...], e_ref[...], chans, 2, og)
        x_ref[mixed(j, count)] = value.astype(BF16)
    empty = jnp.zeros((chans, 4 * width), BF16)
    for index in (0, planes + 1, planes + 2):
        p_scr[index * chans : (index + 1) * chans, :] = empty
    for plane in range(planes):
        at = (plane + 1) * chans
        for parity in range(4):
            p_scr[at : at + chans, parity * width : (parity + 1) * width] = p_ref[
                plane + 1, parity * chans : (parity + 1) * chans, :
            ]
    total = jnp.zeros((block, lanes), F32)
    for plane in range(planes):
        first = (plane % 2) * half
        blocks = moved_blocks(x_ref[plane // 2, first : first + half, :], chans, og)
        for parity in range(4):
            x_scr[plane % 2, :, parity * width : (parity + 1) * width] = window_rows(blocks, parity, og)
        total = total + lax.dot_general(
            x_scr[plane % 2], p_scr[plane * chans : plane * chans + lanes, :], CONTRACT_LAST, preferred_element_type=F32
        )
    total = total * scale
    rows = block_rows(chans)
    tail = total[rows:]
    moved_tail = [pltpu.roll(tail, lanes - (i + 1) * chans, 1) for i in range(3)]
    spare = rows - 3 * (block - rows)
    if spare:
        moved_tail.append(jnp.zeros((spare, lanes), F32))
    lane = lax.broadcasted_iota(jnp.int32, (rows, lanes), 1)
    out_ref[...] = jnp.where(lane < 3 * chans, total[:rows], jnp.concatenate(moved_tail, axis=0)).astype(BF16)


def join_kernel(chans, count, *refs):
    pieces, out_ref, scr = refs[:count], refs[count], refs[count + 1]
    s = lax.axis_index("space")
    lanes = 4 * chans
    block = 9 * chans
    rows = block_rows(chans)
    rest = block - rows
    for step, piece in enumerate(pieces):
        scr[step] = piece[...].astype(F32)
    group = lax.broadcasted_iota(jnp.int32, (block, lanes), 1) // chans
    sums = [jnp.zeros((block, lanes), F32) for _ in range(3)]
    for j in range(count):
        value = scr[lax.rem(s + count - j, count)]
        tail = [pltpu.roll(value[i * rest : (i + 1) * rest], (i + 1) * chans, 1) for i in range(3)]
        tail = jnp.where(group[:rest] == 0, tail[0], jnp.where(group[:rest] == 1, tail[1], tail[2]))
        whole = jnp.concatenate([value, tail], axis=0)
        for depth in range(3):
            shift = (j - (2 - depth)) * chans % lanes
            placed = pltpu.roll(whole, shift, 1) if shift else whole
            sums[depth] = jnp.where(group == j, placed, sums[depth])
    for depth in range(3):
        out_ref[depth * block : (depth + 1) * block, :] = sums[depth]


def in_grad_square_kernel(og, chans, count, w_ref, e_ref, order_ref, *refs):
    sources, out_ref, p_scr = refs[:count], refs[count], refs[count + 1]
    i = lax.axis_index("chan")
    width = og * og
    all_chans = count * chans
    for mask, source in enumerate(sources):
        j = lax.bitwise_xor(i, mask)
        for index in range(4):
            at = pl.multiple_of(index * all_chans + j * chans, chans)
            for parity in range(4):
                p_scr[pl.ds(at, chans), parity * width : (parity + 1) * width] = source[
                    index, parity * chans : (parity + 1) * chans, :
                ]
    joined = in_grad_planes(og, chans, all_chans, w_ref, e_ref, p_scr)
    rows = [
        jnp.concatenate([joined[(plane * 4 + k) * chans : (plane * 4 + k + 1) * chans] for k in range(4)], axis=1)
        for plane in range(2)
    ]
    value = jnp.concatenate(rows, axis=0).astype(BF16)
    value = lax.dot_general(order_ref[...], value, (((0,), (0,)), ((), ())), preferred_element_type=F32)
    out_ref[...] = value.astype(BF16).reshape(out_ref.shape)


def local_call(kernel, out_shape, scratch, flops, *operands):
    total = sum(value.size * value.dtype.itemsize for value in operands)
    total += sum(math.prod(o.shape) * o.dtype.itemsize for o in jax.tree.leaves(out_shape))
    return pl.pallas_call(
        kernel,
        out_shape=out_shape,
        in_specs=[pl.BlockSpec(memory_space=pltpu.VMEM)] * len(operands),
        out_specs=jax.tree.map(lambda _: pl.BlockSpec(memory_space=pltpu.VMEM), out_shape),
        scratch_shapes=scratch,
        cost_estimate=pl.CostEstimate(flops=flops, bytes_accessed=total, transcendentals=0),
        compiler_params=pltpu.CompilerParams(vmem_limit_bytes=50 * 1024 * 1024),
    )(*operands)


def ring(value, step):
    count = lax.axis_size("space")
    return lax.ppermute(value, "space", [(i, (i + step) % count) for i in range(count)])


def ring_shards(inputs, pre_act, out_grad, weight_one, weight_two):
    samples, chans, planes, cells = inputs.shape
    count = lax.axis_size("space")
    og = math.isqrt(out_grad.shape[3])
    width = og * og
    half = 4 * chans
    block = 9 * chans
    all_chans = weight_one.shape[4]
    all_out = weight_two.shape[4]
    w1 = weight_one.reshape(3 * block, all_chans)
    w2 = weight_two.reshape(3 * block, all_out)
    matrix = jnp.asarray(split_matrix(og), BF16)
    shape = jax.ShapeDtypeStruct

    grads = lax.all_gather(out_grad.reshape(-1, width), "chan", axis=0, tiled=True)
    xp, hp = local_call(
        lambda *r: split_kernel(og, planes, chans, *r),
        [shape((planes * half, width), BF16)] * 2,
        [],
        2 * 2 * planes * half * width * width,
        inputs.reshape(chans, planes * cells),
        pre_act.reshape(chans, planes * cells),
        matrix,
    )
    grads_next = ring(grads, count - 1)
    up = [(i, i + 1) for i in range(count - 1)]
    down = [(i + 1, i) for i in range(count - 1)]
    x_prev = lax.ppermute(xp[half:], "space", up)
    x_next = lax.ppermute(xp[:half], "space", down)

    p_own = local_call(
        lambda *r: own_grad_kernel(og, chans, count, *r),
        shape((2 * half, width), BF16),
        [],
        2 * 3 * block * all_out * width,
        w2,
        grads,
        grads_next,
        hp,
    )
    a_own = lax.all_gather(p_own, "chan", axis=0)

    all_grads = [grads] + [ring(grads, step) for step in range(1, count - 1)] + [grads_next]
    all_hp = [hp] + [ring(hp, step) for step in range(1, count)]

    rows = -(-3 * block // (16 * count)) * 16
    pieces = local_call(
        lambda *r: filter_one_kernel(og, chans, count, rows, *r),
        [shape((rows, all_chans), F32)] + [shape((rows, all_chans), BF16)] * (count - 1),
        [
            pltpu.VMEM((2 * all_chans, 4 * width), BF16),
            pltpu.VMEM((4, block, 4 * width), BF16),
            pltpu.VMEM((count * rows, all_chans), F32),
        ],
        2 * 6 * block * all_chans * cells,
        a_own,
        x_prev,
        xp,
        x_next,
    )
    total = pieces[0]
    for step in range(1, count):
        total = total + ring(pieces[step], step).astype(F32)
    scale_one = 1.0 / math.sqrt(samples * planes * count * cells)
    scale_two = 1.0 / math.sqrt(samples * out_grad.shape[2] * count * width)
    total = (total * scale_one).astype(BF16)

    p_rim = local_call(
        lambda *r: rim_grad_kernel(og, chans, count, *r),
        shape((2 * half, width), BF16),
        [],
        2 * 3 * block * all_out * width,
        w2,
        all_grads[1],
        grads,
        grads_next,
        all_hp[1],
        all_hp[count - 1],
    )
    a_rim = lax.all_gather(p_rim, "chan", axis=0)
    in_grad = local_call(
        lambda *r: in_grad_kernel(og, chans, *r),
        shape((chans, planes * cells), BF16),
        [pltpu.VMEM((4 * all_chans, 4 * width), BF16)],
        2 * 6 * block * all_chans * cells,
        w1,
        a_own,
        a_rim,
        matrix,
    )
    filter_two = local_call(
        lambda *r: filter_two_kernel(og, chans, count, scale_two, *r),
        shape((3 * block, all_out), F32),
        [
            pltpu.VMEM((count, all_out, width), BF16),
            pltpu.VMEM((count, block, width), BF16),
            pltpu.VMEM((count, block, width), BF16),
        ],
        2 * 3 * count * block * all_out * width,
        *all_grads,
        *all_hp,
    )
    filter_one = local_call(
        lambda *r: place_kernel(count, rows, *r),
        shape((3 * block, all_chans), F32),
        [pltpu.VMEM((count * rows, all_chans), F32)],
        0,
        total,
        *[ring(total, step) for step in range(1, count)],
    )
    return (
        in_grad.reshape(samples, chans, planes, cells),
        filter_one.reshape(3, 3, 3, chans, all_chans),
        filter_two.reshape(3, 3, 3, chans, all_out),
    )


def spread(value, before_last=()):
    count = lax.axis_size("chan")
    found = {0: value}
    bit = count // 2
    while bit:
        pairs = [(i, i ^ bit) for i in range(count)]
        if bit == 1 and before_last:
            for mask in found:
                if mask:
                    found[mask] = lax.optimization_barrier((found[mask], *before_last))[0]
        found.update({mask ^ bit: lax.ppermute(item, "chan", pairs) for mask, item in found.items()})
        bit //= 2
    return [found[mask] for mask in range(count)]


def square_shards(inputs, pre_act, out_grad, weight_one, weight_two):
    samples, chans, planes, cells = inputs.shape
    count = lax.axis_size("space")
    og = math.isqrt(out_grad.shape[3])
    width = og * og
    half = 4 * chans
    block = 9 * chans
    all_chans = weight_one.shape[4]
    all_out = weight_two.shape[4]
    w1 = weight_one.reshape(3 * block, all_chans)
    w2 = weight_two.reshape(3 * block, all_out)
    matrix = jnp.asarray(split_matrix(og), BF16)
    shape = jax.ShapeDtypeStruct
    both = ("space", "chan")
    scale_one = 1.0 / math.sqrt(samples * planes * count * cells)
    scale_two = 1.0 / math.sqrt(samples * out_grad.shape[2] * count * width)

    order = jnp.asarray(plane_matrix(chans, planes), BF16)
    near = out_grad.reshape(-1, width)
    around = [near] + [ring(near, step) for step in range(1, count)]
    turn = [(mixed(j, count) * count + mixed(a, count), a * count + j) for a in range(count) for j in range(count)]
    x_turned = lax.ppermute(inputs.reshape(chans, planes, cells), both, turn)
    packed = local_call(pack_kernel, shape((count * near.shape[0], width), BF16), [], 0, *around)
    gate = pre_act.reshape(chans, planes, cells)
    gate, packed = lax.optimization_barrier((gate, packed))
    gates = [gate] + [ring(gate, step) for step in range(1, count)]
    grads = lax.all_gather(packed, "chan", axis=0)
    x_all = lax.all_gather(x_turned, "chan", axis=0)
    rows = block_rows(chans)
    p_local, grads, act, piece = local_call(
        lambda *r: all_grad_kernel(og, chans, count, scale_one, *r),
        [
            shape((4, half, width), BF16),
            shape((count, all_out, width), BF16),
            shape((count, planes * half, width), BF16),
            shape((rows, all_chans), BF16),
        ],
        [
            pltpu.VMEM((count, planes * half, width), BF16),
            pltpu.VMEM((planes * count + 2, half, width), BF16),
            pltpu.VMEM((count, planes * half, width), BF16),
            pltpu.VMEM(((planes * count + 3) * chans, 4 * width), BF16),
            pltpu.VMEM((2, block, 4 * width), BF16),
        ],
        2 * 3 * count * block * (all_out * width + all_chans * cells),
        w2,
        matrix,
        order,
        grads,
        *gates,
        x_all,
    )
    pieces = []
    for step in range(count):
        pairs = [(a * count + j, (j + step) % count * count + mixed(a, count)) for a in range(count) for j in range(count)]
        pieces.append(lax.ppermute(piece, both, pairs))
    near_p = spread(p_local, pieces)
    filter_two = local_call(
        lambda *r: filter_two_square_kernel(og, chans, count, scale_two, *r),
        shape((3 * block, all_out), F32),
        [
            pltpu.VMEM((count, block, width), BF16),
            pltpu.VMEM((count, block, width), BF16),
        ],
        2 * 3 * count * block * all_out * width,
        grads,
        act,
    )
    in_grad = local_call(
        lambda *r: in_grad_square_kernel(og, chans, count, *r),
        shape((chans, planes, cells), BF16),
        [pltpu.VMEM((4 * all_chans, 4 * width), BF16)],
        2 * 6 * block * all_chans * cells,
        w1,
        matrix,
        order,
        *near_p,
    )
    filter_one = local_call(
        lambda *r: join_kernel(chans, count, *r),
        shape((3 * block, all_chans), F32),
        [pltpu.VMEM((count, rows, all_chans), F32)],
        0,
        *pieces,
    )
    return (
        in_grad.reshape(samples, chans, planes, cells),
        filter_one.reshape(3, 3, 3, chans, all_chans),
        filter_two.reshape(3, 3, 3, chans, all_out),
    )


def shards(*arguments):
    count = lax.axis_size("space")
    square = count == lax.axis_size("chan") and 4 * arguments[0].shape[1] == arguments[3].shape[4]
    return (square_shards if square else ring_shards)(*arguments)


def solution(mesh):
    in_specs = (
        P("groups", "chan", "space", None),
        P("groups", "chan", "space", None),
        P("groups", "chan", "space", None),
        P(None, None, None, "chan", None),
        P(None, None, None, "chan", None),
    )
    out_specs = (
        P("groups", "chan", "space", None),
        P("groups", None, None, "chan", None),
        P("groups", None, None, "chan", None),
    )
    return jax.shard_map(shards, mesh=mesh, in_specs=in_specs, out_specs=out_specs, check_vma=False)
```

```python
import math

import jax
import jax.numpy as jnp
import numpy as np
from jax import lax
from jax.experimental import pallas as pl
from jax.experimental.pallas import tpu as pltpu
from jax.sharding import PartitionSpec as P

leak_slope = 0.3
F32 = jnp.float32
BF16 = jnp.bfloat16
CONTRACT_LAST = (((1,), (1,)), ((), ()))


def moved(value, rows, cols, og):
    if rows == 0 and cols == 0:
        return value
    width = og * og
    value = value.astype(F32)
    lane = lax.broadcasted_iota(jnp.int32, value.shape, 1)
    rolled = pltpu.roll(value, (-(rows * og + cols)) % width, 1)
    keep = None
    for step, place in ((rows, lane // og), (cols, lane % og)):
        if step:
            good = place < og - 1 if step > 0 else place > 0
            keep = good if keep is None else keep & good
    return jnp.where(keep, rolled, 0.0)


def neighbour(parity, step):
    place = parity + step
    return place % 2, place // 2


def leaky(value, gate):
    return jnp.where(gate > 0, value, leak_slope * value)


def lane_matrix(og):
    width = og * og
    cell = lax.broadcasted_iota(jnp.int32, (width, width), 0)
    place = lax.broadcasted_iota(jnp.int32, (width, width), 1)
    row, col = cell // (2 * og), cell % (2 * og)
    target = (row % 2 * 2 + col % 2) * (width // 4) + row // 2 * og + col // 2
    return jnp.where(place == target, 1.0, 0.0).astype(BF16)


def order_matrix(chans, planes):
    rows = chans * planes
    place = lax.broadcasted_iota(jnp.int32, (rows, rows), 0)
    row = lax.broadcasted_iota(jnp.int32, (rows, rows), 1)
    return jnp.where(place == row % planes * chans + row // planes, 1.0, 0.0).astype(BF16)


def split_matrix(og):
    width = og * og
    grid = 2 * og
    cell = np.arange(width)
    row, col = cell // grid, cell % grid
    place = ((row % 2) * 2 + col % 2) * (width // 4) + (row // 2) * og + col // 2
    return (place[:, None] == np.arange(width)[None, :]).astype(np.float32)


def split_kernel(og, planes, chans, x_ref, h_ref, e_ref, xp_ref, hp_ref):
    width = og * og
    part = width // 4
    matrix = e_ref[...]
    for source, target in ((x_ref, xp_ref), (h_ref, hp_ref)):
        value = source[...]
        stacked = jnp.concatenate([value[:, i * width : (i + 1) * width] for i in range(4 * planes)], axis=0)
        sorted_cells = jnp.dot(stacked, matrix, preferred_element_type=F32)
        for plane in range(planes):
            for parity in range(4):
                pieces = [
                    sorted_cells[(plane * 4 + i) * chans : (plane * 4 + i + 1) * chans, parity * part : (parity + 1) * part]
                    for i in range(4)
                ]
                at = (plane * 4 + parity) * chans
                target[at : at + chans, :] = jnp.concatenate(pieces, axis=1).astype(BF16)


def transposed_taps(taps, chans, og):
    def tap(row, col):
        at = (row * 3 + col) * chans
        return taps[at : at + chans]

    return [
        tap(1, 1),
        tap(1, 2) + moved(tap(1, 0), 0, 1, og),
        tap(2, 1) + moved(tap(0, 1), 1, 0, og),
        tap(2, 2) + moved(tap(0, 2), 1, 0, og) + moved(tap(2, 0), 0, 1, og) + moved(tap(0, 0), 1, 1, og),
    ]


def plane_grad(w_ref, near, after, gates, chans, og, out_ref, at, live):
    block = 9 * chans
    if after is None:
        taps = jnp.dot(w_ref[block : 2 * block, :], near, preferred_element_type=F32)
    else:
        taps = jnp.dot(w_ref[2 * block : 3 * block, :], near, preferred_element_type=F32)
        taps = taps + jnp.dot(w_ref[0:block, :], after, preferred_element_type=F32)
    for parity, value in enumerate(transposed_taps(taps, chans, og)):
        gate = gates[parity * chans : (parity + 1) * chans].astype(F32)
        value = leaky(value, gate)
        if live is not None:
            value = jnp.where(live, value, 0.0)
        out_ref[at + parity * chans : at + (parity + 1) * chans, :] = value.astype(BF16)


def own_grad_kernel(og, chans, count, w_ref, g_ref, gn_ref, hp_ref, p_ref):
    s = lax.axis_index("space")
    half = 4 * chans
    here = g_ref[...]
    after = jnp.where(s < count - 1, gn_ref[...].astype(F32), 0.0).astype(BF16)
    plane_grad(w_ref, here, None, hp_ref[0:half, :], chans, og, p_ref, 0, None)
    plane_grad(w_ref, here, after, hp_ref[half : 2 * half, :], chans, og, p_ref, half, None)


def rim_grad_kernel(og, chans, count, w_ref, gp_ref, g_ref, gn_ref, hp_prev_ref, hp_next_ref, p_ref):
    s = lax.axis_index("space")
    half = 4 * chans
    plane_grad(w_ref, gp_ref[...], g_ref[...], hp_prev_ref[half : 2 * half, :], chans, og, p_ref, 0, s > 0)
    plane_grad(w_ref, gn_ref[...], None, hp_next_ref[0:half, :], chans, og, p_ref, half, s < count - 1)


def window_rows(blocks, parity, og):
    rows = []
    for row_tap in range(3):
        row_parity, row_move = neighbour(parity // 2, row_tap - 1)
        for col_tap in range(3):
            col_parity, col_move = neighbour(parity % 2, col_tap - 1)
            rows.append(blocks[(row_parity * 2 + col_parity, row_move, col_move)])
    return jnp.concatenate(rows, axis=0)


def moved_blocks(plane, chans, og):
    result = {}
    for parity in range(4):
        value = plane[parity * chans : (parity + 1) * chans]
        for row_move in (0, -1 if parity // 2 else 1):
            for col_move in (0, -1 if parity % 2 else 1):
                result[parity, row_move, col_move] = moved(value, row_move, col_move, og).astype(BF16)
    return result


def filter_one_kernel(og, chans, count, rows, a_ref, xprev_ref, xp_ref, xnext_ref, own_ref, *rest):
    outs, (p_scr, x_scr, f_scr) = rest[: count - 1], rest[count - 1 :]
    s = lax.axis_index("space")
    width = og * og
    shards = a_ref.shape[0]
    all_chans = shards * chans
    half = 4 * chans
    block = 9 * chans
    for plane in range(2):
        for parity in range(4):
            for j in range(shards):
                at = plane * all_chans + j * chans
                p_scr[at : at + chans, parity * width : (parity + 1) * width] = a_ref[
                    j, (plane * 4 + parity) * chans : (plane * 4 + parity + 1) * chans, :
                ]
    planes = (xprev_ref[...], xp_ref[0:half, :], xp_ref[half : 2 * half, :], xnext_ref[...])
    ends = ((0, all_chans), (0, 2 * all_chans), (0, 2 * all_chans), (all_chans, 2 * all_chans))
    products = []
    for index, plane in enumerate(planes):
        blocks = moved_blocks(plane, chans, og)
        for parity in range(4):
            x_scr[index, :, parity * width : (parity + 1) * width] = window_rows(blocks, parity, og)
        first, last = ends[index]
        products.append(
            lax.dot_general(x_scr[index], p_scr[first:last, :], CONTRACT_LAST, preferred_element_type=F32)
        )
    before, even, odd, after = products
    f_scr[0:block, :] = before + even[:, all_chans:]
    f_scr[block : 2 * block, :] = even[:, :all_chans] + odd[:, all_chans:]
    f_scr[2 * block : 3 * block, :] = odd[:, :all_chans] + after
    if count * rows > 3 * block:
        f_scr[3 * block :, :] = jnp.zeros((count * rows - 3 * block, all_chans), F32)

    def piece(step):
        at = pl.multiple_of(lax.rem(s + step, count) * rows, 16)
        return f_scr[pl.ds(at, rows), :]

    own_ref[...] = piece(0)
    for step, out in enumerate(outs):
        out[...] = piece(step + 1).astype(BF16)


def in_grad_kernel(og, chans, w_ref, a_ref, r_ref, e_ref, out_ref, p_scr):
    width = og * og
    shards = a_ref.shape[0]
    all_chans = shards * chans
    for index in range(4):
        source, first = (r_ref, index // 3) if index in (0, 3) else (a_ref, index - 1)
        for parity in range(4):
            for j in range(shards):
                at = index * all_chans + j * chans
                p_scr[at : at + chans, parity * width : (parity + 1) * width] = source[
                    j, (first * 4 + parity) * chans : (first * 4 + parity + 1) * chans, :
                ]
    joined = in_grad_planes(og, chans, all_chans, w_ref, e_ref[...], p_scr)
    for i in range(8):
        out_ref[:, i * width : (i + 1) * width] = joined[i * chans : (i + 1) * chans].astype(BF16)


def in_grad_planes(og, chans, all_chans, w_ref, matrix, p_scr):
    width = og * og
    part = width // 4
    block = 9 * chans
    weights = jnp.concatenate([w_ref[depth * block : (depth + 1) * block, :] for depth in (2, 1, 0)], axis=1)
    stacked = []
    for plane in range(2):
        taps = jnp.dot(
            weights, p_scr[plane * all_chans : (plane + 3) * all_chans, :], preferred_element_type=F32
        )
        sums = []
        for parity in range(4):
            terms = {}
            for row_tap in range(3):
                row_parity, row_move = neighbour(parity // 2, 1 - row_tap)
                for col_tap in range(3):
                    col_parity, col_move = neighbour(parity % 2, 1 - col_tap)
                    at = (row_tap * 3 + col_tap) * chans
                    lane = (row_parity * 2 + col_parity) * width
                    term = taps[at : at + chans, lane : lane + width]
                    key = (row_move, col_move)
                    terms[key] = term if key not in terms else terms[key] + term
            total = None
            for (row_move, col_move), term in terms.items():
                term = moved(term, row_move, col_move, og)
                total = term if total is None else total + term
            sums.append(total)
        for i in range(4):
            stacked.append(
                jnp.concatenate([value[:, i * part : (i + 1) * part] for value in sums], axis=1).astype(BF16)
            )
    return lax.dot_general(jnp.concatenate(stacked, axis=0), matrix, CONTRACT_LAST, preferred_element_type=F32)


def filter_two_kernel(og, chans, count, scale, *refs):
    grads, gates, out_ref = refs[:count], refs[count : 2 * count], refs[2 * count]
    g_scr, even_scr, odd_scr = refs[2 * count + 1 :]
    s = lax.axis_index("space")
    half = 4 * chans
    block = 9 * chans
    for step in range(count):
        at = lax.rem(s + count - step, count)
        g_scr[at] = grads[step][...]
        value = gates[step][...].astype(F32)
        act = leaky(value, value).astype(BF16)
        for plane, target in enumerate((even_scr, odd_scr)):
            blocks = moved_blocks(act[plane * half : (plane + 1) * half], chans, og)
            target[at] = window_rows(blocks, 0, og)
    filter_two_sums(count, block, scale, g_scr, even_scr, odd_scr, out_ref)


def filter_two_square_kernel(og, chans, count, scale, g_ref, act_ref, out_ref, even_scr, odd_scr):
    half = 4 * chans
    for at in range(count):
        for plane, target in enumerate((even_scr, odd_scr)):
            blocks = moved_blocks(act_ref[at, plane * half : (plane + 1) * half, :], chans, og)
            target[at] = window_rows(blocks, 0, og)
    filter_two_sums(count, 9 * chans, scale, g_ref, even_scr, odd_scr, out_ref)


def filter_two_sums(count, block, scale, g_scr, even_scr, odd_scr, out_ref):
    totals = [jnp.zeros((block, g_scr.shape[1]), F32) for _ in range(3)]
    for at in range(count):
        sources = (odd_scr.at[at - 1] if at else None, even_scr.at[at], odd_scr.at[at])
        for depth, source in enumerate(sources):
            if source is not None:
                totals[depth] = totals[depth] + lax.dot_general(
                    source[...], g_scr[at], CONTRACT_LAST, preferred_element_type=F32
                )
    for depth in range(3):
        out_ref[depth * block : (depth + 1) * block, :] = totals[depth] * scale


def place_kernel(count, rows, *refs):
    pieces, out_ref, scr = refs[:count], refs[count], refs[count + 1]
    s = lax.axis_index("space")
    for step, piece in enumerate(pieces):
        at = pl.multiple_of(lax.rem(s + count - step, count) * rows, 16)
        scr[pl.ds(at, rows), :] = piece[...].astype(F32)
    out_ref[...] = scr[0 : out_ref.shape[0], :]


def split_planes(value, order, matrix, chans, planes, og):
    width = og * og
    part = width // 4
    value = value.reshape(chans * planes, 4 * width)
    value = jnp.dot(order, value, preferred_element_type=F32).astype(BF16)
    stacked = jnp.concatenate([value[:, i * width : (i + 1) * width] for i in range(4)], axis=0)
    cells = jnp.dot(stacked, matrix, preferred_element_type=F32)
    rows = chans * planes
    result = []
    for plane in range(planes):
        for parity in range(4):
            pieces = [
                cells[i * rows + plane * chans : i * rows + (plane + 1) * chans, parity * part : (parity + 1) * part]
                for i in range(4)
            ]
            result.append(jnp.concatenate(pieces, axis=1))
    return jnp.concatenate(result, axis=0)


def pack_kernel(*refs):
    sources, out_ref = refs[:-1], refs[-1]
    rows = sources[0].shape[0]
    for step, source in enumerate(sources):
        out_ref[step * rows : (step + 1) * rows, :] = source[...]


def gate_kernel(og, chans, h_ref, out_ref):
    value = split_planes(h_ref[...], order_matrix(chans, 2), lane_matrix(og), chans, 2, og)
    out_ref[...] = value.astype(BF16)


def all_grad_kernel(og, chans, count, scale, w_ref, *refs):
    grads, gates, sources, refs = refs[0], refs[1 : count + 1], refs[count + 1 : 2 * count + 1], refs[2 * count + 1 :]
    local_ref, g_ref, act_ref, piece_ref, h_scr, p_scr, *block_refs = refs
    matrix, order = lane_matrix(og), order_matrix(chans, 2)
    s = lax.axis_index("space")
    half = 4 * chans
    part = grads.shape[1] // count
    for step in range(count):
        at = lax.bitwise_xor(s, step)
        for j in range(count):
            g_ref[at, j * part : (j + 1) * part, :] = grads[j, step * part : (step + 1) * part, :]
        value = gates[step][...]
        h_scr[at] = value
        value = value.astype(F32)
        act_ref[at] = leaky(value, value).astype(BF16)
    empty = jnp.zeros((half, og * og), BF16)
    p_scr[0] = empty
    p_scr[2 * count + 1] = empty
    for q in range(count):
        here = g_ref[q]
        plane_grad(w_ref, here, None, h_scr[q, 0:half, :], chans, og, p_scr.at[2 * q + 1], 0, None)
        after = g_ref[q + 1] if q < count - 1 else jnp.zeros_like(here)
        plane_grad(w_ref, here, after, h_scr[q, half : 2 * half, :], chans, og, p_scr.at[2 * q + 2], 0, None)
    local_ref[...] = p_scr[pl.ds(2 * s, 4)]
    filter_block(og, chans, count, scale, p_scr, matrix, order, sources, piece_ref, *block_refs)


def mixed(index, count):
    return index % 2 * (count // 2) + index // 2


def block_rows(chans):
    return -(-27 * chans // 64) * 16


def filter_block(og, chans, count, scale, p_ref, matrix, order, sources, out_ref, x_ref, p_scr, x_scr):
    i = lax.axis_index("chan")
    width = og * og
    half = 4 * chans
    block = 9 * chans
    lanes = 4 * chans
    planes = 2 * count
    for mask, source in enumerate(sources):
        value = split_planes(source[...], order, matrix, chans, 2, og)
        x_ref[mixed(lax.bitwise_xor(i, mask), count)] = value.astype(BF16)
    empty = jnp.zeros((chans, 4 * width), BF16)
    for index in (0, planes + 1, planes + 2):
        p_scr[index * chans : (index + 1) * chans, :] = empty
    for plane in range(planes):
        at = (plane + 1) * chans
        for parity in range(4):
            p_scr[at : at + chans, parity * width : (parity + 1) * width] = p_ref[
                plane + 1, parity * chans : (parity + 1) * chans, :
            ]
    total = jnp.zeros((block, lanes), F32)
    for plane in range(planes):
        first = (plane % 2) * half
        blocks = moved_blocks(x_ref[plane // 2, first : first + half, :], chans, og)
        for parity in range(4):
            x_scr[plane % 2, :, parity * width : (parity + 1) * width] = window_rows(blocks, parity, og)
        total = total + lax.dot_general(
            x_scr[plane % 2], p_scr[plane * chans : plane * chans + lanes, :], CONTRACT_LAST, preferred_element_type=F32
        )
    total = total * scale
    rows = block_rows(chans)
    tail = total[rows:]
    moved_tail = [pltpu.roll(tail, lanes - (i + 1) * chans, 1) for i in range(3)]
    spare = rows - 3 * (block - rows)
    if spare:
        moved_tail.append(jnp.zeros((spare, lanes), F32))
    lane = lax.broadcasted_iota(jnp.int32, (rows, lanes), 1)
    out_ref[...] = jnp.where(lane < 3 * chans, total[:rows], jnp.concatenate(moved_tail, axis=0)).astype(BF16)


def join_matrix(chans, count):
    lanes = 4 * chans
    result = np.zeros((count * lanes, 4 * lanes), np.float32)
    for j in range(count):
        for group in range(4):
            target = 2 - group if group < 3 else 3
            for c in range(chans):
                result[j * lanes + group * chans + c, target * lanes + j * chans + c] = 1
    return result


def join_kernel(chans, count, m_ref, *refs):
    pieces, out_ref, scr = refs[:count], refs[count], refs[count + 1]
    s = lax.axis_index("space")
    lanes = 4 * chans
    block = 9 * chans
    rows = block_rows(chans)
    rest = block - rows
    for step, piece in enumerate(pieces):
        scr[step] = piece[...]
    side = jnp.concatenate([scr[lax.bitwise_xor(s, j)] for j in range(count)], axis=1)
    joined = jnp.dot(side, m_ref[...], preferred_element_type=F32)
    for depth in range(3):
        out_ref[depth * block : depth * block + rows, :] = joined[:, depth * lanes : (depth + 1) * lanes]
        at = (2 - depth) * rest
        out_ref[depth * block + rows : (depth + 1) * block, :] = joined[at : at + rest, 3 * lanes :]


def in_grad_square_kernel(og, chans, count, w_ref, *refs):
    sources, out_ref, p_scr = refs[:count], refs[count], refs[count + 1]
    i = lax.axis_index("chan")
    width = og * og
    all_chans = count * chans
    for mask, source in enumerate(sources):
        j = lax.bitwise_xor(i, mask)
        for index in range(4):
            at = pl.multiple_of(index * all_chans + j * chans, chans)
            for parity in range(4):
                p_scr[pl.ds(at, chans), parity * width : (parity + 1) * width] = source[
                    index, parity * chans : (parity + 1) * chans, :
                ]
    joined = in_grad_planes(og, chans, all_chans, w_ref, lane_matrix(og), p_scr)
    rows = [
        jnp.concatenate([joined[(plane * 4 + k) * chans : (plane * 4 + k + 1) * chans] for k in range(4)], axis=1)
        for plane in range(2)
    ]
    value = jnp.concatenate(rows, axis=0).astype(BF16)
    value = lax.dot_general(order_matrix(chans, 2), value, (((0,), (0,)), ((), ())), preferred_element_type=F32)
    out_ref[...] = value.astype(BF16).reshape(out_ref.shape)


def local_call(kernel, out_shape, scratch, flops, *operands):
    total = sum(value.size * value.dtype.itemsize for value in operands)
    total += sum(math.prod(o.shape) * o.dtype.itemsize for o in jax.tree.leaves(out_shape))
    return pl.pallas_call(
        kernel,
        out_shape=out_shape,
        in_specs=[pl.BlockSpec(memory_space=pltpu.VMEM)] * len(operands),
        out_specs=jax.tree.map(lambda _: pl.BlockSpec(memory_space=pltpu.VMEM), out_shape),
        scratch_shapes=scratch,
        cost_estimate=pl.CostEstimate(flops=flops, bytes_accessed=total, transcendentals=0),
        compiler_params=pltpu.CompilerParams(vmem_limit_bytes=50 * 1024 * 1024),
    )(*operands)


def ring(value, step):
    count = lax.axis_size("space")
    return lax.ppermute(value, "space", [(i, (i + step) % count) for i in range(count)])


def ring_shards(inputs, pre_act, out_grad, weight_one, weight_two):
    samples, chans, planes, cells = inputs.shape
    count = lax.axis_size("space")
    og = math.isqrt(out_grad.shape[3])
    width = og * og
    half = 4 * chans
    block = 9 * chans
    all_chans = weight_one.shape[4]
    all_out = weight_two.shape[4]
    w1 = weight_one.reshape(3 * block, all_chans)
    w2 = weight_two.reshape(3 * block, all_out)
    matrix = jnp.asarray(split_matrix(og), BF16)
    shape = jax.ShapeDtypeStruct

    grads = lax.all_gather(out_grad.reshape(-1, width), "chan", axis=0, tiled=True)
    xp, hp = local_call(
        lambda *r: split_kernel(og, planes, chans, *r),
        [shape((planes * half, width), BF16)] * 2,
        [],
        2 * 2 * planes * half * width * width,
        inputs.reshape(chans, planes * cells),
        pre_act.reshape(chans, planes * cells),
        matrix,
    )
    grads_next = ring(grads, count - 1)
    up = [(i, i + 1) for i in range(count - 1)]
    down = [(i + 1, i) for i in range(count - 1)]
    x_prev = lax.ppermute(xp[half:], "space", up)
    x_next = lax.ppermute(xp[:half], "space", down)

    p_own = local_call(
        lambda *r: own_grad_kernel(og, chans, count, *r),
        shape((2 * half, width), BF16),
        [],
        2 * 3 * block * all_out * width,
        w2,
        grads,
        grads_next,
        hp,
    )
    a_own = lax.all_gather(p_own, "chan", axis=0)

    all_grads = [grads] + [ring(grads, step) for step in range(1, count - 1)] + [grads_next]
    all_hp = [hp] + [ring(hp, step) for step in range(1, count)]

    rows = -(-3 * block // (16 * count)) * 16
    pieces = local_call(
        lambda *r: filter_one_kernel(og, chans, count, rows, *r),
        [shape((rows, all_chans), F32)] + [shape((rows, all_chans), BF16)] * (count - 1),
        [
            pltpu.VMEM((2 * all_chans, 4 * width), BF16),
            pltpu.VMEM((4, block, 4 * width), BF16),
            pltpu.VMEM((count * rows, all_chans), F32),
        ],
        2 * 6 * block * all_chans * cells,
        a_own,
        x_prev,
        xp,
        x_next,
    )
    total = pieces[0]
    for step in range(1, count):
        total = total + ring(pieces[step], step).astype(F32)
    scale_one = 1.0 / math.sqrt(samples * planes * count * cells)
    scale_two = 1.0 / math.sqrt(samples * out_grad.shape[2] * count * width)
    total = (total * scale_one).astype(BF16)

    p_rim = local_call(
        lambda *r: rim_grad_kernel(og, chans, count, *r),
        shape((2 * half, width), BF16),
        [],
        2 * 3 * block * all_out * width,
        w2,
        all_grads[1],
        grads,
        grads_next,
        all_hp[1],
        all_hp[count - 1],
    )
    a_rim = lax.all_gather(p_rim, "chan", axis=0)
    in_grad = local_call(
        lambda *r: in_grad_kernel(og, chans, *r),
        shape((chans, planes * cells), BF16),
        [pltpu.VMEM((4 * all_chans, 4 * width), BF16)],
        2 * 6 * block * all_chans * cells,
        w1,
        a_own,
        a_rim,
        matrix,
    )
    filter_two = local_call(
        lambda *r: filter_two_kernel(og, chans, count, scale_two, *r),
        shape((3 * block, all_out), F32),
        [
            pltpu.VMEM((count, all_out, width), BF16),
            pltpu.VMEM((count, block, width), BF16),
            pltpu.VMEM((count, block, width), BF16),
        ],
        2 * 3 * count * block * all_out * width,
        *all_grads,
        *all_hp,
    )
    filter_one = local_call(
        lambda *r: place_kernel(count, rows, *r),
        shape((3 * block, all_chans), F32),
        [pltpu.VMEM((count * rows, all_chans), F32)],
        0,
        total,
        *[ring(total, step) for step in range(1, count)],
    )
    return (
        in_grad.reshape(samples, chans, planes, cells),
        filter_one.reshape(3, 3, 3, chans, all_chans),
        filter_two.reshape(3, 3, 3, chans, all_out),
    )


def spread(value, before_last=()):
    count = lax.axis_size("chan")
    found = {0: value}
    bit = count // 2
    while bit:
        pairs = [(i, i ^ bit) for i in range(count)]
        if bit == 1 and before_last:
            for mask in found:
                if mask:
                    found[mask] = lax.optimization_barrier((found[mask], *before_last))[0]
        found.update({mask ^ bit: lax.ppermute(item, "chan", pairs) for mask, item in found.items()})
        bit //= 2
    return [found[mask] for mask in range(count)]


def paired(value, mask):
    return lax.ppermute(value, "space", [(i, i ^ mask) for i in range(lax.axis_size("space"))])


def square_shards(inputs, pre_act, out_grad, weight_one, weight_two):
    samples, chans, planes, cells = inputs.shape
    count = lax.axis_size("space")
    og = math.isqrt(out_grad.shape[3])
    width = og * og
    half = 4 * chans
    block = 9 * chans
    all_chans = weight_one.shape[4]
    all_out = weight_two.shape[4]
    w1 = weight_one.reshape(3 * block, all_chans)
    w2 = weight_two.reshape(3 * block, all_out)
    shape = jax.ShapeDtypeStruct
    both = ("space", "chan")
    scale_one = 1.0 / math.sqrt(samples * planes * count * cells)
    scale_two = 1.0 / math.sqrt(samples * out_grad.shape[2] * count * width)

    near = out_grad.reshape(-1, width)
    around = [near] + [paired(near, step) for step in range(1, count)]
    turn = [(mixed(j, count) * count + mixed(a, count), a * count + j) for a in range(count) for j in range(count)]
    x_turned = lax.ppermute(inputs.reshape(chans, planes, cells), both, turn)
    packed = local_call(pack_kernel, shape((count * near.shape[0], width), BF16), [], 0, *around)
    gate = local_call(
        lambda *r: gate_kernel(og, chans, *r),
        shape((planes * half, width), BF16),
        [],
        2 * planes * half * width * width,
        pre_act.reshape(chans, planes, cells),
    )
    gates = [gate] + [paired(gate, step) for step in range(1, count)]
    grads = lax.all_gather(packed, "chan", axis=0)
    x_all = spread(x_turned, (grads, *gates[1:]))
    rows = block_rows(chans)
    p_local, grads, act, piece = local_call(
        lambda *r: all_grad_kernel(og, chans, count, scale_one, *r),
        [
            shape((4, half, width), BF16),
            shape((count, all_out, width), BF16),
            shape((count, planes * half, width), BF16),
            shape((rows, all_chans), BF16),
        ],
        [
            pltpu.VMEM((count, planes * half, width), BF16),
            pltpu.VMEM((planes * count + 2, half, width), BF16),
            pltpu.VMEM((count, planes * half, width), BF16),
            pltpu.VMEM(((planes * count + 3) * chans, 4 * width), BF16),
            pltpu.VMEM((2, block, 4 * width), BF16),
        ],
        2 * 3 * count * block * (all_out * width + all_chans * cells),
        w2,
        grads,
        *gates,
        *x_all,
    )
    pieces = []
    for step in range(count):
        pairs = [(a * count + j, (j ^ step) * count + mixed(a, count)) for a in range(count) for j in range(count)]
        pieces.append(lax.ppermute(piece, both, pairs))
    filter_two = local_call(
        lambda *r: filter_two_square_kernel(og, chans, count, scale_two, *r),
        shape((3 * block, all_out), F32),
        [
            pltpu.VMEM((count, block, width), BF16),
            pltpu.VMEM((count, block, width), BF16),
        ],
        2 * 3 * count * block * all_out * width,
        grads,
        act,
    )
    near_p = spread(p_local, (*pieces, filter_two))
    in_grad = local_call(
        lambda *r: in_grad_square_kernel(og, chans, count, *r),
        shape((chans, planes, cells), BF16),
        [pltpu.VMEM((4 * all_chans, 4 * width), BF16)],
        2 * 6 * block * all_chans * cells,
        w1,
        *near_p,
    )
    filter_one = local_call(
        lambda *r: join_kernel(chans, count, *r),
        shape((3 * block, all_chans), F32),
        [pltpu.VMEM((count, rows, all_chans), BF16)],
        2 * rows * 16 * all_chans * all_chans,
        jnp.asarray(join_matrix(chans, count), BF16),
        *pieces,
    )
    return (
        in_grad.reshape(samples, chans, planes, cells),
        filter_one.reshape(3, 3, 3, chans, all_chans),
        filter_two.reshape(3, 3, 3, chans, all_out),
    )


def shards(*arguments):
    count = lax.axis_size("space")
    square = count == lax.axis_size("chan") and count & (count - 1) == 0 and 4 * arguments[0].shape[1] == arguments[3].shape[4]
    return (square_shards if square else ring_shards)(*arguments)


def solution(mesh):
    in_specs = (
        P("groups", "chan", "space", None),
        P("groups", "chan", "space", None),
        P("groups", "chan", "space", None),
        P(None, None, None, "chan", None),
        P(None, None, None, "chan", None),
    )
    out_specs = (
        P("groups", "chan", "space", None),
        P("groups", None, None, "chan", None),
        P("groups", None, None, "chan", None),
    )
    return jax.shard_map(shards, mesh=mesh, in_specs=in_specs, out_specs=out_specs, check_vma=False)
```

```python
import math

import jax
import jax.numpy as jnp
import numpy as np
from jax import lax
from jax.experimental import pallas as pl
from jax.experimental.pallas import tpu as pltpu
from jax.sharding import PartitionSpec as P

leak_slope = 0.3
F32 = jnp.float32
BF16 = jnp.bfloat16
CONTRACT_LAST = (((1,), (1,)), ((), ()))


def moved(value, rows, cols, og):
    if rows == 0 and cols == 0:
        return value
    width = og * og
    value = value.astype(F32)
    lane = lax.broadcasted_iota(jnp.int32, value.shape, 1)
    rolled = pltpu.roll(value, (-(rows * og + cols)) % width, 1)
    keep = None
    for step, place in ((rows, lane // og), (cols, lane % og)):
        if step:
            good = place < og - 1 if step > 0 else place > 0
            keep = good if keep is None else keep & good
    return jnp.where(keep, rolled, 0.0)


def neighbour(parity, step):
    place = parity + step
    return place % 2, place // 2


def leaky(value, gate):
    return jnp.where(gate > 0, value, leak_slope * value)


def lane_matrix(og):
    width = og * og
    cell = lax.broadcasted_iota(jnp.int32, (width, width), 0)
    place = lax.broadcasted_iota(jnp.int32, (width, width), 1)
    row, col = cell // (2 * og), cell % (2 * og)
    target = (row % 2 * 2 + col % 2) * (width // 4) + row // 2 * og + col // 2
    return jnp.where(place == target, 1.0, 0.0).astype(BF16)


def order_matrix(chans, planes):
    rows = chans * planes
    place = lax.broadcasted_iota(jnp.int32, (rows, rows), 0)
    row = lax.broadcasted_iota(jnp.int32, (rows, rows), 1)
    return jnp.where(place == row % planes * chans + row // planes, 1.0, 0.0).astype(BF16)


def split_matrix(og):
    width = og * og
    grid = 2 * og
    cell = np.arange(width)
    row, col = cell // grid, cell % grid
    place = ((row % 2) * 2 + col % 2) * (width // 4) + (row // 2) * og + col // 2
    return (place[:, None] == np.arange(width)[None, :]).astype(np.float32)


def split_kernel(og, planes, chans, x_ref, h_ref, e_ref, xp_ref, hp_ref):
    width = og * og
    part = width // 4
    matrix = e_ref[...]
    for source, target in ((x_ref, xp_ref), (h_ref, hp_ref)):
        value = source[...]
        stacked = jnp.concatenate([value[:, i * width : (i + 1) * width] for i in range(4 * planes)], axis=0)
        sorted_cells = jnp.dot(stacked, matrix, preferred_element_type=F32)
        for plane in range(planes):
            for parity in range(4):
                pieces = [
                    sorted_cells[(plane * 4 + i) * chans : (plane * 4 + i + 1) * chans, parity * part : (parity + 1) * part]
                    for i in range(4)
                ]
                at = (plane * 4 + parity) * chans
                target[at : at + chans, :] = jnp.concatenate(pieces, axis=1).astype(BF16)


def transposed_taps(taps, chans, og):
    def tap(row, col):
        at = (row * 3 + col) * chans
        return taps[at : at + chans]

    return [
        tap(1, 1),
        tap(1, 2) + moved(tap(1, 0), 0, 1, og),
        tap(2, 1) + moved(tap(0, 1), 1, 0, og),
        tap(2, 2) + moved(tap(0, 2), 1, 0, og) + moved(tap(2, 0), 0, 1, og) + moved(tap(0, 0), 1, 1, og),
    ]


def plane_grad(w_ref, near, after, gates, chans, og, out_ref, at, live):
    block = 9 * chans
    if after is None:
        taps = jnp.dot(w_ref[block : 2 * block, :], near, preferred_element_type=F32)
    else:
        taps = jnp.dot(w_ref[2 * block : 3 * block, :], near, preferred_element_type=F32)
        taps = taps + jnp.dot(w_ref[0:block, :], after, preferred_element_type=F32)
    for parity, value in enumerate(transposed_taps(taps, chans, og)):
        gate = gates[parity * chans : (parity + 1) * chans].astype(F32)
        value = leaky(value, gate)
        if live is not None:
            value = jnp.where(live, value, 0.0)
        out_ref[at + parity * chans : at + (parity + 1) * chans, :] = value.astype(BF16)


def own_grad_kernel(og, chans, count, w_ref, g_ref, gn_ref, hp_ref, p_ref):
    s = lax.axis_index("space")
    half = 4 * chans
    here = g_ref[...]
    after = jnp.where(s < count - 1, gn_ref[...].astype(F32), 0.0).astype(BF16)
    plane_grad(w_ref, here, None, hp_ref[0:half, :], chans, og, p_ref, 0, None)
    plane_grad(w_ref, here, after, hp_ref[half : 2 * half, :], chans, og, p_ref, half, None)


def rim_grad_kernel(og, chans, count, w_ref, gp_ref, g_ref, gn_ref, hp_prev_ref, hp_next_ref, p_ref):
    s = lax.axis_index("space")
    half = 4 * chans
    plane_grad(w_ref, gp_ref[...], g_ref[...], hp_prev_ref[half : 2 * half, :], chans, og, p_ref, 0, s > 0)
    plane_grad(w_ref, gn_ref[...], None, hp_next_ref[0:half, :], chans, og, p_ref, half, s < count - 1)


def window_rows(blocks, parity, og):
    rows = []
    for row_tap in range(3):
        row_parity, row_move = neighbour(parity // 2, row_tap - 1)
        for col_tap in range(3):
            col_parity, col_move = neighbour(parity % 2, col_tap - 1)
            rows.append(blocks[(row_parity * 2 + col_parity, row_move, col_move)])
    return jnp.concatenate(rows, axis=0)


def moved_blocks(plane, chans, og):
    result = {}
    for parity in range(4):
        value = plane[parity * chans : (parity + 1) * chans]
        for row_move in (0, -1 if parity // 2 else 1):
            for col_move in (0, -1 if parity % 2 else 1):
                result[parity, row_move, col_move] = moved(value, row_move, col_move, og).astype(BF16)
    return result


def filter_one_kernel(og, chans, count, rows, a_ref, xprev_ref, xp_ref, xnext_ref, own_ref, *rest):
    outs, (p_scr, x_scr, f_scr) = rest[: count - 1], rest[count - 1 :]
    s = lax.axis_index("space")
    width = og * og
    shards = a_ref.shape[0]
    all_chans = shards * chans
    half = 4 * chans
    block = 9 * chans
    for plane in range(2):
        for parity in range(4):
            for j in range(shards):
                at = plane * all_chans + j * chans
                p_scr[at : at + chans, parity * width : (parity + 1) * width] = a_ref[
                    j, (plane * 4 + parity) * chans : (plane * 4 + parity + 1) * chans, :
                ]
    planes = (xprev_ref[...], xp_ref[0:half, :], xp_ref[half : 2 * half, :], xnext_ref[...])
    ends = ((0, all_chans), (0, 2 * all_chans), (0, 2 * all_chans), (all_chans, 2 * all_chans))
    products = []
    for index, plane in enumerate(planes):
        blocks = moved_blocks(plane, chans, og)
        for parity in range(4):
            x_scr[index, :, parity * width : (parity + 1) * width] = window_rows(blocks, parity, og)
        first, last = ends[index]
        products.append(
            lax.dot_general(x_scr[index], p_scr[first:last, :], CONTRACT_LAST, preferred_element_type=F32)
        )
    before, even, odd, after = products
    f_scr[0:block, :] = before + even[:, all_chans:]
    f_scr[block : 2 * block, :] = even[:, :all_chans] + odd[:, all_chans:]
    f_scr[2 * block : 3 * block, :] = odd[:, :all_chans] + after
    if count * rows > 3 * block:
        f_scr[3 * block :, :] = jnp.zeros((count * rows - 3 * block, all_chans), F32)

    def piece(step):
        at = pl.multiple_of(lax.rem(s + step, count) * rows, 16)
        return f_scr[pl.ds(at, rows), :]

    own_ref[...] = piece(0)
    for step, out in enumerate(outs):
        out[...] = piece(step + 1).astype(BF16)


def in_grad_kernel(og, chans, w_ref, a_ref, r_ref, e_ref, out_ref, p_scr):
    width = og * og
    shards = a_ref.shape[0]
    all_chans = shards * chans
    for index in range(4):
        source, first = (r_ref, index // 3) if index in (0, 3) else (a_ref, index - 1)
        for parity in range(4):
            for j in range(shards):
                at = index * all_chans + j * chans
                p_scr[at : at + chans, parity * width : (parity + 1) * width] = source[
                    j, (first * 4 + parity) * chans : (first * 4 + parity + 1) * chans, :
                ]
    joined = in_grad_planes(og, chans, all_chans, w_ref, e_ref[...], p_scr)
    for i in range(8):
        out_ref[:, i * width : (i + 1) * width] = joined[i * chans : (i + 1) * chans].astype(BF16)


def in_grad_planes(og, chans, all_chans, w_ref, matrix, p_scr):
    width = og * og
    part = width // 4
    block = 9 * chans
    empty = jnp.zeros((block, all_chans), BF16)
    weights = [w_ref[depth * block : (depth + 1) * block, :] for depth in (2, 1, 0)]
    weights = jnp.concatenate(
        [jnp.concatenate(weights + [empty], axis=1), jnp.concatenate([empty] + weights, axis=1)], axis=0
    )
    both = jnp.dot(weights, p_scr[...], preferred_element_type=F32)
    stacked = []
    for plane in range(2):
        taps = both[plane * block : (plane + 1) * block]
        sums = []
        for parity in range(4):
            terms = {}
            for row_tap in range(3):
                row_parity, row_move = neighbour(parity // 2, 1 - row_tap)
                for col_tap in range(3):
                    col_parity, col_move = neighbour(parity % 2, 1 - col_tap)
                    at = (row_tap * 3 + col_tap) * chans
                    lane = (row_parity * 2 + col_parity) * width
                    term = taps[at : at + chans, lane : lane + width]
                    key = (row_move, col_move)
                    terms[key] = term if key not in terms else terms[key] + term
            total = None
            for (row_move, col_move), term in terms.items():
                term = moved(term, row_move, col_move, og)
                total = term if total is None else total + term
            sums.append(total)
        for i in range(4):
            stacked.append(
                jnp.concatenate([value[:, i * part : (i + 1) * part] for value in sums], axis=1).astype(BF16)
            )
    return lax.dot_general(jnp.concatenate(stacked, axis=0), matrix, CONTRACT_LAST, preferred_element_type=F32)


def filter_two_kernel(og, chans, count, scale, *refs):
    grads, gates, out_ref = refs[:count], refs[count : 2 * count], refs[2 * count]
    g_scr, even_scr, odd_scr = refs[2 * count + 1 :]
    s = lax.axis_index("space")
    half = 4 * chans
    block = 9 * chans
    for step in range(count):
        at = lax.rem(s + count - step, count)
        g_scr[at] = grads[step][...]
        value = gates[step][...].astype(F32)
        act = leaky(value, value).astype(BF16)
        for plane, target in enumerate((even_scr, odd_scr)):
            blocks = moved_blocks(act[plane * half : (plane + 1) * half], chans, og)
            target[at] = window_rows(blocks, 0, og)
    filter_two_sums(count, block, scale, g_scr, even_scr, odd_scr, out_ref)


def filter_two_square_kernel(og, chans, count, scale, g_ref, act_ref, out_ref, even_scr, odd_scr):
    half = 4 * chans
    for at in range(count):
        for plane, target in enumerate((even_scr, odd_scr)):
            blocks = moved_blocks(act_ref[at, plane * half : (plane + 1) * half, :], chans, og)
            target[at] = window_rows(blocks, 0, og)
    filter_two_sums(count, 9 * chans, scale, g_ref, even_scr, odd_scr, out_ref)


def filter_two_sums(count, block, scale, g_scr, even_scr, odd_scr, out_ref):
    totals = [jnp.zeros((block, g_scr.shape[1]), F32) for _ in range(3)]
    for at in range(count):
        sources = (odd_scr.at[at - 1] if at else None, even_scr.at[at], odd_scr.at[at])
        for depth, source in enumerate(sources):
            if source is not None:
                totals[depth] = totals[depth] + lax.dot_general(
                    source[...], g_scr[at], CONTRACT_LAST, preferred_element_type=F32
                )
    for depth in range(3):
        out_ref[depth * block : (depth + 1) * block, :] = totals[depth] * scale


def place_kernel(count, rows, *refs):
    pieces, out_ref, scr = refs[:count], refs[count], refs[count + 1]
    s = lax.axis_index("space")
    for step, piece in enumerate(pieces):
        at = pl.multiple_of(lax.rem(s + count - step, count) * rows, 16)
        scr[pl.ds(at, rows), :] = piece[...].astype(F32)
    out_ref[...] = scr[0 : out_ref.shape[0], :]


def split_planes(value, order, matrix, chans, planes, og):
    width = og * og
    part = width // 4
    value = value.reshape(chans * planes, 4 * width)
    value = jnp.dot(order, value, preferred_element_type=F32).astype(BF16)
    stacked = jnp.concatenate([value[:, i * width : (i + 1) * width] for i in range(4)], axis=0)
    cells = jnp.dot(stacked, matrix, preferred_element_type=F32)
    rows = chans * planes
    result = []
    for plane in range(planes):
        for parity in range(4):
            pieces = [
                cells[i * rows + plane * chans : i * rows + (plane + 1) * chans, parity * part : (parity + 1) * part]
                for i in range(4)
            ]
            result.append(jnp.concatenate(pieces, axis=1))
    return jnp.concatenate(result, axis=0)


def pack_kernel(*refs):
    sources, out_ref = refs[:-1], refs[-1]
    rows = sources[0].shape[0]
    for step, source in enumerate(sources):
        out_ref[step * rows : (step + 1) * rows, :] = source[...]


def gate_kernel(og, chans, h_ref, out_ref):
    value = split_planes(h_ref[...], order_matrix(chans, 2), lane_matrix(og), chans, 2, og)
    out_ref[...] = value.astype(BF16)


def all_grad_kernel(og, chans, count, w_ref, *refs):
    grads, gates, refs = refs[0], refs[1 : count + 1], refs[count + 1 :]
    local_ref, q_ref, g_ref, act_ref, h_scr = refs
    s = lax.axis_index("space")
    half = 4 * chans
    part = grads.shape[1] // count
    for step in range(count):
        at = lax.bitwise_xor(s, step)
        for j in range(count):
            g_ref[at, j * part : (j + 1) * part, :] = grads[j, step * part : (step + 1) * part, :]
        value = gates[step][...]
        h_scr[at] = value
        value = value.astype(F32)
        act_ref[at] = leaky(value, value).astype(BF16)
    empty = jnp.zeros((chans, q_ref.shape[1]), BF16)
    for index in (0, 2 * count + 1, 2 * count + 2):
        q_ref[index * chans : (index + 1) * chans, :] = empty
    block = 9 * chans
    for q in range(count):
        here = g_ref[q]
        even = jnp.dot(w_ref[block : 2 * block, :], here, preferred_element_type=F32)
        odd = jnp.dot(w_ref[2 * block : 3 * block, :], here, preferred_element_type=F32)
        if q < count - 1:
            odd = odd + jnp.dot(w_ref[0:block, :], g_ref[q + 1], preferred_element_type=F32)
        for plane, value in enumerate((even, odd)):
            row = (2 * q + plane + 1) * chans
            blocks = []
            for parity, term in enumerate(transposed_taps(value, chans, og)):
                at = (plane * 4 + parity) * chans
                blocks.append(leaky(term, h_scr[q, at : at + chans, :].astype(F32)).astype(BF16))
            q_ref[row : row + chans, :] = jnp.concatenate(blocks, axis=1)
    local_ref[...] = q_ref[pl.ds(pl.multiple_of(2 * s * chans, chans), half), :]


def mixed(index, count):
    return index % 2 * (count // 2) + index // 2


def block_rows(chans):
    return -(-27 * chans // 64) * 16


def filter_block_kernel(og, chans, count, scale, q_ref, *refs):
    sources, (out_ref, x_scr) = refs[:count], refs[count:]
    matrix, order = lane_matrix(og), order_matrix(chans, 2)
    i = lax.axis_index("chan")
    width = og * og
    half = 4 * chans
    block = 9 * chans
    lanes = 4 * chans
    across = 2 * count * chans
    for index, source in enumerate(sources):
        value = split_planes(source[...], order, matrix, chans, 2, og)
        for plane in range(2):
            blocks = moved_blocks(value[plane * half : (plane + 1) * half], chans, og)
            at = (2 * index + plane) * block
            for parity in range(4):
                x_scr[at : at + block, parity * width : (parity + 1) * width] = window_rows(blocks, parity, og)
    products = lax.dot_general(
        x_scr[...], q_ref[chans : chans + across, :], CONTRACT_LAST, preferred_element_type=F32
    )
    group = lax.broadcasted_iota(jnp.int32, (block, lanes), 1) // chans
    total = jnp.zeros((block, lanes), F32)
    for mask in range(count):
        for plane in range(2):
            place = 2 * mixed(lax.bitwise_xor(i, mask), count) + plane
            at = (2 * mask + plane) * block
            term = pltpu.roll(products[at : at + block], lax.rem(across + chans - place * chans, across), 1)[:, :lanes]
            inside = (group + place > 0) & (group + place <= 2 * count)
            total = total + jnp.where(inside, term, 0.0)
    total = total * scale
    rows = block_rows(chans)
    tail = total[rows:]
    moved_tail = [pltpu.roll(tail, lanes - (i + 1) * chans, 1) for i in range(3)]
    spare = rows - 3 * (block - rows)
    if spare:
        moved_tail.append(jnp.zeros((spare, lanes), F32))
    lane = lax.broadcasted_iota(jnp.int32, (rows, lanes), 1)
    out_ref[...] = jnp.where(lane < 3 * chans, total[:rows], jnp.concatenate(moved_tail, axis=0)).astype(BF16)


def join_matrix(chans, count):
    lanes = 4 * chans
    result = np.zeros((count * lanes, 4 * lanes), np.float32)
    for j in range(count):
        for group in range(4):
            target = 2 - group if group < 3 else 3
            for c in range(chans):
                result[j * lanes + group * chans + c, target * lanes + j * chans + c] = 1
    return result


def pair_kernel(own_ref, mate_ref, out_ref):
    odd = lax.axis_index("chan") % 2
    rows = own_ref.shape[0]
    out_ref[pl.ds(pl.multiple_of(odd * rows, 16), rows), :] = own_ref[...]
    out_ref[pl.ds(pl.multiple_of((1 - odd) * rows, 16), rows), :] = mate_ref[...]


def join_kernel(chans, count, m_ref, *refs):
    pieces, out_ref, scr = refs[:-2], refs[-2], refs[-1]
    s = lax.axis_index("space")
    lanes = 4 * chans
    block = 9 * chans
    rows = block_rows(chans)
    rest = block - rows
    for step, piece in enumerate(pieces):
        scr[step] = piece[...]
    side = [
        scr[lax.bitwise_xor(s // 2, j // 2), j % 2 * rows : (j % 2 + 1) * rows, :] for j in range(count)
    ]
    joined = jnp.dot(jnp.concatenate(side, axis=1), m_ref[...], preferred_element_type=F32)
    for depth in range(3):
        out_ref[depth * block : depth * block + rows, :] = joined[:, depth * lanes : (depth + 1) * lanes]
        at = (2 - depth) * rest
        out_ref[depth * block + rows : (depth + 1) * block, :] = joined[at : at + rest, 3 * lanes :]


def in_grad_square_kernel(og, chans, count, w_ref, *refs):
    sources, out_ref, p_scr = refs[:count], refs[count], refs[count + 1]
    i = lax.axis_index("chan")
    width = og * og
    all_chans = count * chans
    for mask, source in enumerate(sources):
        j = lax.bitwise_xor(i, mask)
        for index in range(4):
            at = pl.multiple_of(index * all_chans + j * chans, chans)
            p_scr[pl.ds(at, chans), :] = source[index * chans : (index + 1) * chans, :]
    joined = in_grad_planes(og, chans, all_chans, w_ref, lane_matrix(og), p_scr)
    rows = [
        jnp.concatenate([joined[(plane * 4 + k) * chans : (plane * 4 + k + 1) * chans] for k in range(4)], axis=1)
        for plane in range(2)
    ]
    value = jnp.concatenate(rows, axis=0).astype(BF16)
    value = lax.dot_general(order_matrix(chans, 2), value, (((0,), (0,)), ((), ())), preferred_element_type=F32)
    out_ref[...] = value.astype(BF16).reshape(out_ref.shape)


def local_call(kernel, out_shape, scratch, flops, *operands):
    total = sum(value.size * value.dtype.itemsize for value in operands)
    total += sum(math.prod(o.shape) * o.dtype.itemsize for o in jax.tree.leaves(out_shape))
    return pl.pallas_call(
        kernel,
        out_shape=out_shape,
        in_specs=[pl.BlockSpec(memory_space=pltpu.VMEM)] * len(operands),
        out_specs=jax.tree.map(lambda _: pl.BlockSpec(memory_space=pltpu.VMEM), out_shape),
        scratch_shapes=scratch,
        cost_estimate=pl.CostEstimate(flops=flops, bytes_accessed=total, transcendentals=0),
        compiler_params=pltpu.CompilerParams(vmem_limit_bytes=50 * 1024 * 1024),
    )(*operands)


def ring(value, step):
    count = lax.axis_size("space")
    return lax.ppermute(value, "space", [(i, (i + step) % count) for i in range(count)])


def ring_shards(inputs, pre_act, out_grad, weight_one, weight_two):
    samples, chans, planes, cells = inputs.shape
    count = lax.axis_size("space")
    og = math.isqrt(out_grad.shape[3])
    width = og * og
    half = 4 * chans
    block = 9 * chans
    all_chans = weight_one.shape[4]
    all_out = weight_two.shape[4]
    w1 = weight_one.reshape(3 * block, all_chans)
    w2 = weight_two.reshape(3 * block, all_out)
    matrix = jnp.asarray(split_matrix(og), BF16)
    shape = jax.ShapeDtypeStruct

    grads = lax.all_gather(out_grad.reshape(-1, width), "chan", axis=0, tiled=True)
    xp, hp = local_call(
        lambda *r: split_kernel(og, planes, chans, *r),
        [shape((planes * half, width), BF16)] * 2,
        [],
        2 * 2 * planes * half * width * width,
        inputs.reshape(chans, planes * cells),
        pre_act.reshape(chans, planes * cells),
        matrix,
    )
    grads_next = ring(grads, count - 1)
    up = [(i, i + 1) for i in range(count - 1)]
    down = [(i + 1, i) for i in range(count - 1)]
    x_prev = lax.ppermute(xp[half:], "space", up)
    x_next = lax.ppermute(xp[:half], "space", down)

    p_own = local_call(
        lambda *r: own_grad_kernel(og, chans, count, *r),
        shape((2 * half, width), BF16),
        [],
        2 * 3 * block * all_out * width,
        w2,
        grads,
        grads_next,
        hp,
    )
    a_own = lax.all_gather(p_own, "chan", axis=0)

    all_grads = [grads] + [ring(grads, step) for step in range(1, count - 1)] + [grads_next]
    all_hp = [hp] + [ring(hp, step) for step in range(1, count)]

    rows = -(-3 * block // (16 * count)) * 16
    pieces = local_call(
        lambda *r: filter_one_kernel(og, chans, count, rows, *r),
        [shape((rows, all_chans), F32)] + [shape((rows, all_chans), BF16)] * (count - 1),
        [
            pltpu.VMEM((2 * all_chans, 4 * width), BF16),
            pltpu.VMEM((4, block, 4 * width), BF16),
            pltpu.VMEM((count * rows, all_chans), F32),
        ],
        2 * 6 * block * all_chans * cells,
        a_own,
        x_prev,
        xp,
        x_next,
    )
    total = pieces[0]
    for step in range(1, count):
        total = total + ring(pieces[step], step).astype(F32)
    scale_one = 1.0 / math.sqrt(samples * planes * count * cells)
    scale_two = 1.0 / math.sqrt(samples * out_grad.shape[2] * count * width)
    total = (total * scale_one).astype(BF16)

    p_rim = local_call(
        lambda *r: rim_grad_kernel(og, chans, count, *r),
        shape((2 * half, width), BF16),
        [],
        2 * 3 * block * all_out * width,
        w2,
        all_grads[1],
        grads,
        grads_next,
        all_hp[1],
        all_hp[count - 1],
    )
    a_rim = lax.all_gather(p_rim, "chan", axis=0)
    in_grad = local_call(
        lambda *r: in_grad_kernel(og, chans, *r),
        shape((chans, planes * cells), BF16),
        [pltpu.VMEM((4 * all_chans, 4 * width), BF16)],
        2 * 6 * block * all_chans * cells,
        w1,
        a_own,
        a_rim,
        matrix,
    )
    filter_two = local_call(
        lambda *r: filter_two_kernel(og, chans, count, scale_two, *r),
        shape((3 * block, all_out), F32),
        [
            pltpu.VMEM((count, all_out, width), BF16),
            pltpu.VMEM((count, block, width), BF16),
            pltpu.VMEM((count, block, width), BF16),
        ],
        2 * 3 * count * block * all_out * width,
        *all_grads,
        *all_hp,
    )
    filter_one = local_call(
        lambda *r: place_kernel(count, rows, *r),
        shape((3 * block, all_chans), F32),
        [pltpu.VMEM((count * rows, all_chans), F32)],
        0,
        total,
        *[ring(total, step) for step in range(1, count)],
    )
    return (
        in_grad.reshape(samples, chans, planes, cells),
        filter_one.reshape(3, 3, 3, chans, all_chans),
        filter_two.reshape(3, 3, 3, chans, all_out),
    )


def spread(value, before_last=()):
    count = lax.axis_size("chan")
    found = {0: value}
    bit = count // 2
    while bit:
        pairs = [(i, i ^ bit) for i in range(count)]
        if bit == 1 and before_last:
            for mask in found:
                if mask:
                    found[mask] = lax.optimization_barrier((found[mask], *before_last))[0]
        found.update({mask ^ bit: lax.ppermute(item, "chan", pairs) for mask, item in found.items()})
        bit //= 2
    return [found[mask] for mask in range(count)]


def paired(value, mask):
    return lax.ppermute(value, "space", [(i, i ^ mask) for i in range(lax.axis_size("space"))])


def square_shards(inputs, pre_act, out_grad, weight_one, weight_two):
    samples, chans, planes, cells = inputs.shape
    count = lax.axis_size("space")
    og = math.isqrt(out_grad.shape[3])
    width = og * og
    half = 4 * chans
    block = 9 * chans
    all_chans = weight_one.shape[4]
    all_out = weight_two.shape[4]
    w1 = weight_one.reshape(3 * block, all_chans)
    w2 = weight_two.reshape(3 * block, all_out)
    shape = jax.ShapeDtypeStruct
    both = ("space", "chan")
    scale_one = 1.0 / math.sqrt(samples * planes * count * cells)
    scale_two = 1.0 / math.sqrt(samples * out_grad.shape[2] * count * width)

    near = out_grad.reshape(-1, width)
    around = [near] + [paired(near, step) for step in range(1, count)]
    turn = [(mixed(j, count) * count + mixed(a, count), a * count + j) for a in range(count) for j in range(count)]
    x_turned = lax.ppermute(inputs.reshape(chans, planes, cells), both, turn)
    packed = local_call(pack_kernel, shape((count * near.shape[0], width), BF16), [], 0, *around)
    gate = local_call(
        lambda *r: gate_kernel(og, chans, *r),
        shape((planes * half, width), BF16),
        [],
        2 * planes * half * width * width,
        pre_act.reshape(chans, planes, cells),
    )
    gates = [gate] + [paired(gate, step) for step in range(1, count)]
    grads = lax.all_gather(packed, "chan", axis=0)
    rows = block_rows(chans)
    p_local, p_all, grads, act = local_call(
        lambda *r: all_grad_kernel(og, chans, count, *r),
        [
            shape((half, 4 * width), BF16),
            shape(((planes * count + 3) * chans, 4 * width), BF16),
            shape((count, all_out, width), BF16),
            shape((count, planes * half, width), BF16),
        ],
        [pltpu.VMEM((count, planes * half, width), BF16)],
        2 * 3 * count * block * all_out * width,
        w2,
        grads,
        *gates,
    )
    x_all = spread(x_turned, (p_local,))
    piece = local_call(
        lambda *r: filter_block_kernel(og, chans, count, scale_one, *r),
        shape((rows, all_chans), BF16),
        [pltpu.VMEM((planes * count * block, 4 * width), BF16)],
        2 * 3 * count * block * all_chans * cells,
        p_all,
        *x_all,
    )
    mate = lax.ppermute(piece, "chan", [(j, j ^ 1) for j in range(count)])
    pair = local_call(
        lambda *r: pair_kernel(*r),
        shape((2 * rows, all_chans), BF16),
        [],
        0,
        piece,
        mate,
    )
    pieces = []
    for step in range(count // 2):
        pairs = [
            (a * count + j, (j % 2 + (step ^ j // 2) * 2) * count + mixed(a, count))
            for a in range(count)
            for j in range(count)
        ]
        pieces.append(lax.ppermute(pair, both, pairs))
    filter_two = local_call(
        lambda *r: filter_two_square_kernel(og, chans, count, scale_two, *r),
        shape((3 * block, all_out), F32),
        [
            pltpu.VMEM((count, block, width), BF16),
            pltpu.VMEM((count, block, width), BF16),
        ],
        2 * 3 * count * block * all_out * width,
        grads,
        act,
    )
    near_p = [p_local] + [
        lax.ppermute(p_local, "chan", [(i, i ^ mask) for i in range(count)]) for mask in range(1, count)
    ]
    in_grad = local_call(
        lambda *r: in_grad_square_kernel(og, chans, count, *r),
        shape((chans, planes, cells), BF16),
        [pltpu.VMEM((4 * all_chans, 4 * width), BF16)],
        2 * 6 * block * all_chans * cells,
        w1,
        *near_p,
    )
    filter_one = local_call(
        lambda *r: join_kernel(chans, count, *r),
        shape((3 * block, all_chans), F32),
        [pltpu.VMEM((count // 2, 2 * rows, all_chans), BF16)],
        2 * rows * 16 * all_chans * all_chans,
        jnp.asarray(join_matrix(chans, count), BF16),
        *pieces,
    )
    return (
        in_grad.reshape(samples, chans, planes, cells),
        filter_one.reshape(3, 3, 3, chans, all_chans),
        filter_two.reshape(3, 3, 3, chans, all_out),
    )


def shards(*arguments):
    count = lax.axis_size("space")
    square = count == lax.axis_size("chan") and count & (count - 1) == 0 and 4 * arguments[0].shape[1] == arguments[3].shape[4]
    return (square_shards if square else ring_shards)(*arguments)


def solution(mesh):
    in_specs = (
        P("groups", "chan", "space", None),
        P("groups", "chan", "space", None),
        P("groups", "chan", "space", None),
        P(None, None, None, "chan", None),
        P(None, None, None, "chan", None),
    )
    out_specs = (
        P("groups", "chan", "space", None),
        P("groups", None, None, "chan", None),
        P("groups", None, None, "chan", None),
    )
    return jax.shard_map(shards, mesh=mesh, in_specs=in_specs, out_specs=out_specs, check_vma=False)
```

```python
import math

import jax
import jax.numpy as jnp
import numpy as np
from jax import lax
from jax.experimental import pallas as pl
from jax.experimental.pallas import tpu as pltpu
from jax.sharding import PartitionSpec as P

leak_slope = 0.3
F32 = jnp.float32
BF16 = jnp.bfloat16
CONTRACT_LAST = (((1,), (1,)), ((), ()))


def moved(value, rows, cols, og):
    if rows == 0 and cols == 0:
        return value
    width = og * og
    value = value.astype(F32)
    lane = lax.broadcasted_iota(jnp.int32, value.shape, 1)
    rolled = pltpu.roll(value, (-(rows * og + cols)) % width, 1)
    keep = None
    for step, place in ((rows, lane // og), (cols, lane % og)):
        if step:
            good = place < og - 1 if step > 0 else place > 0
            keep = good if keep is None else keep & good
    return jnp.where(keep, rolled, 0.0)


def neighbour(parity, step):
    place = parity + step
    return place % 2, place // 2


def leaky(value, gate):
    return jnp.where(gate > 0, value, leak_slope * value)


def lane_matrix(og):
    width = og * og
    cell = lax.broadcasted_iota(jnp.int32, (width, width), 0)
    place = lax.broadcasted_iota(jnp.int32, (width, width), 1)
    row, col = cell // (2 * og), cell % (2 * og)
    target = (row % 2 * 2 + col % 2) * (width // 4) + row // 2 * og + col // 2
    return jnp.where(place == target, 1.0, 0.0).astype(BF16)


def order_matrix(chans, planes):
    rows = chans * planes
    place = lax.broadcasted_iota(jnp.int32, (rows, rows), 0)
    row = lax.broadcasted_iota(jnp.int32, (rows, rows), 1)
    return jnp.where(place == row % planes * chans + row // planes, 1.0, 0.0).astype(BF16)


def split_matrix(og):
    width = og * og
    grid = 2 * og
    cell = np.arange(width)
    row, col = cell // grid, cell % grid
    place = ((row % 2) * 2 + col % 2) * (width // 4) + (row // 2) * og + col // 2
    return (place[:, None] == np.arange(width)[None, :]).astype(np.float32)


def split_kernel(og, planes, chans, x_ref, h_ref, e_ref, xp_ref, hp_ref):
    width = og * og
    part = width // 4
    matrix = e_ref[...]
    for source, target in ((x_ref, xp_ref), (h_ref, hp_ref)):
        value = source[...]
        stacked = jnp.concatenate([value[:, i * width : (i + 1) * width] for i in range(4 * planes)], axis=0)
        sorted_cells = jnp.dot(stacked, matrix, preferred_element_type=F32)
        for plane in range(planes):
            for parity in range(4):
                pieces = [
                    sorted_cells[(plane * 4 + i) * chans : (plane * 4 + i + 1) * chans, parity * part : (parity + 1) * part]
                    for i in range(4)
                ]
                at = (plane * 4 + parity) * chans
                target[at : at + chans, :] = jnp.concatenate(pieces, axis=1).astype(BF16)


def transposed_taps(taps, chans, og):
    def tap(row, col):
        at = (row * 3 + col) * chans
        return taps[at : at + chans]

    return [
        tap(1, 1),
        tap(1, 2) + moved(tap(1, 0), 0, 1, og),
        tap(2, 1) + moved(tap(0, 1), 1, 0, og),
        tap(2, 2) + moved(tap(0, 2), 1, 0, og) + moved(tap(2, 0), 0, 1, og) + moved(tap(0, 0), 1, 1, og),
    ]


def plane_grad(w_ref, near, after, gates, chans, og, out_ref, at, live):
    block = 9 * chans
    if after is None:
        taps = jnp.dot(w_ref[block : 2 * block, :], near, preferred_element_type=F32)
    else:
        taps = jnp.dot(w_ref[2 * block : 3 * block, :], near, preferred_element_type=F32)
        taps = taps + jnp.dot(w_ref[0:block, :], after, preferred_element_type=F32)
    for parity, value in enumerate(transposed_taps(taps, chans, og)):
        gate = gates[parity * chans : (parity + 1) * chans].astype(F32)
        value = leaky(value, gate)
        if live is not None:
            value = jnp.where(live, value, 0.0)
        out_ref[at + parity * chans : at + (parity + 1) * chans, :] = value.astype(BF16)


def own_grad_kernel(og, chans, count, w_ref, g_ref, gn_ref, hp_ref, p_ref):
    s = lax.axis_index("space")
    half = 4 * chans
    here = g_ref[...]
    after = jnp.where(s < count - 1, gn_ref[...].astype(F32), 0.0).astype(BF16)
    plane_grad(w_ref, here, None, hp_ref[0:half, :], chans, og, p_ref, 0, None)
    plane_grad(w_ref, here, after, hp_ref[half : 2 * half, :], chans, og, p_ref, half, None)


def rim_grad_kernel(og, chans, count, w_ref, gp_ref, g_ref, gn_ref, hp_prev_ref, hp_next_ref, p_ref):
    s = lax.axis_index("space")
    half = 4 * chans
    plane_grad(w_ref, gp_ref[...], g_ref[...], hp_prev_ref[half : 2 * half, :], chans, og, p_ref, 0, s > 0)
    plane_grad(w_ref, gn_ref[...], None, hp_next_ref[0:half, :], chans, og, p_ref, half, s < count - 1)


def window_rows(blocks, parity, og):
    rows = []
    for row_tap in range(3):
        row_parity, row_move = neighbour(parity // 2, row_tap - 1)
        for col_tap in range(3):
            col_parity, col_move = neighbour(parity % 2, col_tap - 1)
            rows.append(blocks[(row_parity * 2 + col_parity, row_move, col_move)])
    return jnp.concatenate(rows, axis=0)


def moved_blocks(plane, chans, og):
    result = {}
    for parity in range(4):
        value = plane[parity * chans : (parity + 1) * chans]
        for row_move in (0, -1 if parity // 2 else 1):
            for col_move in (0, -1 if parity % 2 else 1):
                result[parity, row_move, col_move] = moved(value, row_move, col_move, og).astype(BF16)
    return result


def filter_one_kernel(og, chans, count, rows, a_ref, xprev_ref, xp_ref, xnext_ref, own_ref, *rest):
    outs, (p_scr, x_scr, f_scr) = rest[: count - 1], rest[count - 1 :]
    s = lax.axis_index("space")
    width = og * og
    shards = a_ref.shape[0]
    all_chans = shards * chans
    half = 4 * chans
    block = 9 * chans
    for plane in range(2):
        for parity in range(4):
            for j in range(shards):
                at = plane * all_chans + j * chans
                p_scr[at : at + chans, parity * width : (parity + 1) * width] = a_ref[
                    j, (plane * 4 + parity) * chans : (plane * 4 + parity + 1) * chans, :
                ]
    planes = (xprev_ref[...], xp_ref[0:half, :], xp_ref[half : 2 * half, :], xnext_ref[...])
    ends = ((0, all_chans), (0, 2 * all_chans), (0, 2 * all_chans), (all_chans, 2 * all_chans))
    products = []
    for index, plane in enumerate(planes):
        blocks = moved_blocks(plane, chans, og)
        for parity in range(4):
            x_scr[index, :, parity * width : (parity + 1) * width] = window_rows(blocks, parity, og)
        first, last = ends[index]
        products.append(
            lax.dot_general(x_scr[index], p_scr[first:last, :], CONTRACT_LAST, preferred_element_type=F32)
        )
    before, even, odd, after = products
    f_scr[0:block, :] = before + even[:, all_chans:]
    f_scr[block : 2 * block, :] = even[:, :all_chans] + odd[:, all_chans:]
    f_scr[2 * block : 3 * block, :] = odd[:, :all_chans] + after
    if count * rows > 3 * block:
        f_scr[3 * block :, :] = jnp.zeros((count * rows - 3 * block, all_chans), F32)

    def piece(step):
        at = pl.multiple_of(lax.rem(s + step, count) * rows, 16)
        return f_scr[pl.ds(at, rows), :]

    own_ref[...] = piece(0)
    for step, out in enumerate(outs):
        out[...] = piece(step + 1).astype(BF16)


def in_grad_kernel(og, chans, w_ref, a_ref, r_ref, e_ref, out_ref, p_scr):
    width = og * og
    shards = a_ref.shape[0]
    all_chans = shards * chans
    for index in range(4):
        source, first = (r_ref, index // 3) if index in (0, 3) else (a_ref, index - 1)
        for parity in range(4):
            for j in range(shards):
                at = index * all_chans + j * chans
                p_scr[at : at + chans, parity * width : (parity + 1) * width] = source[
                    j, (first * 4 + parity) * chans : (first * 4 + parity + 1) * chans, :
                ]
    joined = in_grad_planes(og, chans, all_chans, w_ref, e_ref[...], p_scr)
    for i in range(8):
        out_ref[:, i * width : (i + 1) * width] = joined[i * chans : (i + 1) * chans].astype(BF16)


def in_grad_planes(og, chans, all_chans, w_ref, matrix, p_scr):
    width = og * og
    part = width // 4
    block = 9 * chans
    empty = jnp.zeros((block, all_chans), BF16)
    weights = [w_ref[depth * block : (depth + 1) * block, :] for depth in (2, 1, 0)]
    weights = jnp.concatenate(
        [jnp.concatenate(weights + [empty], axis=1), jnp.concatenate([empty] + weights, axis=1)], axis=0
    )
    both = jnp.dot(weights, p_scr[...], preferred_element_type=F32)
    stacked = []
    for plane in range(2):
        taps = both[plane * block : (plane + 1) * block]
        sums = []
        for parity in range(4):
            terms = {}
            for row_tap in range(3):
                row_parity, row_move = neighbour(parity // 2, 1 - row_tap)
                for col_tap in range(3):
                    col_parity, col_move = neighbour(parity % 2, 1 - col_tap)
                    at = (row_tap * 3 + col_tap) * chans
                    lane = (row_parity * 2 + col_parity) * width
                    term = taps[at : at + chans, lane : lane + width]
                    key = (row_move, col_move)
                    terms[key] = term if key not in terms else terms[key] + term
            total = None
            for (row_move, col_move), term in terms.items():
                term = moved(term, row_move, col_move, og)
                total = term if total is None else total + term
            sums.append(total)
        for i in range(4):
            stacked.append(
                jnp.concatenate([value[:, i * part : (i + 1) * part] for value in sums], axis=1).astype(BF16)
            )
    return lax.dot_general(jnp.concatenate(stacked, axis=0), matrix, CONTRACT_LAST, preferred_element_type=F32)


def filter_two_kernel(og, chans, count, scale, *refs):
    grads, gates, out_ref = refs[:count], refs[count : 2 * count], refs[2 * count]
    g_scr, even_scr, odd_scr = refs[2 * count + 1 :]
    s = lax.axis_index("space")
    half = 4 * chans
    block = 9 * chans
    for step in range(count):
        at = lax.rem(s + count - step, count)
        g_scr[at] = grads[step][...]
        value = gates[step][...].astype(F32)
        act = leaky(value, value).astype(BF16)
        for plane, target in enumerate((even_scr, odd_scr)):
            blocks = moved_blocks(act[plane * half : (plane + 1) * half], chans, og)
            target[at] = window_rows(blocks, 0, og)
    filter_two_sums(count, block, scale, g_scr, even_scr, odd_scr, out_ref)


def filter_two_square_kernel(og, chans, count, scale, g_ref, act_ref, out_ref, even_scr, odd_scr):
    half = 4 * chans
    for at in range(count):
        for plane, target in enumerate((even_scr, odd_scr)):
            blocks = moved_blocks(act_ref[at, plane * half : (plane + 1) * half, :], chans, og)
            target[at] = window_rows(blocks, 0, og)
    filter_two_sums(count, 9 * chans, scale, g_ref, even_scr, odd_scr, out_ref)


def filter_two_sums(count, block, scale, g_scr, even_scr, odd_scr, out_ref):
    totals = [jnp.zeros((block, g_scr.shape[1]), F32) for _ in range(3)]
    for at in range(count):
        sources = (odd_scr.at[at - 1] if at else None, even_scr.at[at], odd_scr.at[at])
        for depth, source in enumerate(sources):
            if source is not None:
                totals[depth] = totals[depth] + lax.dot_general(
                    source[...], g_scr[at], CONTRACT_LAST, preferred_element_type=F32
                )
    for depth in range(3):
        out_ref[depth * block : (depth + 1) * block, :] = totals[depth] * scale


def place_kernel(count, rows, *refs):
    pieces, out_ref, scr = refs[:count], refs[count], refs[count + 1]
    s = lax.axis_index("space")
    for step, piece in enumerate(pieces):
        at = pl.multiple_of(lax.rem(s + count - step, count) * rows, 16)
        scr[pl.ds(at, rows), :] = piece[...].astype(F32)
    out_ref[...] = scr[0 : out_ref.shape[0], :]


def split_planes(value, order, matrix, chans, planes, og):
    width = og * og
    part = width // 4
    value = value.reshape(chans * planes, 4 * width)
    value = jnp.dot(order, value, preferred_element_type=F32).astype(BF16)
    stacked = jnp.concatenate([value[:, i * width : (i + 1) * width] for i in range(4)], axis=0)
    cells = jnp.dot(stacked, matrix, preferred_element_type=F32)
    rows = chans * planes
    result = []
    for plane in range(planes):
        for parity in range(4):
            pieces = [
                cells[i * rows + plane * chans : i * rows + (plane + 1) * chans, parity * part : (parity + 1) * part]
                for i in range(4)
            ]
            result.append(jnp.concatenate(pieces, axis=1))
    return jnp.concatenate(result, axis=0)


def pack_kernel(*refs):
    sources, out_ref = refs[:-1], refs[-1]
    rows = sources[0].shape[0]
    for step, source in enumerate(sources):
        out_ref[step * rows : (step + 1) * rows, :] = source[...]


def gate_kernel(og, chans, h_ref, out_ref):
    value = split_planes(h_ref[...], order_matrix(chans, 2), lane_matrix(og), chans, 2, og)
    out_ref[...] = value.astype(BF16)


def all_grad_kernel(og, chans, count, w_ref, *refs):
    grads, gates, refs = refs[:count], refs[count : 2 * count], refs[2 * count :]
    local_ref, q_ref, g_ref, act_ref, h_scr = refs
    s = lax.axis_index("space")
    half = 4 * chans
    i = lax.axis_index("chan")
    part = grads[0].shape[0] // count
    for step in range(count):
        at = lax.bitwise_xor(s, step)
        for mask in range(count):
            row = pl.multiple_of(lax.bitwise_xor(i, mask) * part, part)
            g_ref[at, pl.ds(row, part), :] = grads[mask][step * part : (step + 1) * part, :]
        value = gates[step][...]
        h_scr[at] = value
        value = value.astype(F32)
        act_ref[at] = leaky(value, value).astype(BF16)
    empty = jnp.zeros((chans, q_ref.shape[1]), BF16)
    for index in (0, 2 * count + 1, 2 * count + 2):
        q_ref[index * chans : (index + 1) * chans, :] = empty
    block = 9 * chans
    for q in range(count):
        here = g_ref[q]
        even = jnp.dot(w_ref[block : 2 * block, :], here, preferred_element_type=F32)
        odd = jnp.dot(w_ref[2 * block : 3 * block, :], here, preferred_element_type=F32)
        if q < count - 1:
            odd = odd + jnp.dot(w_ref[0:block, :], g_ref[q + 1], preferred_element_type=F32)
        for plane, value in enumerate((even, odd)):
            row = (2 * q + plane + 1) * chans
            blocks = []
            for parity, term in enumerate(transposed_taps(value, chans, og)):
                at = (plane * 4 + parity) * chans
                blocks.append(leaky(term, h_scr[q, at : at + chans, :].astype(F32)).astype(BF16))
            q_ref[row : row + chans, :] = jnp.concatenate(blocks, axis=1)
    local_ref[...] = q_ref[pl.ds(pl.multiple_of(2 * s * chans, chans), half), :]


def mixed(index, count):
    return index % 2 * (count // 2) + index // 2


def block_rows(chans):
    return -(-27 * chans // 64) * 16


def filter_block_kernel(og, chans, count, scale, q_ref, *refs):
    sources, (out_ref, x_scr) = refs[:count], refs[count:]
    matrix, order = lane_matrix(og), order_matrix(chans, 2)
    i = lax.axis_index("chan")
    width = og * og
    half = 4 * chans
    block = 9 * chans
    lanes = 4 * chans
    across = 2 * count * chans
    for index, source in enumerate(sources):
        value = split_planes(source[...], order, matrix, chans, 2, og)
        for plane in range(2):
            blocks = moved_blocks(value[plane * half : (plane + 1) * half], chans, og)
            at = (2 * index + plane) * block
            for parity in range(4):
                x_scr[at : at + block, parity * width : (parity + 1) * width] = window_rows(blocks, parity, og)
    products = lax.dot_general(
        x_scr[...], q_ref[chans : chans + across, :], CONTRACT_LAST, preferred_element_type=F32
    )
    group = lax.broadcasted_iota(jnp.int32, (block, lanes), 1) // chans
    total = jnp.zeros((block, lanes), F32)
    for mask in range(count):
        for plane in range(2):
            place = 2 * mixed(lax.bitwise_xor(i, mask), count) + plane
            at = (2 * mask + plane) * block
            term = pltpu.roll(products[at : at + block], lax.rem(across + chans - place * chans, across), 1)[:, :lanes]
            inside = (group + place > 0) & (group + place <= 2 * count)
            total = total + jnp.where(inside, term, 0.0)
    total = total * scale
    rows = block_rows(chans)
    tail = total[rows:]
    moved_tail = [pltpu.roll(tail, lanes - (i + 1) * chans, 1) for i in range(3)]
    spare = rows - 3 * (block - rows)
    if spare:
        moved_tail.append(jnp.zeros((spare, lanes), F32))
    lane = lax.broadcasted_iota(jnp.int32, (rows, lanes), 1)
    out_ref[...] = jnp.where(lane < 3 * chans, total[:rows], jnp.concatenate(moved_tail, axis=0)).astype(BF16)


def join_matrix(chans, count):
    lanes = 4 * chans
    result = np.zeros((count * lanes, 4 * lanes), np.float32)
    for j in range(count):
        for group in range(4):
            target = 2 - group if group < 3 else 3
            for c in range(chans):
                result[j * lanes + group * chans + c, target * lanes + j * chans + c] = 1
    return result


def pair_kernel(own_ref, mate_ref, out_ref):
    odd = lax.axis_index("chan") % 2
    rows = own_ref.shape[0]
    out_ref[pl.ds(pl.multiple_of(odd * rows, 16), rows), :] = own_ref[...]
    out_ref[pl.ds(pl.multiple_of((1 - odd) * rows, 16), rows), :] = mate_ref[...]


def join_kernel(chans, count, m_ref, *refs):
    pieces, out_ref, scr = refs[:-2], refs[-2], refs[-1]
    s = lax.axis_index("space")
    lanes = 4 * chans
    block = 9 * chans
    rows = block_rows(chans)
    rest = block - rows
    for step, piece in enumerate(pieces):
        scr[step] = piece[...]
    side = [
        scr[lax.bitwise_xor(s // 2, j // 2), j % 2 * rows : (j % 2 + 1) * rows, :] for j in range(count)
    ]
    joined = jnp.dot(jnp.concatenate(side, axis=1), m_ref[...], preferred_element_type=F32)
    for depth in range(3):
        out_ref[depth * block : depth * block + rows, :] = joined[:, depth * lanes : (depth + 1) * lanes]
        at = (2 - depth) * rest
        out_ref[depth * block + rows : (depth + 1) * block, :] = joined[at : at + rest, 3 * lanes :]


def in_grad_square_kernel(og, chans, count, w_ref, *refs):
    sources, out_ref, p_scr = refs[:count], refs[count], refs[count + 1]
    i = lax.axis_index("chan")
    width = og * og
    all_chans = count * chans
    for mask, source in enumerate(sources):
        j = lax.bitwise_xor(i, mask)
        for index in range(4):
            at = pl.multiple_of(index * all_chans + j * chans, chans)
            p_scr[pl.ds(at, chans), :] = source[index * chans : (index + 1) * chans, :]
    joined = in_grad_planes(og, chans, all_chans, w_ref, lane_matrix(og), p_scr)
    rows = [
        jnp.concatenate([joined[(plane * 4 + k) * chans : (plane * 4 + k + 1) * chans] for k in range(4)], axis=1)
        for plane in range(2)
    ]
    value = jnp.concatenate(rows, axis=0).astype(BF16)
    value = lax.dot_general(order_matrix(chans, 2), value, (((0,), (0,)), ((), ())), preferred_element_type=F32)
    out_ref[...] = value.astype(BF16).reshape(out_ref.shape)


def local_call(kernel, out_shape, scratch, flops, *operands):
    total = sum(value.size * value.dtype.itemsize for value in operands)
    total += sum(math.prod(o.shape) * o.dtype.itemsize for o in jax.tree.leaves(out_shape))
    return pl.pallas_call(
        kernel,
        out_shape=out_shape,
        in_specs=[pl.BlockSpec(memory_space=pltpu.VMEM)] * len(operands),
        out_specs=jax.tree.map(lambda _: pl.BlockSpec(memory_space=pltpu.VMEM), out_shape),
        scratch_shapes=scratch,
        cost_estimate=pl.CostEstimate(flops=flops, bytes_accessed=total, transcendentals=0),
        compiler_params=pltpu.CompilerParams(vmem_limit_bytes=50 * 1024 * 1024),
    )(*operands)


def ring(value, step):
    count = lax.axis_size("space")
    return lax.ppermute(value, "space", [(i, (i + step) % count) for i in range(count)])


def ring_shards(inputs, pre_act, out_grad, weight_one, weight_two):
    samples, chans, planes, cells = inputs.shape
    count = lax.axis_size("space")
    og = math.isqrt(out_grad.shape[3])
    width = og * og
    half = 4 * chans
    block = 9 * chans
    all_chans = weight_one.shape[4]
    all_out = weight_two.shape[4]
    w1 = weight_one.reshape(3 * block, all_chans)
    w2 = weight_two.reshape(3 * block, all_out)
    matrix = jnp.asarray(split_matrix(og), BF16)
    shape = jax.ShapeDtypeStruct

    grads = lax.all_gather(out_grad.reshape(-1, width), "chan", axis=0, tiled=True)
    xp, hp = local_call(
        lambda *r: split_kernel(og, planes, chans, *r),
        [shape((planes * half, width), BF16)] * 2,
        [],
        2 * 2 * planes * half * width * width,
        inputs.reshape(chans, planes * cells),
        pre_act.reshape(chans, planes * cells),
        matrix,
    )
    grads_next = ring(grads, count - 1)
    up = [(i, i + 1) for i in range(count - 1)]
    down = [(i + 1, i) for i in range(count - 1)]
    x_prev = lax.ppermute(xp[half:], "space", up)
    x_next = lax.ppermute(xp[:half], "space", down)

    p_own = local_call(
        lambda *r: own_grad_kernel(og, chans, count, *r),
        shape((2 * half, width), BF16),
        [],
        2 * 3 * block * all_out * width,
        w2,
        grads,
        grads_next,
        hp,
    )
    a_own = lax.all_gather(p_own, "chan", axis=0)

    all_grads = [grads] + [ring(grads, step) for step in range(1, count - 1)] + [grads_next]
    all_hp = [hp] + [ring(hp, step) for step in range(1, count)]

    rows = -(-3 * block // (16 * count)) * 16
    pieces = local_call(
        lambda *r: filter_one_kernel(og, chans, count, rows, *r),
        [shape((rows, all_chans), F32)] + [shape((rows, all_chans), BF16)] * (count - 1),
        [
            pltpu.VMEM((2 * all_chans, 4 * width), BF16),
            pltpu.VMEM((4, block, 4 * width), BF16),
            pltpu.VMEM((count * rows, all_chans), F32),
        ],
        2 * 6 * block * all_chans * cells,
        a_own,
        x_prev,
        xp,
        x_next,
    )
    total = pieces[0]
    for step in range(1, count):
        total = total + ring(pieces[step], step).astype(F32)
    scale_one = 1.0 / math.sqrt(samples * planes * count * cells)
    scale_two = 1.0 / math.sqrt(samples * out_grad.shape[2] * count * width)
    total = (total * scale_one).astype(BF16)

    p_rim = local_call(
        lambda *r: rim_grad_kernel(og, chans, count, *r),
        shape((2 * half, width), BF16),
        [],
        2 * 3 * block * all_out * width,
        w2,
        all_grads[1],
        grads,
        grads_next,
        all_hp[1],
        all_hp[count - 1],
    )
    a_rim = lax.all_gather(p_rim, "chan", axis=0)
    in_grad = local_call(
        lambda *r: in_grad_kernel(og, chans, *r),
        shape((chans, planes * cells), BF16),
        [pltpu.VMEM((4 * all_chans, 4 * width), BF16)],
        2 * 6 * block * all_chans * cells,
        w1,
        a_own,
        a_rim,
        matrix,
    )
    filter_two = local_call(
        lambda *r: filter_two_kernel(og, chans, count, scale_two, *r),
        shape((3 * block, all_out), F32),
        [
            pltpu.VMEM((count, all_out, width), BF16),
            pltpu.VMEM((count, block, width), BF16),
            pltpu.VMEM((count, block, width), BF16),
        ],
        2 * 3 * count * block * all_out * width,
        *all_grads,
        *all_hp,
    )
    filter_one = local_call(
        lambda *r: place_kernel(count, rows, *r),
        shape((3 * block, all_chans), F32),
        [pltpu.VMEM((count * rows, all_chans), F32)],
        0,
        total,
        *[ring(total, step) for step in range(1, count)],
    )
    return (
        in_grad.reshape(samples, chans, planes, cells),
        filter_one.reshape(3, 3, 3, chans, all_chans),
        filter_two.reshape(3, 3, 3, chans, all_out),
    )


def spread(value, before_last=(), axis="chan"):
    count = lax.axis_size(axis)
    found = {0: value}
    bit = count // 2
    while bit:
        pairs = [(i, i ^ bit) for i in range(count)]
        if bit == 1 and before_last:
            for mask in found:
                if mask:
                    found[mask] = lax.optimization_barrier((found[mask], *before_last))[0]
        found.update({mask ^ bit: lax.ppermute(item, axis, pairs) for mask, item in found.items()})
        bit //= 2
    return [found[mask] for mask in range(count)]


def paired(value, mask):
    return lax.ppermute(value, "space", [(i, i ^ mask) for i in range(lax.axis_size("space"))])


def square_shards(inputs, pre_act, out_grad, weight_one, weight_two):
    samples, chans, planes, cells = inputs.shape
    count = lax.axis_size("space")
    og = math.isqrt(out_grad.shape[3])
    width = og * og
    half = 4 * chans
    block = 9 * chans
    all_chans = weight_one.shape[4]
    all_out = weight_two.shape[4]
    w1 = weight_one.reshape(3 * block, all_chans)
    w2 = weight_two.reshape(3 * block, all_out)
    shape = jax.ShapeDtypeStruct
    both = ("space", "chan")
    scale_one = 1.0 / math.sqrt(samples * planes * count * cells)
    scale_two = 1.0 / math.sqrt(samples * out_grad.shape[2] * count * width)

    near = out_grad.reshape(-1, width)
    around = [near] + [paired(near, step) for step in range(1, count)]
    turn = [(mixed(j, count) * count + mixed(a, count), a * count + j) for a in range(count) for j in range(count)]
    x_turned = lax.ppermute(inputs.reshape(chans, planes, cells), both, turn)
    packed = local_call(pack_kernel, shape((count * near.shape[0], width), BF16), [], 0, *around)
    gate = local_call(
        lambda *r: gate_kernel(og, chans, *r),
        shape((planes * half, width), BF16),
        [],
        2 * planes * half * width * width,
        pre_act.reshape(chans, planes, cells),
    )
    gates = spread(gate, (), "space")
    grads = spread(packed)
    rows = block_rows(chans)
    p_local, p_all, grads, act = local_call(
        lambda *r: all_grad_kernel(og, chans, count, *r),
        [
            shape((half, 4 * width), BF16),
            shape(((planes * count + 3) * chans, 4 * width), BF16),
            shape((count, all_out, width), BF16),
            shape((count, planes * half, width), BF16),
        ],
        [pltpu.VMEM((count, planes * half, width), BF16)],
        2 * 3 * count * block * all_out * width,
        w2,
        *grads,
        *gates,
    )
    x_all = spread(x_turned)
    piece = local_call(
        lambda *r: filter_block_kernel(og, chans, count, scale_one, *r),
        shape((rows, all_chans), BF16),
        [pltpu.VMEM((planes * count * block, 4 * width), BF16)],
        2 * 3 * count * block * all_chans * cells,
        p_all,
        *x_all,
    )
    mate = lax.ppermute(piece, "chan", [(j, j ^ 1) for j in range(count)])
    pair = local_call(
        lambda *r: pair_kernel(*r),
        shape((2 * rows, all_chans), BF16),
        [],
        0,
        piece,
        mate,
    )
    pieces = []
    for step in range(count // 2):
        pairs = [
            (a * count + j, (j % 2 + (step ^ j // 2) * 2) * count + mixed(a, count))
            for a in range(count)
            for j in range(count)
        ]
        pieces.append(lax.ppermute(pair, both, pairs))
    filter_two = local_call(
        lambda *r: filter_two_square_kernel(og, chans, count, scale_two, *r),
        shape((3 * block, all_out), F32),
        [
            pltpu.VMEM((count, block, width), BF16),
            pltpu.VMEM((count, block, width), BF16),
        ],
        2 * 3 * count * block * all_out * width,
        grads,
        act,
    )
    near_p = [p_local] + [
        lax.ppermute(p_local, "chan", [(i, i ^ mask) for i in range(count)]) for mask in range(1, count)
    ]
    in_grad = local_call(
        lambda *r: in_grad_square_kernel(og, chans, count, *r),
        shape((chans, planes, cells), BF16),
        [pltpu.VMEM((4 * all_chans, 4 * width), BF16)],
        2 * 6 * block * all_chans * cells,
        w1,
        *near_p,
    )
    filter_one = local_call(
        lambda *r: join_kernel(chans, count, *r),
        shape((3 * block, all_chans), F32),
        [pltpu.VMEM((count // 2, 2 * rows, all_chans), BF16)],
        2 * rows * 16 * all_chans * all_chans,
        jnp.asarray(join_matrix(chans, count), BF16),
        *pieces,
    )
    return (
        in_grad.reshape(samples, chans, planes, cells),
        filter_one.reshape(3, 3, 3, chans, all_chans),
        filter_two.reshape(3, 3, 3, chans, all_out),
    )


def shards(*arguments):
    count = lax.axis_size("space")
    square = count == lax.axis_size("chan") and count & (count - 1) == 0 and 4 * arguments[0].shape[1] == arguments[3].shape[4]
    return (square_shards if square else ring_shards)(*arguments)


def solution(mesh):
    in_specs = (
        P("groups", "chan", "space", None),
        P("groups", "chan", "space", None),
        P("groups", "chan", "space", None),
        P(None, None, None, "chan", None),
        P(None, None, None, "chan", None),
    )
    out_specs = (
        P("groups", "chan", "space", None),
        P("groups", None, None, "chan", None),
        P("groups", None, None, "chan", None),
    )
    return jax.shard_map(shards, mesh=mesh, in_specs=in_specs, out_specs=out_specs, check_vma=False)
```

```python
import math

import jax
import jax.numpy as jnp
import numpy as np
from jax import lax
from jax.experimental import pallas as pl
from jax.experimental.pallas import tpu as pltpu
from jax.sharding import PartitionSpec as P

leak_slope = 0.3
F32 = jnp.float32
BF16 = jnp.bfloat16
CONTRACT_LAST = (((1,), (1,)), ((), ()))


def moved(value, rows, cols, og):
    if rows == 0 and cols == 0:
        return value
    width = og * og
    value = value.astype(F32)
    lane = lax.broadcasted_iota(jnp.int32, value.shape, 1)
    rolled = pltpu.roll(value, (-(rows * og + cols)) % width, 1)
    keep = None
    for step, place in ((rows, lane // og), (cols, lane % og)):
        if step:
            good = place < og - 1 if step > 0 else place > 0
            keep = good if keep is None else keep & good
    return jnp.where(keep, rolled, 0.0)


def neighbour(parity, step):
    place = parity + step
    return place % 2, place // 2


def leaky(value, gate):
    return jnp.where(gate > 0, value, leak_slope * value)


def lane_matrix(og):
    width = og * og
    cell = lax.broadcasted_iota(jnp.int32, (width, width), 0)
    place = lax.broadcasted_iota(jnp.int32, (width, width), 1)
    row, col = cell // (2 * og), cell % (2 * og)
    target = (row % 2 * 2 + col % 2) * (width // 4) + row // 2 * og + col // 2
    return jnp.where(place == target, 1.0, 0.0).astype(BF16)


def order_matrix(chans, planes):
    rows = chans * planes
    place = lax.broadcasted_iota(jnp.int32, (rows, rows), 0)
    row = lax.broadcasted_iota(jnp.int32, (rows, rows), 1)
    return jnp.where(place == row % planes * chans + row // planes, 1.0, 0.0).astype(BF16)


def split_matrix(og):
    width = og * og
    grid = 2 * og
    cell = np.arange(width)
    row, col = cell // grid, cell % grid
    place = ((row % 2) * 2 + col % 2) * (width // 4) + (row // 2) * og + col // 2
    return (place[:, None] == np.arange(width)[None, :]).astype(np.float32)


def split_kernel(og, planes, chans, x_ref, h_ref, e_ref, xp_ref, hp_ref):
    width = og * og
    part = width // 4
    matrix = e_ref[...]
    for source, target in ((x_ref, xp_ref), (h_ref, hp_ref)):
        value = source[...]
        stacked = jnp.concatenate([value[:, i * width : (i + 1) * width] for i in range(4 * planes)], axis=0)
        sorted_cells = jnp.dot(stacked, matrix, preferred_element_type=F32)
        for plane in range(planes):
            for parity in range(4):
                pieces = [
                    sorted_cells[(plane * 4 + i) * chans : (plane * 4 + i + 1) * chans, parity * part : (parity + 1) * part]
                    for i in range(4)
                ]
                at = (plane * 4 + parity) * chans
                target[at : at + chans, :] = jnp.concatenate(pieces, axis=1).astype(BF16)


def transposed_taps(taps, chans, og):
    def tap(row, col):
        at = (row * 3 + col) * chans
        return taps[at : at + chans]

    return [
        tap(1, 1),
        tap(1, 2) + moved(tap(1, 0), 0, 1, og),
        tap(2, 1) + moved(tap(0, 1), 1, 0, og),
        tap(2, 2) + moved(tap(0, 2), 1, 0, og) + moved(tap(2, 0), 0, 1, og) + moved(tap(0, 0), 1, 1, og),
    ]


def plane_grad(w_ref, near, after, gates, chans, og, out_ref, at, live):
    block = 9 * chans
    if after is None:
        taps = jnp.dot(w_ref[block : 2 * block, :], near, preferred_element_type=F32)
    else:
        taps = jnp.dot(w_ref[2 * block : 3 * block, :], near, preferred_element_type=F32)
        taps = taps + jnp.dot(w_ref[0:block, :], after, preferred_element_type=F32)
    for parity, value in enumerate(transposed_taps(taps, chans, og)):
        gate = gates[parity * chans : (parity + 1) * chans].astype(F32)
        value = leaky(value, gate)
        if live is not None:
            value = jnp.where(live, value, 0.0)
        out_ref[at + parity * chans : at + (parity + 1) * chans, :] = value.astype(BF16)


def own_grad_kernel(og, chans, count, w_ref, g_ref, gn_ref, hp_ref, p_ref):
    s = lax.axis_index("space")
    half = 4 * chans
    here = g_ref[...]
    after = jnp.where(s < count - 1, gn_ref[...].astype(F32), 0.0).astype(BF16)
    plane_grad(w_ref, here, None, hp_ref[0:half, :], chans, og, p_ref, 0, None)
    plane_grad(w_ref, here, after, hp_ref[half : 2 * half, :], chans, og, p_ref, half, None)


def rim_grad_kernel(og, chans, count, w_ref, gp_ref, g_ref, gn_ref, hp_prev_ref, hp_next_ref, p_ref):
    s = lax.axis_index("space")
    half = 4 * chans
    plane_grad(w_ref, gp_ref[...], g_ref[...], hp_prev_ref[half : 2 * half, :], chans, og, p_ref, 0, s > 0)
    plane_grad(w_ref, gn_ref[...], None, hp_next_ref[0:half, :], chans, og, p_ref, half, s < count - 1)


def window_rows(blocks, parity, og):
    rows = []
    for row_tap in range(3):
        row_parity, row_move = neighbour(parity // 2, row_tap - 1)
        for col_tap in range(3):
            col_parity, col_move = neighbour(parity % 2, col_tap - 1)
            rows.append(blocks[(row_parity * 2 + col_parity, row_move, col_move)])
    return jnp.concatenate(rows, axis=0)


def moved_blocks(plane, chans, og):
    result = {}
    for parity in range(4):
        value = plane[parity * chans : (parity + 1) * chans]
        for row_move in (0, -1 if parity // 2 else 1):
            for col_move in (0, -1 if parity % 2 else 1):
                result[parity, row_move, col_move] = moved(value, row_move, col_move, og).astype(BF16)
    return result


def filter_one_kernel(og, chans, count, rows, a_ref, xprev_ref, xp_ref, xnext_ref, own_ref, *rest):
    outs, (p_scr, x_scr, f_scr) = rest[: count - 1], rest[count - 1 :]
    s = lax.axis_index("space")
    width = og * og
    shards = a_ref.shape[0]
    all_chans = shards * chans
    half = 4 * chans
    block = 9 * chans
    for plane in range(2):
        for parity in range(4):
            for j in range(shards):
                at = plane * all_chans + j * chans
                p_scr[at : at + chans, parity * width : (parity + 1) * width] = a_ref[
                    j, (plane * 4 + parity) * chans : (plane * 4 + parity + 1) * chans, :
                ]
    planes = (xprev_ref[...], xp_ref[0:half, :], xp_ref[half : 2 * half, :], xnext_ref[...])
    ends = ((0, all_chans), (0, 2 * all_chans), (0, 2 * all_chans), (all_chans, 2 * all_chans))
    products = []
    for index, plane in enumerate(planes):
        blocks = moved_blocks(plane, chans, og)
        for parity in range(4):
            x_scr[index, :, parity * width : (parity + 1) * width] = window_rows(blocks, parity, og)
        first, last = ends[index]
        products.append(
            lax.dot_general(x_scr[index], p_scr[first:last, :], CONTRACT_LAST, preferred_element_type=F32)
        )
    before, even, odd, after = products
    f_scr[0:block, :] = before + even[:, all_chans:]
    f_scr[block : 2 * block, :] = even[:, :all_chans] + odd[:, all_chans:]
    f_scr[2 * block : 3 * block, :] = odd[:, :all_chans] + after
    if count * rows > 3 * block:
        f_scr[3 * block :, :] = jnp.zeros((count * rows - 3 * block, all_chans), F32)

    def piece(step):
        at = pl.multiple_of(lax.rem(s + step, count) * rows, 16)
        return f_scr[pl.ds(at, rows), :]

    own_ref[...] = piece(0)
    for step, out in enumerate(outs):
        out[...] = piece(step + 1).astype(BF16)


def in_grad_kernel(og, chans, w_ref, a_ref, r_ref, e_ref, out_ref, p_scr):
    width = og * og
    shards = a_ref.shape[0]
    all_chans = shards * chans
    for index in range(4):
        source, first = (r_ref, index // 3) if index in (0, 3) else (a_ref, index - 1)
        for parity in range(4):
            for j in range(shards):
                at = index * all_chans + j * chans
                p_scr[at : at + chans, parity * width : (parity + 1) * width] = source[
                    j, (first * 4 + parity) * chans : (first * 4 + parity + 1) * chans, :
                ]
    joined = in_grad_planes(og, chans, all_chans, w_ref, e_ref[...], p_scr)
    for i in range(8):
        out_ref[:, i * width : (i + 1) * width] = joined[i * chans : (i + 1) * chans].astype(BF16)


def in_grad_planes(og, chans, all_chans, w_ref, matrix, p_scr):
    width = og * og
    part = width // 4
    block = 9 * chans
    empty = jnp.zeros((block, all_chans), BF16)
    weights = [w_ref[depth * block : (depth + 1) * block, :] for depth in (2, 1, 0)]
    weights = jnp.concatenate(
        [jnp.concatenate(weights + [empty], axis=1), jnp.concatenate([empty] + weights, axis=1)], axis=0
    )
    both = jnp.dot(weights, p_scr[...], preferred_element_type=F32)
    stacked = []
    for plane in range(2):
        taps = both[plane * block : (plane + 1) * block]
        sums = []
        for parity in range(4):
            terms = {}
            for row_tap in range(3):
                row_parity, row_move = neighbour(parity // 2, 1 - row_tap)
                for col_tap in range(3):
                    col_parity, col_move = neighbour(parity % 2, 1 - col_tap)
                    at = (row_tap * 3 + col_tap) * chans
                    lane = (row_parity * 2 + col_parity) * width
                    term = taps[at : at + chans, lane : lane + width]
                    key = (row_move, col_move)
                    terms[key] = term if key not in terms else terms[key] + term
            total = None
            for (row_move, col_move), term in terms.items():
                term = moved(term, row_move, col_move, og)
                total = term if total is None else total + term
            sums.append(total)
        for i in range(4):
            stacked.append(
                jnp.concatenate([value[:, i * part : (i + 1) * part] for value in sums], axis=1).astype(BF16)
            )
    return lax.dot_general(jnp.concatenate(stacked, axis=0), matrix, CONTRACT_LAST, preferred_element_type=F32)


def filter_two_kernel(og, chans, count, scale, *refs):
    grads, gates, out_ref = refs[:count], refs[count : 2 * count], refs[2 * count]
    g_scr, even_scr, odd_scr = refs[2 * count + 1 :]
    s = lax.axis_index("space")
    half = 4 * chans
    block = 9 * chans
    for step in range(count):
        at = lax.rem(s + count - step, count)
        g_scr[at] = grads[step][...]
        value = gates[step][...].astype(F32)
        act = leaky(value, value).astype(BF16)
        for plane, target in enumerate((even_scr, odd_scr)):
            blocks = moved_blocks(act[plane * half : (plane + 1) * half], chans, og)
            target[at] = window_rows(blocks, 0, og)
    filter_two_sums(count, block, scale, g_scr, even_scr, odd_scr, out_ref)


def filter_two_square_kernel(og, chans, count, scale, g_ref, act_ref, out_ref, even_scr, odd_scr, stage, sems):
    half = 4 * chans
    block = 9 * chans
    for at in range(count):
        for plane, target in enumerate((even_scr, odd_scr)):
            blocks = moved_blocks(act_ref[at, plane * half : (plane + 1) * half, :], chans, og)
            target[at] = window_rows(blocks, 0, og)
    copies = []
    for depth in range(3):
        total = None
        for at in range(count):
            if depth == 0 and at == 0:
                continue
            source = even_scr[at] if depth == 1 else odd_scr[at - 1 if depth == 0 else at]
            term = lax.dot_general(source, g_ref[at], CONTRACT_LAST, preferred_element_type=F32)
            total = term if total is None else total + term
        stage[depth] = total * scale
        copies.append(pltpu.make_async_copy(stage.at[depth], out_ref.at[depth], sems.at[depth]))
        copies[-1].start()
    for copy in copies:
        copy.wait()


def filter_two_sums(count, block, scale, g_scr, even_scr, odd_scr, out_ref):
    totals = [jnp.zeros((block, g_scr.shape[1]), F32) for _ in range(3)]
    for at in range(count):
        sources = (odd_scr.at[at - 1] if at else None, even_scr.at[at], odd_scr.at[at])
        for depth, source in enumerate(sources):
            if source is not None:
                totals[depth] = totals[depth] + lax.dot_general(
                    source[...], g_scr[at], CONTRACT_LAST, preferred_element_type=F32
                )
    for depth in range(3):
        out_ref[depth * block : (depth + 1) * block, :] = totals[depth] * scale


def place_kernel(count, rows, *refs):
    pieces, out_ref, scr = refs[:count], refs[count], refs[count + 1]
    s = lax.axis_index("space")
    for step, piece in enumerate(pieces):
        at = pl.multiple_of(lax.rem(s + count - step, count) * rows, 16)
        scr[pl.ds(at, rows), :] = piece[...].astype(F32)
    out_ref[...] = scr[0 : out_ref.shape[0], :]


def split_planes(value, order, matrix, chans, planes, og):
    width = og * og
    part = width // 4
    value = value.reshape(chans * planes, 4 * width)
    value = jnp.dot(order, value, preferred_element_type=F32).astype(BF16)
    stacked = jnp.concatenate([value[:, i * width : (i + 1) * width] for i in range(4)], axis=0)
    cells = jnp.dot(stacked, matrix, preferred_element_type=F32)
    rows = chans * planes
    result = []
    for plane in range(planes):
        for parity in range(4):
            pieces = [
                cells[i * rows + plane * chans : i * rows + (plane + 1) * chans, parity * part : (parity + 1) * part]
                for i in range(4)
            ]
            result.append(jnp.concatenate(pieces, axis=1))
    return jnp.concatenate(result, axis=0)


def pack_kernel(*refs):
    sources, out_ref = refs[:-1], refs[-1]
    rows = sources[0].shape[0]
    for step, source in enumerate(sources):
        out_ref[step * rows : (step + 1) * rows, :] = source[...]


def gate_kernel(og, chans, h_ref, out_ref):
    value = split_planes(h_ref[...], order_matrix(chans, 2), lane_matrix(og), chans, 2, og)
    out_ref[...] = value.astype(BF16)


def all_grad_kernel(og, chans, count, w_ref, *refs):
    grads, gates, refs = refs[:count], refs[count : 2 * count], refs[2 * count :]
    local_ref, q_ref, g_ref, act_ref, h_scr = refs
    s = lax.axis_index("space")
    half = 4 * chans
    i = lax.axis_index("chan")
    part = grads[0].shape[0] // count
    for step in range(count):
        at = lax.bitwise_xor(s, step)
        for mask in range(count):
            row = pl.multiple_of(lax.bitwise_xor(i, mask) * part, part)
            g_ref[at, pl.ds(row, part), :] = grads[mask][step * part : (step + 1) * part, :]
        value = gates[step][...]
        h_scr[at] = value
        value = value.astype(F32)
        act_ref[at] = leaky(value, value).astype(BF16)
    empty = jnp.zeros((chans, q_ref.shape[1]), BF16)
    for index in (0, 2 * count + 1, 2 * count + 2):
        q_ref[index * chans : (index + 1) * chans, :] = empty
    block = 9 * chans
    for q in range(count):
        here = g_ref[q]
        even = jnp.dot(w_ref[block : 2 * block, :], here, preferred_element_type=F32)
        odd = jnp.dot(w_ref[2 * block : 3 * block, :], here, preferred_element_type=F32)
        if q < count - 1:
            odd = odd + jnp.dot(w_ref[0:block, :], g_ref[q + 1], preferred_element_type=F32)
        for plane, value in enumerate((even, odd)):
            row = (2 * q + plane + 1) * chans
            blocks = []
            for parity, term in enumerate(transposed_taps(value, chans, og)):
                at = (plane * 4 + parity) * chans
                blocks.append(leaky(term, h_scr[q, at : at + chans, :].astype(F32)).astype(BF16))
            q_ref[row : row + chans, :] = jnp.concatenate(blocks, axis=1)
    local_ref[...] = q_ref[pl.ds(pl.multiple_of(2 * s * chans, chans), half), :]


def mixed(index, count):
    return index % 2 * (count // 2) + index // 2


def block_rows(chans):
    return -(-27 * chans // 64) * 16


def filter_block_kernel(og, chans, count, scale, q_ref, *refs):
    sources, (out_ref, x_scr) = refs[:count], refs[count:]
    matrix, order = lane_matrix(og), order_matrix(chans, 2)
    i = lax.axis_index("chan")
    width = og * og
    half = 4 * chans
    block = 9 * chans
    lanes = 4 * chans
    across = 2 * count * chans
    for index, source in enumerate(sources):
        value = split_planes(source[...], order, matrix, chans, 2, og)
        for plane in range(2):
            blocks = moved_blocks(value[plane * half : (plane + 1) * half], chans, og)
            at = (2 * index + plane) * block
            for parity in range(4):
                x_scr[at : at + block, parity * width : (parity + 1) * width] = window_rows(blocks, parity, og)
    products = lax.dot_general(
        x_scr[...], q_ref[chans : chans + across, :], CONTRACT_LAST, preferred_element_type=F32
    )
    group = lax.broadcasted_iota(jnp.int32, (block, lanes), 1) // chans
    total = jnp.zeros((block, lanes), F32)
    for mask in range(count):
        for plane in range(2):
            place = 2 * mixed(lax.bitwise_xor(i, mask), count) + plane
            at = (2 * mask + plane) * block
            term = pltpu.roll(products[at : at + block], lax.rem(across + chans - place * chans, across), 1)[:, :lanes]
            inside = (group + place > 0) & (group + place <= 2 * count)
            total = total + jnp.where(inside, term, 0.0)
    total = total * scale
    rows = block_rows(chans)
    tail = total[rows:]
    moved_tail = [pltpu.roll(tail, lanes - (i + 1) * chans, 1) for i in range(3)]
    spare = rows - 3 * (block - rows)
    if spare:
        moved_tail.append(jnp.zeros((spare, lanes), F32))
    lane = lax.broadcasted_iota(jnp.int32, (rows, lanes), 1)
    out_ref[...] = jnp.where(lane < 3 * chans, total[:rows], jnp.concatenate(moved_tail, axis=0)).astype(BF16)


def join_matrix(chans, count):
    lanes = 4 * chans
    result = np.zeros((count * lanes, 4 * lanes), np.float32)
    for j in range(count):
        for group in range(4):
            target = 2 - group if group < 3 else 3
            for c in range(chans):
                result[j * lanes + group * chans + c, target * lanes + j * chans + c] = 1
    return result


def pair_kernel(own_ref, mate_ref, out_ref):
    odd = lax.axis_index("chan") % 2
    rows = own_ref.shape[0]
    out_ref[pl.ds(pl.multiple_of(odd * rows, 16), rows), :] = own_ref[...]
    out_ref[pl.ds(pl.multiple_of((1 - odd) * rows, 16), rows), :] = mate_ref[...]


def join_kernel(chans, count, m_ref, *refs):
    pieces, (out_ref, scr, stage, sems) = refs[:-4], refs[-4:]
    s = lax.axis_index("space")
    lanes = 4 * chans
    block = 9 * chans
    rows = block_rows(chans)
    rest = block - rows
    for step, piece in enumerate(pieces):
        scr[step] = piece[...]
    side = [
        scr[lax.bitwise_xor(s // 2, j // 2), j % 2 * rows : (j % 2 + 1) * rows, :] for j in range(count)
    ]
    side = jnp.concatenate(side, axis=1)
    spare = jnp.dot(side, m_ref[:, 3 * lanes :], preferred_element_type=F32)
    copies = []
    for depth in range(3):
        at = (2 - depth) * rest
        stage[depth, :rows, :] = jnp.dot(side, m_ref[:, depth * lanes : (depth + 1) * lanes], preferred_element_type=F32)
        stage[depth, rows:, :] = spare[at : at + rest]
        copies.append(pltpu.make_async_copy(stage.at[depth], out_ref.at[depth], sems.at[depth]))
        copies[-1].start()
    for copy in copies:
        copy.wait()


def in_grad_square_kernel(og, chans, count, w_ref, *refs):
    sources, out_ref, p_scr = refs[:count], refs[count], refs[count + 1]
    i = lax.axis_index("chan")
    width = og * og
    all_chans = count * chans
    for mask, source in enumerate(sources):
        j = lax.bitwise_xor(i, mask)
        for index in range(4):
            at = pl.multiple_of(index * all_chans + j * chans, chans)
            p_scr[pl.ds(at, chans), :] = source[index * chans : (index + 1) * chans, :]
    joined = in_grad_planes(og, chans, all_chans, w_ref, lane_matrix(og), p_scr)
    rows = [
        jnp.concatenate([joined[(plane * 4 + k) * chans : (plane * 4 + k + 1) * chans] for k in range(4)], axis=1)
        for plane in range(2)
    ]
    value = jnp.concatenate(rows, axis=0).astype(BF16)
    value = lax.dot_general(order_matrix(chans, 2), value, (((0,), (0,)), ((), ())), preferred_element_type=F32)
    out_ref[...] = value.astype(BF16).reshape(out_ref.shape)


def local_call(kernel, out_shape, scratch, flops, *operands, out_space=pltpu.VMEM):
    total = sum(value.size * value.dtype.itemsize for value in operands)
    total += sum(math.prod(o.shape) * o.dtype.itemsize for o in jax.tree.leaves(out_shape))
    return pl.pallas_call(
        kernel,
        out_shape=out_shape,
        in_specs=[pl.BlockSpec(memory_space=pltpu.VMEM)] * len(operands),
        out_specs=jax.tree.map(lambda _: pl.BlockSpec(memory_space=out_space), out_shape),
        scratch_shapes=scratch,
        cost_estimate=pl.CostEstimate(flops=flops, bytes_accessed=total, transcendentals=0),
        compiler_params=pltpu.CompilerParams(vmem_limit_bytes=50 * 1024 * 1024),
    )(*operands)


def ring(value, step):
    count = lax.axis_size("space")
    return lax.ppermute(value, "space", [(i, (i + step) % count) for i in range(count)])


def ring_shards(inputs, pre_act, out_grad, weight_one, weight_two):
    samples, chans, planes, cells = inputs.shape
    count = lax.axis_size("space")
    og = math.isqrt(out_grad.shape[3])
    width = og * og
    half = 4 * chans
    block = 9 * chans
    all_chans = weight_one.shape[4]
    all_out = weight_two.shape[4]
    w1 = weight_one.reshape(3 * block, all_chans)
    w2 = weight_two.reshape(3 * block, all_out)
    matrix = jnp.asarray(split_matrix(og), BF16)
    shape = jax.ShapeDtypeStruct

    grads = lax.all_gather(out_grad.reshape(-1, width), "chan", axis=0, tiled=True)
    xp, hp = local_call(
        lambda *r: split_kernel(og, planes, chans, *r),
        [shape((planes * half, width), BF16)] * 2,
        [],
        2 * 2 * planes * half * width * width,
        inputs.reshape(chans, planes * cells),
        pre_act.reshape(chans, planes * cells),
        matrix,
    )
    grads_next = ring(grads, count - 1)
    up = [(i, i + 1) for i in range(count - 1)]
    down = [(i + 1, i) for i in range(count - 1)]
    x_prev = lax.ppermute(xp[half:], "space", up)
    x_next = lax.ppermute(xp[:half], "space", down)

    p_own = local_call(
        lambda *r: own_grad_kernel(og, chans, count, *r),
        shape((2 * half, width), BF16),
        [],
        2 * 3 * block * all_out * width,
        w2,
        grads,
        grads_next,
        hp,
    )
    a_own = lax.all_gather(p_own, "chan", axis=0)

    all_grads = [grads] + [ring(grads, step) for step in range(1, count - 1)] + [grads_next]
    all_hp = [hp] + [ring(hp, step) for step in range(1, count)]

    rows = -(-3 * block // (16 * count)) * 16
    pieces = local_call(
        lambda *r: filter_one_kernel(og, chans, count, rows, *r),
        [shape((rows, all_chans), F32)] + [shape((rows, all_chans), BF16)] * (count - 1),
        [
            pltpu.VMEM((2 * all_chans, 4 * width), BF16),
            pltpu.VMEM((4, block, 4 * width), BF16),
            pltpu.VMEM((count * rows, all_chans), F32),
        ],
        2 * 6 * block * all_chans * cells,
        a_own,
        x_prev,
        xp,
        x_next,
    )
    total = pieces[0]
    for step in range(1, count):
        total = total + ring(pieces[step], step).astype(F32)
    scale_one = 1.0 / math.sqrt(samples * planes * count * cells)
    scale_two = 1.0 / math.sqrt(samples * out_grad.shape[2] * count * width)
    total = (total * scale_one).astype(BF16)

    p_rim = local_call(
        lambda *r: rim_grad_kernel(og, chans, count, *r),
        shape((2 * half, width), BF16),
        [],
        2 * 3 * block * all_out * width,
        w2,
        all_grads[1],
        grads,
        grads_next,
        all_hp[1],
        all_hp[count - 1],
    )
    a_rim = lax.all_gather(p_rim, "chan", axis=0)
    in_grad = local_call(
        lambda *r: in_grad_kernel(og, chans, *r),
        shape((chans, planes * cells), BF16),
        [pltpu.VMEM((4 * all_chans, 4 * width), BF16)],
        2 * 6 * block * all_chans * cells,
        w1,
        a_own,
        a_rim,
        matrix,
    )
    filter_two = local_call(
        lambda *r: filter_two_kernel(og, chans, count, scale_two, *r),
        shape((3 * block, all_out), F32),
        [
            pltpu.VMEM((count, all_out, width), BF16),
            pltpu.VMEM((count, block, width), BF16),
            pltpu.VMEM((count, block, width), BF16),
        ],
        2 * 3 * count * block * all_out * width,
        *all_grads,
        *all_hp,
    )
    filter_one = local_call(
        lambda *r: place_kernel(count, rows, *r),
        shape((3 * block, all_chans), F32),
        [pltpu.VMEM((count * rows, all_chans), F32)],
        0,
        total,
        *[ring(total, step) for step in range(1, count)],
    )
    return (
        in_grad.reshape(samples, chans, planes, cells),
        filter_one.reshape(3, 3, 3, chans, all_chans),
        filter_two.reshape(3, 3, 3, chans, all_out),
    )


def spread(value, before_last=(), axis="chan"):
    count = lax.axis_size(axis)
    found = {0: value}
    bit = count // 2
    while bit:
        pairs = [(i, i ^ bit) for i in range(count)]
        if bit == 1 and before_last:
            for mask in found:
                if mask:
                    found[mask] = lax.optimization_barrier((found[mask], *before_last))[0]
        found.update({mask ^ bit: lax.ppermute(item, axis, pairs) for mask, item in found.items()})
        bit //= 2
    return [found[mask] for mask in range(count)]


def paired(value, mask):
    return lax.ppermute(value, "space", [(i, i ^ mask) for i in range(lax.axis_size("space"))])


def square_shards(inputs, pre_act, out_grad, weight_one, weight_two):
    samples, chans, planes, cells = inputs.shape
    count = lax.axis_size("space")
    og = math.isqrt(out_grad.shape[3])
    width = og * og
    half = 4 * chans
    block = 9 * chans
    all_chans = weight_one.shape[4]
    all_out = weight_two.shape[4]
    w1 = weight_one.reshape(3 * block, all_chans)
    w2 = weight_two.reshape(3 * block, all_out)
    shape = jax.ShapeDtypeStruct
    both = ("space", "chan")
    scale_one = 1.0 / math.sqrt(samples * planes * count * cells)
    scale_two = 1.0 / math.sqrt(samples * out_grad.shape[2] * count * width)

    near = out_grad.reshape(-1, width)
    around = [near] + [paired(near, step) for step in range(1, count)]
    turn = [(mixed(j, count) * count + mixed(a, count), a * count + j) for a in range(count) for j in range(count)]
    x_turned = lax.ppermute(inputs.reshape(chans, planes, cells), both, turn)
    packed = local_call(pack_kernel, shape((count * near.shape[0], width), BF16), [], 0, *around)
    gate = local_call(
        lambda *r: gate_kernel(og, chans, *r),
        shape((planes * half, width), BF16),
        [],
        2 * planes * half * width * width,
        pre_act.reshape(chans, planes, cells),
    )
    gates = spread(gate, (), "space")
    grads = spread(packed)
    rows = block_rows(chans)
    p_local, p_all, grads, act = local_call(
        lambda *r: all_grad_kernel(og, chans, count, *r),
        [
            shape((half, 4 * width), BF16),
            shape(((planes * count + 3) * chans, 4 * width), BF16),
            shape((count, all_out, width), BF16),
            shape((count, planes * half, width), BF16),
        ],
        [pltpu.VMEM((count, planes * half, width), BF16)],
        2 * 3 * count * block * all_out * width,
        w2,
        *grads,
        *gates,
    )
    x_all = spread(x_turned)
    piece = local_call(
        lambda *r: filter_block_kernel(og, chans, count, scale_one, *r),
        shape((rows, all_chans), BF16),
        [pltpu.VMEM((planes * count * block, 4 * width), BF16)],
        2 * 3 * count * block * all_chans * cells,
        p_all,
        *x_all,
    )
    mate = lax.ppermute(piece, "chan", [(j, j ^ 1) for j in range(count)])
    pair = local_call(
        lambda *r: pair_kernel(*r),
        shape((2 * rows, all_chans), BF16),
        [],
        0,
        piece,
        mate,
    )
    pieces = []
    for step in range(count // 2):
        pairs = [
            (a * count + j, (j % 2 + (step ^ j // 2) * 2) * count + mixed(a, count))
            for a in range(count)
            for j in range(count)
        ]
        pieces.append(lax.ppermute(pair, both, pairs))
    filter_two = local_call(
        lambda *r: filter_two_square_kernel(og, chans, count, scale_two, *r),
        shape((3, block, all_out), F32),
        [
            pltpu.VMEM((count, block, width), BF16),
            pltpu.VMEM((count, block, width), BF16),
            pltpu.VMEM((3, block, all_out), F32),
            pltpu.SemaphoreType.DMA((3,)),
        ],
        2 * 3 * count * block * all_out * width,
        grads,
        act,
        out_space=pl.ANY,
    )
    near_p = [p_local] + [
        lax.ppermute(p_local, "chan", [(i, i ^ mask) for i in range(count)]) for mask in range(1, count)
    ]
    in_grad = local_call(
        lambda *r: in_grad_square_kernel(og, chans, count, *r),
        shape((chans, planes, cells), BF16),
        [pltpu.VMEM((4 * all_chans, 4 * width), BF16)],
        2 * 6 * block * all_chans * cells,
        w1,
        *near_p,
    )
    filter_one = local_call(
        lambda *r: join_kernel(chans, count, *r),
        shape((3, block, all_chans), F32),
        [
            pltpu.VMEM((count // 2, 2 * rows, all_chans), BF16),
            pltpu.VMEM((3, block, all_chans), F32),
            pltpu.SemaphoreType.DMA((3,)),
        ],
        2 * rows * 16 * all_chans * all_chans,
        jnp.asarray(join_matrix(chans, count), BF16),
        *pieces,
        out_space=pl.ANY,
    )
    return (
        in_grad.reshape(samples, chans, planes, cells),
        filter_one.reshape(3, 3, 3, chans, all_chans),
        filter_two.reshape(3, 3, 3, chans, all_out),
    )


def shards(*arguments):
    count = lax.axis_size("space")
    square = count == lax.axis_size("chan") and count & (count - 1) == 0 and 4 * arguments[0].shape[1] == arguments[3].shape[4]
    return (square_shards if square else ring_shards)(*arguments)


def solution(mesh):
    in_specs = (
        P("groups", "chan", "space", None),
        P("groups", "chan", "space", None),
        P("groups", "chan", "space", None),
        P(None, None, None, "chan", None),
        P(None, None, None, "chan", None),
    )
    out_specs = (
        P("groups", "chan", "space", None),
        P("groups", None, None, "chan", None),
        P("groups", None, None, "chan", None),
    )
    return jax.shard_map(shards, mesh=mesh, in_specs=in_specs, out_specs=out_specs, check_vma=False)
```

```python
import math

import jax
import jax.numpy as jnp
import numpy as np
from jax import lax
from jax.experimental import pallas as pl
from jax.experimental.pallas import tpu as pltpu
from jax.sharding import PartitionSpec as P

leak_slope = 0.3
F32 = jnp.float32
BF16 = jnp.bfloat16
CONTRACT_LAST = (((1,), (1,)), ((), ()))


def moved(value, rows, cols, og):
    if rows == 0 and cols == 0:
        return value
    width = og * og
    value = value.astype(F32)
    lane = lax.broadcasted_iota(jnp.int32, value.shape, 1)
    rolled = pltpu.roll(value, (-(rows * og + cols)) % width, 1)
    keep = None
    for step, place in ((rows, lane // og), (cols, lane % og)):
        if step:
            good = place < og - 1 if step > 0 else place > 0
            keep = good if keep is None else keep & good
    return jnp.where(keep, rolled, 0.0)


def neighbour(parity, step):
    place = parity + step
    return place % 2, place // 2


def leaky(value, gate):
    return jnp.where(gate > 0, value, leak_slope * value)


def lane_matrix(og):
    width = og * og
    cell = lax.broadcasted_iota(jnp.int32, (width, width), 0)
    place = lax.broadcasted_iota(jnp.int32, (width, width), 1)
    row, col = cell // (2 * og), cell % (2 * og)
    target = (row % 2 * 2 + col % 2) * (width // 4) + row // 2 * og + col // 2
    return jnp.where(place == target, 1.0, 0.0).astype(BF16)


def order_matrix(chans, planes):
    rows = chans * planes
    place = lax.broadcasted_iota(jnp.int32, (rows, rows), 0)
    row = lax.broadcasted_iota(jnp.int32, (rows, rows), 1)
    return jnp.where(place == row % planes * chans + row // planes, 1.0, 0.0).astype(BF16)


def split_matrix(og):
    width = og * og
    grid = 2 * og
    cell = np.arange(width)
    row, col = cell // grid, cell % grid
    place = ((row % 2) * 2 + col % 2) * (width // 4) + (row // 2) * og + col // 2
    return (place[:, None] == np.arange(width)[None, :]).astype(np.float32)


def split_kernel(og, planes, chans, x_ref, h_ref, e_ref, xp_ref, hp_ref):
    width = og * og
    part = width // 4
    matrix = e_ref[...]
    for source, target in ((x_ref, xp_ref), (h_ref, hp_ref)):
        value = source[...]
        stacked = jnp.concatenate([value[:, i * width : (i + 1) * width] for i in range(4 * planes)], axis=0)
        sorted_cells = jnp.dot(stacked, matrix, preferred_element_type=F32)
        for plane in range(planes):
            for parity in range(4):
                pieces = [
                    sorted_cells[(plane * 4 + i) * chans : (plane * 4 + i + 1) * chans, parity * part : (parity + 1) * part]
                    for i in range(4)
                ]
                at = (plane * 4 + parity) * chans
                target[at : at + chans, :] = jnp.concatenate(pieces, axis=1).astype(BF16)


def transposed_taps(taps, chans, og):
    def tap(row, col):
        at = (row * 3 + col) * chans
        return taps[at : at + chans]

    return [
        tap(1, 1),
        tap(1, 2) + moved(tap(1, 0), 0, 1, og),
        tap(2, 1) + moved(tap(0, 1), 1, 0, og),
        tap(2, 2) + moved(tap(0, 2), 1, 0, og) + moved(tap(2, 0), 0, 1, og) + moved(tap(0, 0), 1, 1, og),
    ]


def plane_grad(w_ref, near, after, gates, chans, og, out_ref, at, live):
    block = 9 * chans
    if after is None:
        taps = jnp.dot(w_ref[block : 2 * block, :], near, preferred_element_type=F32)
    else:
        taps = jnp.dot(w_ref[2 * block : 3 * block, :], near, preferred_element_type=F32)
        taps = taps + jnp.dot(w_ref[0:block, :], after, preferred_element_type=F32)
    for parity, value in enumerate(transposed_taps(taps, chans, og)):
        gate = gates[parity * chans : (parity + 1) * chans].astype(F32)
        value = leaky(value, gate)
        if live is not None:
            value = jnp.where(live, value, 0.0)
        out_ref[at + parity * chans : at + (parity + 1) * chans, :] = value.astype(BF16)


def own_grad_kernel(og, chans, count, w_ref, g_ref, gn_ref, hp_ref, p_ref):
    s = lax.axis_index("space")
    half = 4 * chans
    here = g_ref[...]
    after = jnp.where(s < count - 1, gn_ref[...].astype(F32), 0.0).astype(BF16)
    plane_grad(w_ref, here, None, hp_ref[0:half, :], chans, og, p_ref, 0, None)
    plane_grad(w_ref, here, after, hp_ref[half : 2 * half, :], chans, og, p_ref, half, None)


def rim_grad_kernel(og, chans, count, w_ref, gp_ref, g_ref, gn_ref, hp_prev_ref, hp_next_ref, p_ref):
    s = lax.axis_index("space")
    half = 4 * chans
    plane_grad(w_ref, gp_ref[...], g_ref[...], hp_prev_ref[half : 2 * half, :], chans, og, p_ref, 0, s > 0)
    plane_grad(w_ref, gn_ref[...], None, hp_next_ref[0:half, :], chans, og, p_ref, half, s < count - 1)


def window_rows(blocks, parity, og):
    rows = []
    for row_tap in range(3):
        row_parity, row_move = neighbour(parity // 2, row_tap - 1)
        for col_tap in range(3):
            col_parity, col_move = neighbour(parity % 2, col_tap - 1)
            rows.append(blocks[(row_parity * 2 + col_parity, row_move, col_move)])
    return jnp.concatenate(rows, axis=0)


def moved_blocks(plane, chans, og):
    result = {}
    for parity in range(4):
        value = plane[parity * chans : (parity + 1) * chans]
        for row_move in (0, -1 if parity // 2 else 1):
            for col_move in (0, -1 if parity % 2 else 1):
                result[parity, row_move, col_move] = moved(value, row_move, col_move, og).astype(BF16)
    return result


def filter_one_kernel(og, chans, count, rows, a_ref, xprev_ref, xp_ref, xnext_ref, own_ref, *rest):
    outs, (p_scr, x_scr, f_scr) = rest[: count - 1], rest[count - 1 :]
    s = lax.axis_index("space")
    width = og * og
    shards = a_ref.shape[0]
    all_chans = shards * chans
    half = 4 * chans
    block = 9 * chans
    for plane in range(2):
        for parity in range(4):
            for j in range(shards):
                at = plane * all_chans + j * chans
                p_scr[at : at + chans, parity * width : (parity + 1) * width] = a_ref[
                    j, (plane * 4 + parity) * chans : (plane * 4 + parity + 1) * chans, :
                ]
    planes = (xprev_ref[...], xp_ref[0:half, :], xp_ref[half : 2 * half, :], xnext_ref[...])
    ends = ((0, all_chans), (0, 2 * all_chans), (0, 2 * all_chans), (all_chans, 2 * all_chans))
    products = []
    for index, plane in enumerate(planes):
        blocks = moved_blocks(plane, chans, og)
        for parity in range(4):
            x_scr[index, :, parity * width : (parity + 1) * width] = window_rows(blocks, parity, og)
        first, last = ends[index]
        products.append(
            lax.dot_general(x_scr[index], p_scr[first:last, :], CONTRACT_LAST, preferred_element_type=F32)
        )
    before, even, odd, after = products
    f_scr[0:block, :] = before + even[:, all_chans:]
    f_scr[block : 2 * block, :] = even[:, :all_chans] + odd[:, all_chans:]
    f_scr[2 * block : 3 * block, :] = odd[:, :all_chans] + after
    if count * rows > 3 * block:
        f_scr[3 * block :, :] = jnp.zeros((count * rows - 3 * block, all_chans), F32)

    def piece(step):
        at = pl.multiple_of(lax.rem(s + step, count) * rows, 16)
        return f_scr[pl.ds(at, rows), :]

    own_ref[...] = piece(0)
    for step, out in enumerate(outs):
        out[...] = piece(step + 1).astype(BF16)


def in_grad_kernel(og, chans, w_ref, a_ref, r_ref, e_ref, out_ref, p_scr):
    width = og * og
    shards = a_ref.shape[0]
    all_chans = shards * chans
    for index in range(4):
        source, first = (r_ref, index // 3) if index in (0, 3) else (a_ref, index - 1)
        for parity in range(4):
            for j in range(shards):
                at = index * all_chans + j * chans
                p_scr[at : at + chans, parity * width : (parity + 1) * width] = source[
                    j, (first * 4 + parity) * chans : (first * 4 + parity + 1) * chans, :
                ]
    joined = in_grad_planes(og, chans, all_chans, w_ref, e_ref[...], p_scr)
    for i in range(8):
        out_ref[:, i * width : (i + 1) * width] = joined[i * chans : (i + 1) * chans].astype(BF16)


def in_grad_planes(og, chans, all_chans, w_ref, matrix, p_scr):
    width = og * og
    part = width // 4
    block = 9 * chans
    empty = jnp.zeros((block, all_chans), BF16)
    weights = [w_ref[depth * block : (depth + 1) * block, :] for depth in (2, 1, 0)]
    weights = jnp.concatenate(
        [jnp.concatenate(weights + [empty], axis=1), jnp.concatenate([empty] + weights, axis=1)], axis=0
    )
    both = jnp.dot(weights, p_scr[...], preferred_element_type=F32)
    stacked = []
    for plane in range(2):
        taps = both[plane * block : (plane + 1) * block]
        sums = []
        for parity in range(4):
            terms = {}
            for row_tap in range(3):
                row_parity, row_move = neighbour(parity // 2, 1 - row_tap)
                for col_tap in range(3):
                    col_parity, col_move = neighbour(parity % 2, 1 - col_tap)
                    at = (row_tap * 3 + col_tap) * chans
                    lane = (row_parity * 2 + col_parity) * width
                    term = taps[at : at + chans, lane : lane + width]
                    key = (row_move, col_move)
                    terms[key] = term if key not in terms else terms[key] + term
            total = None
            for (row_move, col_move), term in terms.items():
                term = moved(term, row_move, col_move, og)
                total = term if total is None else total + term
            sums.append(total)
        for i in range(4):
            stacked.append(
                jnp.concatenate([value[:, i * part : (i + 1) * part] for value in sums], axis=1).astype(BF16)
            )
    return lax.dot_general(jnp.concatenate(stacked, axis=0), matrix, CONTRACT_LAST, preferred_element_type=F32)


def filter_two_kernel(og, chans, count, scale, *refs):
    grads, gates, out_ref = refs[:count], refs[count : 2 * count], refs[2 * count]
    g_scr, even_scr, odd_scr = refs[2 * count + 1 :]
    s = lax.axis_index("space")
    half = 4 * chans
    block = 9 * chans
    for step in range(count):
        at = lax.rem(s + count - step, count)
        g_scr[at] = grads[step][...]
        value = gates[step][...].astype(F32)
        act = leaky(value, value).astype(BF16)
        for plane, target in enumerate((even_scr, odd_scr)):
            blocks = moved_blocks(act[plane * half : (plane + 1) * half], chans, og)
            target[at] = window_rows(blocks, 0, og)
    filter_two_sums(count, block, scale, g_scr, even_scr, odd_scr, out_ref)


def filter_two_square_kernel(og, chans, count, scale, g_ref, act_ref, out_ref, even_scr, odd_scr):
    half = 4 * chans
    for at in range(count):
        for plane, target in enumerate((even_scr, odd_scr)):
            blocks = moved_blocks(act_ref[at, plane * half : (plane + 1) * half, :], chans, og)
            target[at] = window_rows(blocks, 0, og)
    filter_two_sums(count, 9 * chans, scale, g_ref, even_scr, odd_scr, out_ref)


def filter_two_sums(count, block, scale, g_scr, even_scr, odd_scr, out_ref):
    totals = [jnp.zeros((block, g_scr.shape[1]), F32) for _ in range(3)]
    for at in range(count):
        sources = (odd_scr.at[at - 1] if at else None, even_scr.at[at], odd_scr.at[at])
        for depth, source in enumerate(sources):
            if source is not None:
                totals[depth] = totals[depth] + lax.dot_general(
                    source[...], g_scr[at], CONTRACT_LAST, preferred_element_type=F32
                )
    for depth in range(3):
        out_ref[depth * block : (depth + 1) * block, :] = totals[depth] * scale


def place_kernel(count, rows, *refs):
    pieces, out_ref, scr = refs[:count], refs[count], refs[count + 1]
    s = lax.axis_index("space")
    for step, piece in enumerate(pieces):
        at = pl.multiple_of(lax.rem(s + count - step, count) * rows, 16)
        scr[pl.ds(at, rows), :] = piece[...].astype(F32)
    out_ref[...] = scr[0 : out_ref.shape[0], :]


def split_planes(value, order, matrix, chans, planes, og):
    width = og * og
    part = width // 4
    value = value.reshape(chans * planes, 4 * width)
    value = jnp.dot(order, value, preferred_element_type=F32).astype(BF16)
    stacked = jnp.concatenate([value[:, i * width : (i + 1) * width] for i in range(4)], axis=0)
    cells = jnp.dot(stacked, matrix, preferred_element_type=F32)
    rows = chans * planes
    result = []
    for plane in range(planes):
        for parity in range(4):
            pieces = [
                cells[i * rows + plane * chans : i * rows + (plane + 1) * chans, parity * part : (parity + 1) * part]
                for i in range(4)
            ]
            result.append(jnp.concatenate(pieces, axis=1))
    return jnp.concatenate(result, axis=0)


def pack_kernel(*refs):
    sources, out_ref = refs[:-1], refs[-1]
    rows = sources[0].shape[0]
    for step, source in enumerate(sources):
        out_ref[step * rows : (step + 1) * rows, :] = source[...]


def gate_kernel(og, chans, h_ref, out_ref):
    value = split_planes(h_ref[...], order_matrix(chans, 2), lane_matrix(og), chans, 2, og)
    out_ref[...] = value.astype(BF16)


def all_grad_kernel(og, chans, count, w_ref, *refs):
    grads, gates, refs = refs[:count], refs[count : 2 * count], refs[2 * count :]
    local_ref, q_ref, g_ref, act_ref, h_scr = refs
    s = lax.axis_index("space")
    half = 4 * chans
    i = lax.axis_index("chan")
    part = grads[0].shape[0] // count
    for step in range(count):
        at = lax.bitwise_xor(s, step)
        for mask in range(count):
            row = pl.multiple_of(lax.bitwise_xor(i, mask) * part, part)
            g_ref[at, pl.ds(row, part), :] = grads[mask][step * part : (step + 1) * part, :]
        value = gates[step][...]
        h_scr[at] = value
        value = value.astype(F32)
        act_ref[at] = leaky(value, value).astype(BF16)
    empty = jnp.zeros((chans, q_ref.shape[1]), BF16)
    for index in (0, 2 * count + 1, 2 * count + 2):
        q_ref[index * chans : (index + 1) * chans, :] = empty
    block = 9 * chans
    for q in range(count):
        here = g_ref[q]
        even = jnp.dot(w_ref[block : 2 * block, :], here, preferred_element_type=F32)
        odd = jnp.dot(w_ref[2 * block : 3 * block, :], here, preferred_element_type=F32)
        if q < count - 1:
            odd = odd + jnp.dot(w_ref[0:block, :], g_ref[q + 1], preferred_element_type=F32)
        for plane, value in enumerate((even, odd)):
            row = (2 * q + plane + 1) * chans
            blocks = []
            for parity, term in enumerate(transposed_taps(value, chans, og)):
                at = (plane * 4 + parity) * chans
                blocks.append(leaky(term, h_scr[q, at : at + chans, :].astype(F32)).astype(BF16))
            q_ref[row : row + chans, :] = jnp.concatenate(blocks, axis=1)
    local_ref[...] = q_ref[pl.ds(pl.multiple_of(2 * s * chans, chans), half), :]


def mixed(index, count):
    return index % 2 * (count // 2) + index // 2


def block_rows(chans):
    return -(-27 * chans // 64) * 16


def filter_block_kernel(og, chans, count, scale, q_ref, *refs):
    sources, (out_ref, x_scr) = refs[:count], refs[count:]
    matrix, order = lane_matrix(og), order_matrix(chans, 2)
    i = lax.axis_index("chan")
    width = og * og
    half = 4 * chans
    block = 9 * chans
    lanes = 4 * chans
    across = 2 * count * chans
    for index, source in enumerate(sources):
        value = split_planes(source[...], order, matrix, chans, 2, og)
        for plane in range(2):
            blocks = moved_blocks(value[plane * half : (plane + 1) * half], chans, og)
            at = (2 * index + plane) * block
            for parity in range(4):
                x_scr[at : at + block, parity * width : (parity + 1) * width] = window_rows(blocks, parity, og)
    products = lax.dot_general(
        x_scr[...], q_ref[chans : chans + across, :], CONTRACT_LAST, preferred_element_type=F32
    )
    group = lax.broadcasted_iota(jnp.int32, (block, lanes), 1) // chans
    total = jnp.zeros((block, lanes), F32)
    for mask in range(count):
        for plane in range(2):
            place = 2 * mixed(lax.bitwise_xor(i, mask), count) + plane
            at = (2 * mask + plane) * block
            term = pltpu.roll(products[at : at + block], lax.rem(across + chans - place * chans, across), 1)[:, :lanes]
            inside = (group + place > 0) & (group + place <= 2 * count)
            total = total + jnp.where(inside, term, 0.0)
    total = total * scale
    rows = block_rows(chans)
    tail = total[rows:]
    moved_tail = [pltpu.roll(tail, lanes - (i + 1) * chans, 1) for i in range(3)]
    spare = rows - 3 * (block - rows)
    if spare:
        moved_tail.append(jnp.zeros((spare, lanes), F32))
    lane = lax.broadcasted_iota(jnp.int32, (rows, lanes), 1)
    out_ref[...] = jnp.where(lane < 3 * chans, total[:rows], jnp.concatenate(moved_tail, axis=0)).astype(BF16)


def join_matrix(chans, count):
    lanes = 4 * chans
    result = np.zeros((count * lanes, 4 * lanes), np.float32)
    for j in range(count):
        for group in range(4):
            target = 2 - group if group < 3 else 3
            for c in range(chans):
                result[j * lanes + group * chans + c, target * lanes + j * chans + c] = 1
    return result


def pair_kernel(own_ref, mate_ref, out_ref):
    odd = lax.axis_index("chan") % 2
    rows = own_ref.shape[0]
    out_ref[pl.ds(pl.multiple_of(odd * rows, 16), rows), :] = own_ref[...]
    out_ref[pl.ds(pl.multiple_of((1 - odd) * rows, 16), rows), :] = mate_ref[...]


def join_kernel(chans, count, m_ref, *refs):
    pieces, out_ref, scr = refs[:-2], refs[-2], refs[-1]
    s = lax.axis_index("space")
    lanes = 4 * chans
    block = 9 * chans
    rows = block_rows(chans)
    rest = block - rows
    for step, piece in enumerate(pieces):
        scr[step] = piece[...]
    side = [
        scr[lax.bitwise_xor(s // 2, j // 2), j % 2 * rows : (j % 2 + 1) * rows, :] for j in range(count)
    ]
    joined = jnp.dot(jnp.concatenate(side, axis=1), m_ref[...], preferred_element_type=F32)
    for depth in range(3):
        out_ref[depth * block : depth * block + rows, :] = joined[:, depth * lanes : (depth + 1) * lanes]
        at = (2 - depth) * rest
        out_ref[depth * block + rows : (depth + 1) * block, :] = joined[at : at + rest, 3 * lanes :]


def in_grad_square_kernel(og, chans, count, w_ref, *refs):
    sources, out_ref, p_scr = refs[:count], refs[count], refs[count + 1]
    i = lax.axis_index("chan")
    width = og * og
    all_chans = count * chans
    for mask, source in enumerate(sources):
        j = lax.bitwise_xor(i, mask)
        for index in range(4):
            at = pl.multiple_of(index * all_chans + j * chans, chans)
            p_scr[pl.ds(at, chans), :] = source[index * chans : (index + 1) * chans, :]
    joined = in_grad_planes(og, chans, all_chans, w_ref, lane_matrix(og), p_scr)
    rows = [
        jnp.concatenate([joined[(plane * 4 + k) * chans : (plane * 4 + k + 1) * chans] for k in range(4)], axis=1)
        for plane in range(2)
    ]
    value = jnp.concatenate(rows, axis=0).astype(BF16)
    value = lax.dot_general(order_matrix(chans, 2), value, (((0,), (0,)), ((), ())), preferred_element_type=F32)
    out_ref[...] = value.astype(BF16).reshape(out_ref.shape)


def local_call(kernel, out_shape, scratch, flops, *operands):
    total = sum(value.size * value.dtype.itemsize for value in operands)
    total += sum(math.prod(o.shape) * o.dtype.itemsize for o in jax.tree.leaves(out_shape))
    return pl.pallas_call(
        kernel,
        out_shape=out_shape,
        in_specs=[pl.BlockSpec(memory_space=pltpu.VMEM)] * len(operands),
        out_specs=jax.tree.map(lambda _: pl.BlockSpec(memory_space=pltpu.VMEM), out_shape),
        scratch_shapes=scratch,
        cost_estimate=pl.CostEstimate(flops=flops, bytes_accessed=4 * total, transcendentals=0),
        compiler_params=pltpu.CompilerParams(vmem_limit_bytes=50 * 1024 * 1024),
    )(*operands)


def ring(value, step):
    count = lax.axis_size("space")
    return lax.ppermute(value, "space", [(i, (i + step) % count) for i in range(count)])


def ring_shards(inputs, pre_act, out_grad, weight_one, weight_two):
    samples, chans, planes, cells = inputs.shape
    count = lax.axis_size("space")
    og = math.isqrt(out_grad.shape[3])
    width = og * og
    half = 4 * chans
    block = 9 * chans
    all_chans = weight_one.shape[4]
    all_out = weight_two.shape[4]
    w1 = weight_one.reshape(3 * block, all_chans)
    w2 = weight_two.reshape(3 * block, all_out)
    matrix = jnp.asarray(split_matrix(og), BF16)
    shape = jax.ShapeDtypeStruct

    grads = lax.all_gather(out_grad.reshape(-1, width), "chan", axis=0, tiled=True)
    xp, hp = local_call(
        lambda *r: split_kernel(og, planes, chans, *r),
        [shape((planes * half, width), BF16)] * 2,
        [],
        2 * 2 * planes * half * width * width,
        inputs.reshape(chans, planes * cells),
        pre_act.reshape(chans, planes * cells),
        matrix,
    )
    grads_next = ring(grads, count - 1)
    up = [(i, i + 1) for i in range(count - 1)]
    down = [(i + 1, i) for i in range(count - 1)]
    x_prev = lax.ppermute(xp[half:], "space", up)
    x_next = lax.ppermute(xp[:half], "space", down)

    p_own = local_call(
        lambda *r: own_grad_kernel(og, chans, count, *r),
        shape((2 * half, width), BF16),
        [],
        2 * 3 * block * all_out * width,
        w2,
        grads,
        grads_next,
        hp,
    )
    a_own = lax.all_gather(p_own, "chan", axis=0)

    all_grads = [grads] + [ring(grads, step) for step in range(1, count - 1)] + [grads_next]
    all_hp = [hp] + [ring(hp, step) for step in range(1, count)]

    rows = -(-3 * block // (16 * count)) * 16
    pieces = local_call(
        lambda *r: filter_one_kernel(og, chans, count, rows, *r),
        [shape((rows, all_chans), F32)] + [shape((rows, all_chans), BF16)] * (count - 1),
        [
            pltpu.VMEM((2 * all_chans, 4 * width), BF16),
            pltpu.VMEM((4, block, 4 * width), BF16),
            pltpu.VMEM((count * rows, all_chans), F32),
        ],
        2 * 6 * block * all_chans * cells,
        a_own,
        x_prev,
        xp,
        x_next,
    )
    total = pieces[0]
    for step in range(1, count):
        total = total + ring(pieces[step], step).astype(F32)
    scale_one = 1.0 / math.sqrt(samples * planes * count * cells)
    scale_two = 1.0 / math.sqrt(samples * out_grad.shape[2] * count * width)
    total = (total * scale_one).astype(BF16)

    p_rim = local_call(
        lambda *r: rim_grad_kernel(og, chans, count, *r),
        shape((2 * half, width), BF16),
        [],
        2 * 3 * block * all_out * width,
        w2,
        all_grads[1],
        grads,
        grads_next,
        all_hp[1],
        all_hp[count - 1],
    )
    a_rim = lax.all_gather(p_rim, "chan", axis=0)
    in_grad = local_call(
        lambda *r: in_grad_kernel(og, chans, *r),
        shape((chans, planes * cells), BF16),
        [pltpu.VMEM((4 * all_chans, 4 * width), BF16)],
        2 * 6 * block * all_chans * cells,
        w1,
        a_own,
        a_rim,
        matrix,
    )
    filter_two = local_call(
        lambda *r: filter_two_kernel(og, chans, count, scale_two, *r),
        shape((3 * block, all_out), F32),
        [
            pltpu.VMEM((count, all_out, width), BF16),
            pltpu.VMEM((count, block, width), BF16),
            pltpu.VMEM((count, block, width), BF16),
        ],
        2 * 3 * count * block * all_out * width,
        *all_grads,
        *all_hp,
    )
    filter_one = local_call(
        lambda *r: place_kernel(count, rows, *r),
        shape((3 * block, all_chans), F32),
        [pltpu.VMEM((count * rows, all_chans), F32)],
        0,
        total,
        *[ring(total, step) for step in range(1, count)],
    )
    return (
        in_grad.reshape(samples, chans, planes, cells),
        filter_one.reshape(3, 3, 3, chans, all_chans),
        filter_two.reshape(3, 3, 3, chans, all_out),
    )


def spread(value, before_last=(), axis="chan"):
    count = lax.axis_size(axis)
    found = {0: value}
    bit = count // 2
    while bit:
        pairs = [(i, i ^ bit) for i in range(count)]
        if bit == 1 and before_last:
            for mask in found:
                if mask:
                    found[mask] = lax.optimization_barrier((found[mask], *before_last))[0]
        found.update({mask ^ bit: lax.ppermute(item, axis, pairs) for mask, item in found.items()})
        bit //= 2
    return [found[mask] for mask in range(count)]


def paired(value, mask):
    return lax.ppermute(value, "space", [(i, i ^ mask) for i in range(lax.axis_size("space"))])


def square_shards(inputs, pre_act, out_grad, weight_one, weight_two):
    samples, chans, planes, cells = inputs.shape
    count = lax.axis_size("space")
    og = math.isqrt(out_grad.shape[3])
    width = og * og
    half = 4 * chans
    block = 9 * chans
    all_chans = weight_one.shape[4]
    all_out = weight_two.shape[4]
    w1 = weight_one.reshape(3 * block, all_chans)
    w2 = weight_two.reshape(3 * block, all_out)
    shape = jax.ShapeDtypeStruct
    both = ("space", "chan")
    scale_one = 1.0 / math.sqrt(samples * planes * count * cells)
    scale_two = 1.0 / math.sqrt(samples * out_grad.shape[2] * count * width)

    near = out_grad.reshape(-1, width)
    far = {step: paired(near, step) for step in reversed(range(1, count))}
    around = [near] + [far[step] for step in range(1, count)]
    turn = [(mixed(j, count) * count + mixed(a, count), a * count + j) for a in range(count) for j in range(count)]
    x_turned = lax.ppermute(inputs.reshape(chans, planes, cells), both, turn)
    packed = local_call(pack_kernel, shape((count * near.shape[0], width), BF16), [], 0, *around)
    gate = local_call(
        lambda *r: gate_kernel(og, chans, *r),
        shape((planes * half, width), BF16),
        [],
        2 * planes * half * width * width,
        pre_act.reshape(chans, planes, cells),
    )
    gates = spread(gate, (), "space")
    grads = spread(packed)
    rows = block_rows(chans)
    p_local, p_all, grads, act = local_call(
        lambda *r: all_grad_kernel(og, chans, count, *r),
        [
            shape((half, 4 * width), BF16),
            shape(((planes * count + 3) * chans, 4 * width), BF16),
            shape((count, all_out, width), BF16),
            shape((count, planes * half, width), BF16),
        ],
        [pltpu.VMEM((count, planes * half, width), BF16)],
        2 * 3 * count * block * all_out * width,
        w2,
        *grads,
        *gates,
    )
    x_all = spread(x_turned)
    piece = local_call(
        lambda *r: filter_block_kernel(og, chans, count, scale_one, *r),
        shape((rows, all_chans), BF16),
        [pltpu.VMEM((planes * count * block, 4 * width), BF16)],
        2 * 3 * count * block * all_chans * cells,
        p_all,
        *x_all,
    )
    mate = lax.ppermute(piece, "chan", [(j, j ^ 1) for j in range(count)])
    pair = local_call(
        lambda *r: pair_kernel(*r),
        shape((2 * rows, all_chans), BF16),
        [],
        0,
        piece,
        mate,
    )
    pieces = []
    for step in range(count // 2):
        pairs = [
            (a * count + j, (j % 2 + (step ^ j // 2) * 2) * count + mixed(a, count))
            for a in range(count)
            for j in range(count)
        ]
        pieces.append(lax.ppermute(pair, both, pairs))
    filter_two = local_call(
        lambda *r: filter_two_square_kernel(og, chans, count, scale_two, *r),
        shape((3 * block, all_out), F32),
        [
            pltpu.VMEM((count, block, width), BF16),
            pltpu.VMEM((count, block, width), BF16),
        ],
        2 * 3 * count * block * all_out * width,
        grads,
        act,
    )
    near_p = [p_local] + [
        lax.ppermute(p_local, "chan", [(i, i ^ mask) for i in range(count)]) for mask in range(1, count)
    ]
    in_grad = local_call(
        lambda *r: in_grad_square_kernel(og, chans, count, *r),
        shape((chans, planes, cells), BF16),
        [pltpu.VMEM((4 * all_chans, 4 * width), BF16)],
        2 * 6 * block * all_chans * cells,
        w1,
        *near_p,
    )
    filter_one = local_call(
        lambda *r: join_kernel(chans, count, *r),
        shape((3 * block, all_chans), F32),
        [pltpu.VMEM((count // 2, 2 * rows, all_chans), BF16)],
        2 * rows * 16 * all_chans * all_chans,
        jnp.asarray(join_matrix(chans, count), BF16),
        *pieces,
    )
    return (
        in_grad.reshape(samples, chans, planes, cells),
        filter_one.reshape(3, 3, 3, chans, all_chans),
        filter_two.reshape(3, 3, 3, chans, all_out),
    )


def shards(*arguments):
    count = lax.axis_size("space")
    square = count == lax.axis_size("chan") and count & (count - 1) == 0 and 4 * arguments[0].shape[1] == arguments[3].shape[4]
    return (square_shards if square else ring_shards)(*arguments)


def solution(mesh):
    in_specs = (
        P("groups", "chan", "space", None),
        P("groups", "chan", "space", None),
        P("groups", "chan", "space", None),
        P(None, None, None, "chan", None),
        P(None, None, None, "chan", None),
    )
    out_specs = (
        P("groups", "chan", "space", None),
        P("groups", None, None, "chan", None),
        P("groups", None, None, "chan", None),
    )
    return jax.shard_map(shards, mesh=mesh, in_specs=in_specs, out_specs=out_specs, check_vma=False)
```
